32 devices in a mesh: ctx: 2 (over x), shard: 4 (over z), rep: 4 (over y, core).
Axes of the slice: x: 2, y: 2, z: 4, core: 2. Of those that a mesh axis runs over, the one named last changes fastest.
Arguments:
- frames: bfloat16 [16, 1024, 1536], P(('shard', 'rep'), 'ctx'), may hold values from -6 to 6
- text_states: bfloat16 [16, 64, 1536], P(('shard', 'rep')), may hold values from -6 to 6
- first_gain: bfloat16 [1536], P('shard'), may hold values from 0.5 to 1.5
- first_shift: bfloat16 [1536], P('shard'), may hold values from -2 to 2
- self_query: bfloat16 [1536, 1536], P('shard'), may hold values from -0.15625 to 0.15625
- self_key: bfloat16 [1536, 1536], P('shard'), may hold values from -0.15625 to 0.15625
- self_value: bfloat16 [1536, 1536], P('shard'), may hold values from -0.15625 to 0.15625
- self_output: bfloat16 [1536, 1536], P('shard'), may hold values from -0.875 to 0.875
- second_gain: bfloat16 [1536], P('shard'), may hold values from 0.5 to 1.5
- second_shift: bfloat16 [1536], P('shard'), may hold values from -2 to 2
- cross_query: bfloat16 [1536, 1536], P('shard'), may hold values from -0.15625 to 0.15625
- cross_key: bfloat16 [1536, 1536], P('shard'), may hold values from -0.15625 to 0.15625
- cross_value: bfloat16 [1536, 1536], P('shard'), may hold values from -0.15625 to 0.15625
- cross_output: bfloat16 [1536, 1536], P('shard'), may hold values from -0.625 to 0.625
- third_gain: bfloat16 [1536], P('shard'), may hold values from 0.5 to 1.5
- third_shift: bfloat16 [1536], P('shard'), may hold values from -2 to 2
- up_weight: bfloat16 [1536, 6144], P('shard'), may hold values from -0.15625 to 0.15625
- down_weight: bfloat16 [6144, 1536], P('shard'), may hold values from -0.078125 to 0.078125
- cotangent: bfloat16 [16, 1024, 1536], P(('shard', 'rep'), 'ctx'), may hold values from -6 to 6
Outputs:
- mixed: bfloat16 [16, 1024, 1536], P(('shard', 'rep'), 'ctx')
- grad_frames: float32 [16, 1024, 1536], P(('shard', 'rep'), 'ctx')
- grad_text: float32 [16, 64, 1536], P(('shard', 'rep'))
- grad_first_gain: float32 [1536], P('shard')
- grad_first_shift: float32 [1536], P('shard')
- grad_self_query: float32 [1536, 1536], P('shard')
- grad_self_key: float32 [1536, 1536], P('shard')
- grad_self_value: float32 [1536, 1536], P('shard')
- grad_self_output: float32 [1536, 1536], P('shard')
- grad_second_gain: float32 [1536], P('shard')
- grad_second_shift: float32 [1536], P('shard')
- grad_cross_query: float32 [1536, 1536], P('shard')
- grad_cross_key: float32 [1536, 1536], P('shard')
- grad_cross_value: float32 [1536, 1536], P('shard')
- grad_cross_output: float32 [1536, 1536], P('shard')
- grad_third_gain: float32 [1536], P('shard')
- grad_third_shift: float32 [1536], P('shard')
- grad_up_weight: float32 [1536, 6144], P('shard')
- grad_down_weight: float32 [6144, 1536], P('shard')
The draws below stay inside these ranges and needn't reach their ends.
All inputs are finite; a program needn't handle non-finite values.
Results may differ from the reference program's by a relative error of at most 0.024.
Values may be sent and summed in bfloat16 or wider, within the bound.
No kernel may reach another device: no remote copies, remote signals or barrier semaphores. Data moves between devices by JAX's collectives and lax.ppermute only.
A program may use at most 384 MiB of HBM per device.

```python
import jax
import jax.numpy as jnp
from jax import lax

D = 1536
H = 24
HD = 64
FF = 6144
TXT = 64
SEQ = 1024
CLIPS = 16


def shard_levels(stream_key, extent, shards, low, largest):
    level = 1.0
    for dim, blocks in shards:
        draws = jax.random.uniform(jax.random.fold_in(jax.random.fold_in(stream_key, 6), dim), (blocks,), jnp.float32, low / len(shards), largest / len(shards))
        level = level * jnp.repeat(jnp.exp(draws), extent[dim] // blocks).reshape((-1,) + (1,) * (len(extent) - 1 - dim))
    return level


def bell_draw(rng, shape, deviation, bound, cuts=(), kind=jnp.bfloat16):
    loudness = shard_levels(rng, shape, cuts, -0.22, 0.18) if cuts else 1.0
    entries = jax.random.normal(rng, shape, jnp.float32) * deviation * loudness
    return jnp.minimum(jnp.maximum(entries, -bound), bound).astype(kind)


def setup_inputs(seed: int = 0) -> dict:
    key_list = jax.random.split(jax.random.key(seed), 20)
    return {
        "frames": bell_draw(key_list[0], (CLIPS, SEQ, D), 1.0, 6.0, ((0, 16), (1, 2))),
        "text_states": bell_draw(key_list[1], (CLIPS, TXT, D), 1.0, 6.0, ((0, 16),)),
        "first_gain": jnp.clip(1.0 + 0.1 * jax.random.normal(key_list[2], (D,), jnp.float32), 0.5, 1.5).astype(jnp.bfloat16),
        "first_shift": bell_draw(key_list[3], (D,), 0.3, 2.0, ((0, 4),)),
        "self_query": bell_draw(key_list[4], (D, D), D ** -0.5, 0.15625, ((0, 4),)),
        "self_key": bell_draw(key_list[5], (D, D), D ** -0.5, 0.15625, ((0, 4),)),
        "self_value": bell_draw(key_list[6], (D, D), D ** -0.5, 0.15625, ((0, 4),)),
        "self_output": bell_draw(key_list[7], (D, D), (max(1, D // 32)) ** -0.5, 0.875, ((0, 4),)),
        "second_gain": jnp.clip(1.0 + 0.1 * jax.random.normal(key_list[8], (D,), jnp.float32), 0.5, 1.5).astype(jnp.bfloat16),
        "second_shift": bell_draw(key_list[9], (D,), 0.3, 2.0, ((0, 4),)),
        "cross_query": bell_draw(key_list[10], (D, D), D ** -0.5, 0.15625, ((0, 4),)),
        "cross_key": bell_draw(key_list[11], (D, D), D ** -0.5, 0.15625, ((0, 4),)),
        "cross_value": bell_draw(key_list[12], (D, D), D ** -0.5, 0.15625, ((0, 4),)),
        "cross_output": bell_draw(key_list[13], (D, D), (max(1, D * 4 // TXT)) ** -0.5, 0.625, ((0, 4),)),
        "third_gain": jnp.clip(1.0 + 0.1 * jax.random.normal(key_list[14], (D,), jnp.float32), 0.5, 1.5).astype(jnp.bfloat16),
        "third_shift": bell_draw(key_list[15], (D,), 0.3, 2.0, ((0, 4),)),
        "up_weight": bell_draw(key_list[16], (D, FF), D ** -0.5, 0.15625, ((0, 4),)),
        "down_weight": bell_draw(key_list[17], (FF, D), FF ** -0.5, 0.078125, ((0, 4),)),
        "cotangent": bell_draw(key_list[18], (CLIPS, SEQ, D), 1.0, 6.0, ((0, 16), (1, 2))),
    }


EPS = 1e-05
NEG = -1e+30
HIGH = lax.Precision.HIGHEST

@jax.custom_vjp
def low(v):
    return lax.optimization_barrier(v.astype(jnp.bfloat16)).astype(jnp.float32)

@jax.custom_vjp
def low_back(v):
    return v

def low_keep(v):
    return (low(v), None)

def low_pass(kept, grad):
    return (grad,)

def back_keep(v):
    return (v, None)

def back_low(kept, grad):
    return (low(grad),)
low.defvjp(low_keep, low_pass)
low_back.defvjp(back_keep, back_low)

def layer_norm(hidden, gain, shift):
    mean = lax.optimization_barrier(jnp.mean(hidden, axis=-1, keepdims=True))
    centred = hidden - mean
    spread = lax.optimization_barrier(jnp.mean(centred * centred, axis=-1, keepdims=True))
    return centred * lax.rsqrt(spread + EPS) * gain + shift

def product(left, right):
    return jnp.dot(left, right, preferred_element_type=jnp.float32, precision=HIGH)

def softmax_rows(scores):
    top = lax.optimization_barrier(jnp.max(scores, axis=-1, keepdims=True))
    weights = jnp.exp(scores - top)
    return weights / lax.optimization_barrier(jnp.sum(weights, axis=-1, keepdims=True))

def heads_attend(queries, keys, values, allowed):
    scale = HD ** (-0.5)
    raw = jnp.einsum('qhd,khd->hqk', queries, keys, precision=HIGH)
    scores = low_back(scale * raw)
    if allowed is not None:
        scores = jnp.where(allowed, scores, NEG)
    probs = low(softmax_rows(scores))
    joined = jnp.einsum('hqk,khd->qhd', probs, values, precision=HIGH)
    return low(low_back(joined)).reshape(queries.shape[0], H * HD)

def clip_forward(params, frames, text):
    gain_a, shift_a, w_query, w_key, w_value, w_output, gain_b, shift_b, w_cquery, w_ckey, w_cvalue, w_coutput, gain_c, shift_c, w_up, w_down = params
    positions = jnp.arange(SEQ, dtype=jnp.int32)
    causal = positions[None, :] <= positions[:, None]
    normed = low(layer_norm(frames, gain_a, shift_a))
    queries = low(low_back(product(normed, w_query))).reshape(SEQ, H, HD)
    keys = low(low_back(product(normed, w_key))).reshape(SEQ, H, HD)
    values = low(low_back(product(normed, w_value))).reshape(SEQ, H, HD)
    attended = heads_attend(queries, keys, values, causal)
    hidden = frames + low_back(product(attended, w_output))
    normed = low(layer_norm(hidden, gain_b, shift_b))
    queries = low(low_back(product(normed, w_cquery))).reshape(SEQ, H, HD)
    keys = low(low_back(product(text, w_ckey))).reshape(TXT, H, HD)
    values = low(low_back(product(text, w_cvalue))).reshape(TXT, H, HD)
    attended = heads_attend(queries, keys, values, None)
    hidden = hidden + low_back(product(attended, w_coutput))
    normed = low(layer_norm(hidden, gain_c, shift_c))
    inner = low_back(product(normed, w_up))
    activated = low(jax.nn.gelu(inner, approximate=False))
    return hidden + low_back(product(activated, w_down))

def reference(frames, text_states, first_gain, first_shift, self_query, self_key, self_value, self_output, second_gain, second_shift, cross_query, cross_key, cross_value, cross_output, third_gain, third_shift, up_weight, down_weight, cotangent):
    params = tuple((weight.astype(jnp.float32) for weight in (first_gain, first_shift, self_query, self_key, self_value, self_output, second_gain, second_shift, cross_query, cross_key, cross_value, cross_output, third_gain, third_shift, up_weight, down_weight)))

    def forward(weights, frames_full, text_full):

        def one_clip(inputs):
            return jax.checkpoint(clip_forward)(weights, inputs[0], inputs[1])
        return lax.map(one_clip, (frames_full, text_full))
    outputs, pullback = jax.vjp(forward, params, frames.astype(jnp.float32), text_states.astype(jnp.float32))
    grad_params, grad_frames, grad_text = pullback(cotangent.astype(jnp.float32))
    grad_a, grad_b, grad_c, grad_d, grad_e, grad_f, grad_g, grad_h, grad_i, grad_j, grad_k, grad_l, grad_m, grad_n, grad_o, grad_p = grad_params
    return (outputs.astype(jnp.bfloat16), grad_frames, grad_text, grad_a, grad_b, grad_c, grad_d, grad_e, grad_f, grad_g, grad_h, grad_i, grad_j, grad_k, grad_l, grad_m, grad_n, grad_o, grad_p)
```

```python
import math

import jax
import jax.numpy as jnp
from jax import lax
from jax.experimental import pallas as pl
from jax.experimental.pallas import tpu as pltpu
from jax.sharding import PartitionSpec as P

HD = 64
EPS = 1e-05
NEG = -1e30
BF16 = jnp.bfloat16
F32 = jnp.float32
VMEM_LIMIT = 48 * 1024 * 1024
EVERY = ("shard", "ctx", "rep")


def product(left, right):
    return jnp.dot(left, right, preferred_element_type=F32)


def over_rows(left, right):
    return lax.dot_general(left, right, (((0,), (0,)), ((), ())), preferred_element_type=F32)


def against(left, right):
    return lax.dot_general(left, right, (((1,), (1,)), ((), ())), preferred_element_type=F32)


def xor_permute(array, axis, bit):
    return lax.ppermute(array, axis, [(i, i ^ bit) for i in range(lax.axis_size(axis))])


def swap_ctx(array):
    return xor_permute(array, "ctx", 1)


def swap_row(array):
    return xor_permute(array, "rep", 2)


def swap_core(array):
    return xor_permute(array, "rep", 1)


def shifted(block, axis, distance):
    devices = range(lax.axis_size(axis))
    route = [(i - distance, i) for i in devices if i - distance in devices]
    return lax.ppermute(block, axis, route)


def pick(array, index, axis):
    return lax.dynamic_index_in_dim(array, index, axis, keepdims=False)


def both(own):
    return jnp.concatenate([own, swap_core(own)], axis=0)


def pair_sum(left, right, multiply):
    half = left.shape[0] // 2
    other = swap_core(multiply(left[half:], right).astype(BF16))
    return multiply(left[:half], right) + other.astype(F32)


def nt(left, right):
    return lax.dot_general(left, right, (((1,), (1,)), ((), ())), preferred_element_type=F32)


def tn(left, right):
    return lax.dot_general(left, right, (((0,), (0,)), ((), ())), preferred_element_type=F32)


def nn(left, right):
    return lax.dot_general(left, right, (((1,), (0,)), ((), ())), preferred_element_type=F32)


def query_block(span):
    return math.gcd(span, 256)


def key_chunks(causal, block, index):
    if not causal:
        return [(0, None, "none")]
    return [(0, None, "earlier"), (1, (index + 1) * block, "own")]


def masked(scores, mode, position, block, index):
    if mode == "earlier":
        return jnp.where(position > 0, scores, NEG)
    if mode == "own":
        row = lax.broadcasted_iota(jnp.int32, scores.shape, 0)
        column = lax.broadcasted_iota(jnp.int32, scores.shape, 1) + index * block
        return jnp.where(row <= column, scores, NEG)
    return scores


def attend_kernel(causal, position_ref, q_ref, k_ref, v_ref, o_ref, log_ref):
    position = position_ref[0]
    span = q_ref.shape[1]
    block = query_block(span)
    low = lax.broadcasted_iota(jnp.int32, (block, 2 * HD), 1) < HD
    for index in range(span // block):
        rows = pl.ds(index * block, block)
        queries = q_ref[0, rows, :] * BF16(HD ** -0.5)
        parts = []
        for head in range(2):
            side = jnp.where(low == (head == 0), queries, jnp.zeros_like(queries))
            scores = []
            for part, extent, mode in key_chunks(causal, block, index):
                keys = k_ref[part, 0, :extent, :]
                scores.append(masked(nt(keys, side), mode, position, block, index))
            top = scores[0].max(axis=0, keepdims=True)
            for other in scores[1:]:
                top = jnp.maximum(top, other.max(axis=0, keepdims=True))
            weights = [jnp.exp(each - top) for each in scores]
            total = sum(each.sum(axis=0, keepdims=True) for each in weights)
            inverse = 1.0 / total
            out = None
            for weight, (part, extent, mode) in zip(weights, key_chunks(causal, block, index)):
                term = tn(v_ref[part, 0, :extent, :], (weight * inverse).astype(BF16))
                out = term if out is None else out + term
            parts.append(out)
            log_ref[0, 0, head : head + 1, rows] = top + jnp.log(total)
        upper = lax.broadcasted_iota(jnp.int32, parts[0].shape, 0) < HD
        o_ref[0, rows, :] = jnp.where(upper, parts[0], parts[1]).T.astype(BF16)


def attend_back_kernel(
    causal, position_ref, q_ref, k_ref, v_ref, o_ref, g_ref, log_ref, dq_ref, dk_ref, dv_ref, dk_acc, dv_acc
):
    position = position_ref[0]
    span = q_ref.shape[1]
    block = query_block(span)
    low = lax.broadcasted_iota(jnp.int32, (block, 2 * HD), 1) < HD
    dk_acc[...] = jnp.zeros_like(dk_acc)
    dv_acc[...] = jnp.zeros_like(dv_acc)
    for index in range(span // block):
        rows = pl.ds(index * block, block)
        queries = q_ref[0, rows, :] * BF16(HD ** -0.5)
        grads = g_ref[0, rows, :]
        flat = (grads.astype(F32) * o_ref[0, rows, :].astype(F32)).T
        parts = []
        for head in range(2):
            mine = low == (head == 0)
            side = jnp.where(mine, queries, jnp.zeros_like(queries))
            grad = jnp.where(mine, grads, jnp.zeros_like(grads))
            delta = flat[head * HD : (head + 1) * HD].sum(axis=0, keepdims=True)
            log_total = log_ref[0, 0, head : head + 1, rows]
            dq = None
            for part, extent, mode in key_chunks(causal, block, index):
                keys = k_ref[part, 0, :extent, :]
                scores = masked(nt(keys, side), mode, position, block, index)
                probs = jnp.exp(scores - log_total)
                grad_probs = nt(v_ref[part, 0, :extent, :], grad)
                grad_scores = (probs * (grad_probs - delta)).astype(BF16)
                dk_acc[part, :extent, :] += nn(grad_scores, side)
                dv_acc[part, :extent, :] += nn(probs.astype(BF16), grad)
                term = tn(keys, grad_scores)
                dq = term if dq is None else dq + term
            parts.append(dq)
        upper = lax.broadcasted_iota(jnp.int32, parts[0].shape, 0) < HD
        dq_ref[0, rows, :] = (jnp.where(upper, parts[0], parts[1]).T * HD ** -0.5).astype(BF16)
    dk_ref[:, 0] = dk_acc[...].astype(BF16)
    dv_ref[:, 0] = dv_acc[...].astype(BF16)


def attend(position, queries, keys, values, key_base, value_base, causal):
    clips, span, width = queries.shape
    parts, unused, length, unused = keys.shape
    pair = 2 * HD
    pairs = width // pair
    work = 2 * clips * span * length * parts * width
    return pl.pallas_call(
        lambda *refs: attend_kernel(causal, *refs),
        grid=(clips, pairs),
        in_specs=[
            pl.BlockSpec(memory_space=pltpu.SMEM),
            pl.BlockSpec((1, span, pair), lambda b, j: (b, 0, j)),
            pl.BlockSpec((parts, 1, length, pair), lambda b, j: (0, b, 0, key_base + j)),
            pl.BlockSpec((parts, 1, length, pair), lambda b, j: (0, b, 0, value_base + j)),
        ],
        out_specs=[
            pl.BlockSpec((1, span, pair), lambda b, j: (b, 0, j)),
            pl.BlockSpec((1, 1, 2, span), lambda b, j: (b, j, 0, 0)),
        ],
        out_shape=[
            jax.ShapeDtypeStruct((clips, span, width), BF16),
            jax.ShapeDtypeStruct((clips, pairs, 2, span), F32),
        ],
        compiler_params=pltpu.CompilerParams(vmem_limit_bytes=VMEM_LIMIT),
        cost_estimate=pl.CostEstimate(flops=2 * 2 * work, bytes_accessed=8 * clips * span * width, transcendentals=work // (2 * HD)),
    )(position, queries, keys, values)


def attend_back(position, queries, keys, values, out, grad, logs, key_base, value_base, causal):
    clips, span, width = queries.shape
    parts, unused, length, unused = keys.shape
    pair = 2 * HD
    pairs = width // pair
    work = 2 * clips * span * length * parts * width
    row_spec = pl.BlockSpec((1, span, pair), lambda b, j: (b, 0, j))
    return pl.pallas_call(
        lambda *refs: attend_back_kernel(causal, *refs),
        grid=(clips, pairs),
        in_specs=[
            pl.BlockSpec(memory_space=pltpu.SMEM),
            row_spec,
            pl.BlockSpec((parts, 1, length, pair), lambda b, j: (0, b, 0, key_base + j)),
            pl.BlockSpec((parts, 1, length, pair), lambda b, j: (0, b, 0, value_base + j)),
            row_spec,
            row_spec,
            pl.BlockSpec((1, 1, 2, span), lambda b, j: (b, j, 0, 0)),
        ],
        out_specs=[
            row_spec,
            pl.BlockSpec((parts, 1, length, pair), lambda b, j: (0, b, 0, j)),
            pl.BlockSpec((parts, 1, length, pair), lambda b, j: (0, b, 0, j)),
        ],
        out_shape=[
            jax.ShapeDtypeStruct((clips, span, width), BF16),
            jax.ShapeDtypeStruct((parts, clips, length, width), BF16),
            jax.ShapeDtypeStruct((parts, clips, length, width), BF16),
        ],
        scratch_shapes=[
            pltpu.VMEM((parts, length, pair), F32),
            pltpu.VMEM((parts, length, pair), F32),
        ],
        compiler_params=pltpu.CompilerParams(vmem_limit_bytes=VMEM_LIMIT),
        cost_estimate=pl.CostEstimate(flops=2 * 5 * work, bytes_accessed=20 * clips * span * width, transcendentals=work // (2 * HD)),
    )(position, queries, keys, values, out, grad, logs)


def strip_halves(block, strips, core):
    size = block.shape[-1] // (2 * strips)
    return [block[..., (2 * j + core) * size : (2 * j + core + 1) * size] for j in range(strips)]


class Place:
    def __init__(self, width):
        self.shards = lax.axis_size("shard")
        self.ctx = lax.axis_index("ctx")
        self.z = lax.axis_index("shard")
        rep = lax.axis_index("rep")
        self.core = rep % 2
        self.y = rep // 2
        self.staged = (
            self.shards == 4
            and lax.axis_size("ctx") == 2
            and lax.axis_size("rep") == 4
            and (width // self.shards) % (2 * HD) == 0
            and (width // self.shards) % 128 == 0
        )
        self.strips = self.shards if self.staged else 1
        self.spot = jnp.stack([self.z, self.ctx * 2 + self.y, self.core]).astype(jnp.int32)

    def own_columns(self, array):
        rows, width = array.shape
        return lax.dynamic_slice_in_dim(array, self.core * (width // 2), width // 2, 1)

    def own_rows(self, array):
        rows, width = array.shape
        return lax.dynamic_slice_in_dim(array, self.core * (rows // 2), rows // 2, 0)


    def unit_shape(self, batch):
        kind, shards = batch
        if kind == "columns":
            return shards[0].shape[0], sum(s.shape[1] // 2 for s in shards)
        return shards[0].shape[0] // 2, sum(s.shape[1] for s in shards)

    def first_pieces(self, batches):
        shards = [s for kind, each in batches for s in each]
        shapes = [(rows // 4, width) for rows, width in map(self.unit_shape, batches)]

        def spec(kind, quarter, width):
            if kind == "columns":
                return pl.BlockSpec((quarter, width), lambda i, at: (at[1], 0))
            return pl.BlockSpec((quarter, width), lambda i, at: (at[2] * 4 + at[1], 0))

        def kernel(at, *refs):
            ins, outs = list(refs[: len(shards)]), refs[len(shards) :]
            for core in range(2):

                @pl.when(at[2] == core)
                def unused():
                    rest = list(ins)
                    for (kind, each), out in zip(batches, outs):
                        edge = 0
                        for shard in each:
                            block = rest.pop(0)
                            parts = strip_halves(block, self.strips, core) if kind == "columns" else [block[...]]
                            for part in parts:
                                out[:, edge : edge + part.shape[-1]] = part
                                edge += part.shape[-1]

        return pl.pallas_call(
            kernel,
            grid_spec=pltpu.PrefetchScalarGridSpec(
                num_scalar_prefetch=1,
                grid=(1,),
                in_specs=[
                    spec(kind, self.unit_shape((kind, each))[0] // 4, s.shape[1]) for kind, each in batches for s in each
                ],
                out_specs=[pl.BlockSpec(shape, lambda i, at: (0, 0)) for shape in shapes],
            ),
            out_shape=[jax.ShapeDtypeStruct(shape, BF16) for shape in shapes],
            compiler_params=pltpu.CompilerParams(vmem_limit_bytes=VMEM_LIMIT),
        )(self.spot, *shards)

    def exchange_z(self, mine):
        return jnp.stack([xor_permute(mine, "shard", k) for k in range(1, 4)])

    def exchange_plane(self, from_z):
        half = from_z.shape[-1] // 2
        from_x = swap_ctx(from_z)
        from_y = swap_row(from_z)
        return from_z, from_y, from_x, swap_row(from_x[..., :half]), swap_ctx(from_y[..., half:])

    def assemble(self, batch, received, splits=()):
        kind, shards = batch
        rows, width = self.unit_shape(batch)
        quarter, half = rows // 4, width // 2
        edges = [0, *splits, width]
        spans = list(zip(edges[:-1], edges[1:]))
        count = len(shards)

        def step(turn):
            def index(s, k, at):
                now = jnp.maximum(k, 1) - 1
                return (jnp.where(s == turn, now, jnp.where(s < turn, 0, 2)), 0, 0)

            return index

        def own(s, k, at):
            spot = lax.bitwise_xor(at[1], s)
            return (spot, 0) if kind == "columns" else (at[2] * 4 + spot, 0)

        def target(s, k, at):
            return (lax.bitwise_xor(at[0], k) * 4 + lax.bitwise_xor(at[1], s), 0)

        def kernel(at, *refs):
            ins, (z_ref, y_ref, x_ref, xy_ref, yx_ref), outs = refs[:count], refs[count : count + 5], refs[count + 5 :]
            s, k = pl.program_id(0), pl.program_id(1)

            def put(parts):
                edge = 0
                for part in parts:
                    end = edge + part.shape[-1]
                    for (a, b), out in zip(spans, outs):
                        low, high = max(a, edge), min(b, end)
                        if low < high:
                            out[:, low - a : high - a] = part[:, low - edge : high - edge]
                    edge = end

            for core in range(2):

                @pl.when((k == 0) & (at[2] == core))
                def unused():
                    parts = []
                    for block in ins:
                        parts += strip_halves(block, self.strips, core) if kind == "columns" else [block[...]]
                    put(parts)

            for turn, ref in ((0, z_ref), (1, y_ref), (2, x_ref)):

                @pl.when((k > 0) & (s == turn))
                def unused(ref=ref):
                    put([ref[0]])

            @pl.when((k > 0) & (s == 3))
            def unused():
                put([xy_ref[0], yx_ref[0]])

        return pl.pallas_call(
            kernel,
            grid_spec=pltpu.PrefetchScalarGridSpec(
                num_scalar_prefetch=1,
                grid=(4, 4),
                in_specs=[pl.BlockSpec((quarter, s.shape[1]), own) for s in shards]
                + [pl.BlockSpec((1, quarter, width), step(turn)) for turn in range(3)]
                + [pl.BlockSpec((1, quarter, half), step(3))] * 2,
                out_specs=[pl.BlockSpec((quarter, b - a), target) for a, b in spans],
            ),
            out_shape=[jax.ShapeDtypeStruct((4 * rows, b - a), BF16) for a, b in spans],
            compiler_params=pltpu.CompilerParams(vmem_limit_bytes=VMEM_LIMIT),
            cost_estimate=pl.CostEstimate(flops=0, bytes_accessed=16 * rows * width, transcendentals=0),
        )(self.spot, *shards, *received)

    def gather_plain(self, batch, splits=()):
        kind, shards = batch
        whole = [lax.all_gather(s, "shard", axis=0, tiled=True) for s in shards]
        parts = [self.own_columns(w) if kind == "columns" else self.own_rows(w) for w in whole]
        joined = jnp.concatenate(parts, axis=1)
        edges = [0, *splits, joined.shape[1]]
        return [joined[:, a:b] for a, b in zip(edges[:-1], edges[1:])]


    def total(self, grad):
        rows, width = grad.shape[0] // 4, grad.shape[1]
        quarter, half = rows // 4, width // 2
        x, y = self.ctx, self.y
        pieces = grad.reshape(4, 2, 2, quarter, width)
        first, second = pieces[..., :half], pieces[..., half:]

        def plus(left, right):
            return (left.astype(F32) + right.astype(F32)).astype(BF16)

        kept_a = plus(pick(first, x, 1), swap_ctx(pick(first, 1 - x, 1)))
        kept_b = plus(pick(second, y, 2), swap_row(pick(second, 1 - y, 2)))
        kept_a = plus(pick(kept_a, y, 1), swap_row(pick(kept_a, 1 - y, 1)))
        kept_b = plus(pick(kept_b, x, 1), swap_ctx(pick(kept_b, 1 - x, 1)))
        kept = jnp.concatenate([kept_a, kept_b], axis=-1)
        summed = pick(kept, self.z, 0).astype(F32)
        for k in range(1, 4):
            summed = summed + xor_permute(pick(kept, self.z ^ k, 0), "shard", k).astype(F32)
        return lax.all_gather(summed.astype(BF16), ("ctx", "rep"), axis=0, tiled=False)

    def all_sum(self, array):
        array = lax.psum_scatter(array, "shard", scatter_dimension=0, tiled=True)
        return lax.psum(array, ("ctx", "rep"))

    def scatter_columns(self, grad, count):
        rows, width = grad.shape
        each = width // count
        if not self.staged:
            outs = []
            for i in range(count):
                whole = jnp.zeros((rows, 2 * each), BF16)
                part = grad[:, i * each : (i + 1) * each]
                whole = lax.dynamic_update_slice_in_dim(whole, part, self.core * each, 1)
                outs.append(self.all_sum(whole).astype(F32))
            return outs
        total = self.total(grad)
        quarter = total.shape[1]
        total = total.reshape(4, 2, quarter, width)
        strips = self.strips
        size = each // strips

        def kernel(in_ref, *outs):
            for i, out in enumerate(outs):
                for j in range(strips):
                    for core in range(2):
                        edge = i * each + j * size
                        out[:, (2 * j + core) * size : (2 * j + core + 1) * size] = in_ref[
                            0, core, :, edge : edge + size
                        ].astype(F32)

        return pl.pallas_call(
            kernel,
            grid=(4,),
            in_specs=[pl.BlockSpec((1, 2, quarter, width), lambda p: (p, 0, 0, 0))],
            out_specs=[pl.BlockSpec((quarter, 2 * each), lambda p: (p, 0))] * count,
            out_shape=[jax.ShapeDtypeStruct((4 * quarter, 2 * each), F32)] * count,
            compiler_params=pltpu.CompilerParams(vmem_limit_bytes=VMEM_LIMIT),
        )(total)

    def scatter_rows(self, grad):
        if not self.staged:
            rows, width = grad.shape
            whole = jnp.zeros((2 * rows, width), BF16)
            whole = lax.dynamic_update_slice_in_dim(whole, grad, self.core * rows, 0)
            return self.all_sum(whole).astype(F32)
        total = self.total(grad)
        unused, quarter, width = total.shape

        def kernel(in_ref, out_ref):
            out_ref[...] = in_ref[0].astype(F32)

        return pl.pallas_call(
            kernel,
            grid=(2, 4),
            in_specs=[pl.BlockSpec((1, quarter, width), lambda c, p: (p * 2 + c, 0, 0))],
            out_specs=pl.BlockSpec((quarter, width), lambda c, p: (c * 4 + p, 0)),
            out_shape=jax.ShapeDtypeStruct((8 * quarter, width), F32),
            compiler_params=pltpu.CompilerParams(vmem_limit_bytes=VMEM_LIMIT),
        )(total)


def layer_norm(hidden, gain, shift):
    mean = jnp.mean(hidden, axis=-1, keepdims=True)
    centred = hidden - mean
    spread = jnp.mean(centred * centred, axis=-1, keepdims=True)
    return centred * lax.rsqrt(spread + EPS) * gain + shift


def norm_backward(hidden, gain, grad):
    mean = jnp.mean(hidden, axis=-1, keepdims=True)
    centred = hidden - mean
    inverse = lax.rsqrt(jnp.mean(centred * centred, axis=-1, keepdims=True) + EPS)
    unit = centred * inverse
    scaled = grad * gain
    grad_hidden = inverse * (
        scaled - jnp.mean(scaled, axis=-1, keepdims=True) - unit * jnp.mean(scaled * unit, axis=-1, keepdims=True)
    )
    return grad_hidden, jnp.sum(grad * unit, axis=0), jnp.sum(grad, axis=0)


def gelu_parts(pre):
    phi = 0.5 * lax.erfc(-pre * (0.5 ** 0.5))
    slope = phi + pre * jnp.exp(-0.5 * pre * pre) * ((2.0 * math.pi) ** -0.5)
    return pre * phi, slope


def local(
    frames,
    text_states,
    first_gain,
    first_shift,
    self_query,
    self_key,
    self_value,
    self_output,
    second_gain,
    second_shift,
    cross_query,
    cross_key,
    cross_value,
    cross_output,
    third_gain,
    third_shift,
    up_weight,
    down_weight,
    cotangent,
):
    clips, span, width = frames.shape
    texts = text_states.shape[1]
    rows = clips * span
    place = Place(width)
    position = place.ctx.astype(jnp.int32).reshape(1)
    half = width // 2
    pairs = half // (2 * HD)

    batches = [
        ("columns", [self_query, self_key, self_value]),
        ("rows", [self_output]),
        ("columns", [cross_query, cross_key, cross_value]),
        ("rows", [cross_output]),
        ("columns", [up_weight]),
        ("rows", [down_weight]),
    ]
    cuts = [[half], [], [half], [], [], []]
    if place.staged:
        pieces = place.first_pieces(batches)
        from_z = [place.exchange_z(piece) for piece in pieces]
        weights = [
            place.assemble(batch, place.exchange_plane(each), cut) for batch, each, cut in zip(batches, from_z, cuts)
        ]
    else:
        weights = [place.gather_plain(batch, cut) for batch, cut in zip(batches, cuts)]
    (w_query, w_key_value), (w_out,), (w_cross_query, w_cross_kv), (w_cross_out,), (w_up,), (w_down,) = weights
    norms = jnp.stack([first_gain, first_shift, second_gain, second_shift, third_gain, third_shift])
    norms = lax.all_gather(norms, "shard", axis=1, tiled=True).astype(F32)
    gain_one, shift_one, gain_two, shift_two, gain_three, shift_three = (norms[i] for i in range(6))

    frames_own = frames.reshape(rows, width)
    frames_before = shifted(frames_own, "ctx", 1)
    frames_all = jnp.concatenate([both(frames_before), both(frames_own)], axis=0)
    normed_one = layer_norm(frames_all.astype(F32), gain_one, shift_one).astype(BF16)
    normed_own = normed_one[2 * rows :]
    queries = product(normed_own, w_query).astype(BF16).reshape(2 * clips, span, half)
    key_values = product(normed_one, w_key_value).astype(BF16).reshape(2, 2 * clips, span, width)
    attended, logs = attend(position, queries, key_values, key_values, 0, pairs, True)
    attended = attended.reshape(2 * rows, half)
    hidden_zero = frames_own.astype(F32)
    hidden_one = hidden_zero + pair_sum(attended, w_out, product)

    normed_two = both(layer_norm(hidden_one, gain_two, shift_two).astype(BF16))
    text = both(text_states.reshape(clips * texts, width))
    cross_q = product(normed_two, w_cross_query).astype(BF16).reshape(2 * clips, span, half)
    cross_kv = product(text, w_cross_kv).astype(BF16).reshape(1, 2 * clips, texts, width)
    cross_att, cross_logs = attend(position, cross_q, cross_kv, cross_kv, 0, pairs, False)
    cross_att = cross_att.reshape(2 * rows, half)
    hidden_two = hidden_one + pair_sum(cross_att, w_cross_out, product)

    normed_three = both(layer_norm(hidden_two, gain_three, shift_three).astype(BF16))
    pre_act = product(normed_three, w_up)
    activated, slope = gelu_parts(pre_act)
    activated = activated.astype(BF16)
    mixed = (hidden_two + pair_sum(activated, w_down, product)).astype(BF16).reshape(clips, span, width)

    cotangent_own = cotangent.reshape(rows, width)
    grad_branch = both(cotangent_own)
    grad_pre = (against(grad_branch, w_down) * slope).astype(BF16)
    grad_down = over_rows(activated, grad_branch).astype(BF16)
    grad_up = over_rows(normed_three, grad_pre).astype(BF16)
    grad_hid, grad_gain_three, grad_shift_three = norm_backward(
        hidden_two, gain_three, pair_sum(grad_pre, w_up, against)
    )
    grad_res = cotangent_own.astype(F32) + grad_hid

    grad_branch = both(grad_res.astype(BF16))
    grad_cross_out = over_rows(cross_att, grad_branch).astype(BF16)
    grad_catt = against(grad_branch, w_cross_out).astype(BF16).reshape(2 * clips, span, half)
    grad_cq, part_ck, part_cv = attend_back(
        position, cross_q, cross_kv, cross_kv, cross_att.reshape(2 * clips, span, half), grad_catt, cross_logs, 0, pairs, False
    )
    grad_cq = grad_cq.reshape(2 * rows, half)
    part = jnp.concatenate([part_ck, part_cv], axis=-1).reshape(2 * clips, texts, width)
    grad_ckv = (part.astype(F32) + swap_ctx(part).astype(F32)).astype(BF16)
    share = texts // lax.axis_size("ctx")
    start = place.ctx * share

    def part_rows(array):
        array = array.reshape(2 * clips, texts, width)
        return lax.dynamic_slice_in_dim(array, start, share, 1).reshape(2 * clips * share, width)

    grad_cross_kv = over_rows(part_rows(text), part_rows(grad_ckv)).astype(BF16)
    grad_text = pair_sum(grad_ckv.reshape(2 * clips * texts, width), w_cross_kv, against).reshape(clips, texts, width)
    grad_cross_query = over_rows(normed_two, grad_cq).astype(BF16)
    grad_hid, grad_gain_two, grad_shift_two = norm_backward(
        hidden_one, gain_two, pair_sum(grad_cq, w_cross_query, against)
    )
    grad_res = grad_res + grad_hid

    grad_branch = both(grad_res.astype(BF16))
    grad_out = over_rows(attended, grad_branch).astype(BF16)
    grad_att = against(grad_branch, w_out).astype(BF16).reshape(2 * clips, span, half)
    grad_q, grad_k, grad_v = attend_back(
        position,
        queries,
        key_values,
        key_values,
        attended.reshape(2 * clips, span, half),
        grad_att,
        logs,
        0,
        pairs,
        True,
    )
    grad_q = grad_q.reshape(2 * rows, half)
    grad_k = grad_k.reshape(4 * rows, half)
    grad_v = grad_v.reshape(4 * rows, half)
    grad_query = over_rows(normed_own, grad_q).astype(BF16)
    grad_kv = jnp.concatenate([grad_k, grad_v], axis=1)
    grad_key_value = over_rows(normed_one, grad_kv).astype(BF16)
    grad_normed_before = pair_sum(grad_kv[: 2 * rows], w_key_value, against)
    returned = shifted(grad_normed_before.astype(BF16), "ctx", -1)
    grad_normed = pair_sum(grad_q, w_query, against) + pair_sum(grad_kv[2 * rows :], w_key_value, against)
    grad_hid, grad_gain_one, grad_shift_one = norm_backward(
        hidden_zero, gain_one, grad_normed + returned.astype(F32)
    )
    grad_frames = (grad_res + grad_hid).reshape(clips, span, width)

    total_down = place.scatter_rows(grad_down)
    (total_up,) = place.scatter_columns(grad_up, 1)
    total_cross_out = place.scatter_rows(grad_cross_out)
    total_cross_key, total_cross_value = place.scatter_columns(grad_cross_kv, 2)
    (total_cross_query,) = place.scatter_columns(grad_cross_query, 1)
    total_out = place.scatter_rows(grad_out)
    total_key, total_value = place.scatter_columns(grad_key_value, 2)
    (total_query,) = place.scatter_columns(grad_query, 1)
    small = jnp.stack(
        [grad_gain_one, grad_shift_one, grad_gain_two, grad_shift_two, grad_gain_three, grad_shift_three]
    )
    small = lax.psum(small, EVERY)
    share = width // place.shards
    small = lax.dynamic_slice_in_dim(small, place.z * share, share, 1)
    return (
        mixed,
        grad_frames,
        grad_text,
        small[0],
        small[1],
        total_query,
        total_key,
        total_value,
        total_out,
        small[2],
        small[3],
        total_cross_query,
        total_cross_key,
        total_cross_value,
        total_cross_out,
        small[4],
        small[5],
        total_up,
        total_down,
    )


def solution(mesh):
    rows = P(("shard", "rep"), "ctx", None)
    vector = P("shard")
    weight = P("shard", None)
    block = (vector, vector, weight, weight, weight, weight)
    in_specs = (rows, P(("shard", "rep"), None, None), *block, *block, vector, vector, weight, weight, rows)
    out_specs = (rows, rows, P(("shard", "rep"), None, None), *block, *block, vector, vector, weight, weight)
    return jax.shard_map(local, mesh=mesh, in_specs=in_specs, out_specs=out_specs, check_vma=False)
```

```python
import math

import jax
import jax.numpy as jnp
from jax import lax
from jax.experimental import pallas as pl
from jax.experimental.pallas import tpu as pltpu
from jax.sharding import PartitionSpec as P

HD = 64
EPS = 1e-05
NEG = -1e30
BF16 = jnp.bfloat16
F32 = jnp.float32
VMEM_LIMIT = 48 * 1024 * 1024
PLANE = ("ctx", "y")
FEED = ("shard", "y")
EVERY = ("shard", "ctx", "y", "core")


def product(left, right):
    return jnp.dot(left, right, preferred_element_type=F32)


def over_rows(left, right):
    return lax.dot_general(left, right, (((0,), (0,)), ((), ())), preferred_element_type=F32)


def against(left, right):
    return lax.dot_general(left, right, (((1,), (1,)), ((), ())), preferred_element_type=F32)


def xor_permute(array, axis, bit):
    return lax.ppermute(array, axis, [(i, i ^ bit) for i in range(lax.axis_size(axis))])


def swap_ctx(array):
    return xor_permute(array, "ctx", 1)


def swap_row(array):
    return xor_permute(array, "y", 1)


def swap_core(array):
    return xor_permute(array, "core", 1)


def tied(*groups):
    return lax.optimization_barrier(groups)


def shifted(block, axis, distance):
    devices = range(lax.axis_size(axis))
    route = [(i - distance, i) for i in devices if i - distance in devices]
    return lax.ppermute(block, axis, route)


def pick(array, index, axis):
    return lax.dynamic_index_in_dim(array, index, axis, keepdims=False)


def both(own):
    return jnp.concatenate([own, swap_core(own)], axis=0)


def pair_sum(left, right, multiply):
    half = left.shape[0] // 2
    other = swap_core(multiply(left[half:], right).astype(BF16))
    return multiply(left[:half], right) + other.astype(F32)


class QuadSum:
    def __init__(self, near, far, right, multiply):
        half = near.shape[0] // 2
        sent = jnp.concatenate(
            [multiply(far[half:], right).astype(BF16), multiply(near[half:], right).astype(BF16)], axis=0
        )
        self.parts = sent, multiply(far[:half], right), multiply(near[:half], right)

    def cores(self):
        sent, far, near = self.parts
        half = near.shape[0]
        got = swap_core(sent).astype(F32)
        return (far + got[:half]).astype(BF16), near + got[half:]

    def total(self):
        far, near = self.cores()
        return near + swap_ctx(far).astype(F32)


def nt(left, right):
    return lax.dot_general(left, right, (((1,), (1,)), ((), ())), preferred_element_type=F32)


def tn(left, right):
    return lax.dot_general(left, right, (((0,), (0,)), ((), ())), preferred_element_type=F32)


def nn(left, right):
    return lax.dot_general(left, right, (((1,), (0,)), ((), ())), preferred_element_type=F32)


def query_block(span):
    return math.gcd(span, 256)


def key_chunks(causal, block, index):
    if not causal:
        return [(0, None, "none")]
    return [(0, None, "earlier"), (1, (index + 1) * block, "own")]


def masked(scores, mode, position, block, index):
    if mode == "earlier":
        return jnp.where(position > 0, scores, NEG)
    if mode == "own":
        row = lax.broadcasted_iota(jnp.int32, scores.shape, 0)
        column = lax.broadcasted_iota(jnp.int32, scores.shape, 1) + index * block
        return jnp.where(row <= column, scores, NEG)
    return scores


def attend_kernel(causal, position_ref, q_ref, k_ref, v_ref, o_ref, log_ref):
    position = position_ref[0]
    span = q_ref.shape[1]
    block = query_block(span)
    low = lax.broadcasted_iota(jnp.int32, (block, 2 * HD), 1) < HD
    for index in range(span // block):
        rows = pl.ds(index * block, block)
        queries = q_ref[0, rows, :] * BF16(HD ** -0.5)
        parts = []
        for head in range(2):
            side = jnp.where(low == (head == 0), queries, jnp.zeros_like(queries))
            scores = []
            for part, extent, mode in key_chunks(causal, block, index):
                keys = k_ref[part, 0, :extent, :]
                scores.append(masked(nt(keys, side), mode, position, block, index))
            top = scores[0].max(axis=0, keepdims=True)
            for other in scores[1:]:
                top = jnp.maximum(top, other.max(axis=0, keepdims=True))
            weights = [jnp.exp(each - top) for each in scores]
            total = sum(each.sum(axis=0, keepdims=True) for each in weights)
            inverse = 1.0 / total
            out = None
            for weight, (part, extent, mode) in zip(weights, key_chunks(causal, block, index)):
                term = tn(v_ref[part, 0, :extent, :], (weight * inverse).astype(BF16))
                out = term if out is None else out + term
            parts.append(out)
            log_ref[0, 0, head : head + 1, rows] = top + jnp.log(total)
        upper = lax.broadcasted_iota(jnp.int32, parts[0].shape, 0) < HD
        o_ref[0, rows, :] = jnp.where(upper, parts[0], parts[1]).T.astype(BF16)


def attend_back_kernel(
    causal, position_ref, q_ref, k_ref, v_ref, o_ref, g_ref, log_ref, dq_ref, dk_ref, dv_ref, dk_acc, dv_acc
):
    position = position_ref[0]
    span = q_ref.shape[1]
    block = query_block(span)
    low = lax.broadcasted_iota(jnp.int32, (block, 2 * HD), 1) < HD
    dk_acc[...] = jnp.zeros_like(dk_acc)
    dv_acc[...] = jnp.zeros_like(dv_acc)
    for index in range(span // block):
        rows = pl.ds(index * block, block)
        queries = q_ref[0, rows, :] * BF16(HD ** -0.5)
        grads = g_ref[0, rows, :]
        flat = (grads.astype(F32) * o_ref[0, rows, :].astype(F32)).T
        parts = []
        for head in range(2):
            mine = low == (head == 0)
            side = jnp.where(mine, queries, jnp.zeros_like(queries))
            grad = jnp.where(mine, grads, jnp.zeros_like(grads))
            delta = flat[head * HD : (head + 1) * HD].sum(axis=0, keepdims=True)
            log_total = log_ref[0, 0, head : head + 1, rows]
            dq = None
            for part, extent, mode in key_chunks(causal, block, index):
                keys = k_ref[part, 0, :extent, :]
                scores = masked(nt(keys, side), mode, position, block, index)
                probs = jnp.exp(scores - log_total)
                grad_probs = nt(v_ref[part, 0, :extent, :], grad)
                grad_scores = (probs * (grad_probs - delta)).astype(BF16)
                dk_acc[part, :extent, :] += nn(grad_scores, side)
                dv_acc[part, :extent, :] += nn(probs.astype(BF16), grad)
                term = tn(keys, grad_scores)
                dq = term if dq is None else dq + term
            parts.append(dq)
        upper = lax.broadcasted_iota(jnp.int32, parts[0].shape, 0) < HD
        dq_ref[0, rows, :] = (jnp.where(upper, parts[0], parts[1]).T * HD ** -0.5).astype(BF16)
    dk_ref[:, 0] = dk_acc[...].astype(BF16)
    dv_ref[:, 0] = dv_acc[...].astype(BF16)


def attend(position, queries, keys, values, key_base, value_base, causal):
    clips, span, width = queries.shape
    parts, unused, length, unused = keys.shape
    pair = 2 * HD
    pairs = width // pair
    work = 2 * clips * span * length * parts * width
    return pl.pallas_call(
        lambda *refs: attend_kernel(causal, *refs),
        grid=(clips, pairs),
        in_specs=[
            pl.BlockSpec(memory_space=pltpu.SMEM),
            pl.BlockSpec((1, span, pair), lambda b, j: (b, 0, j)),
            pl.BlockSpec((parts, 1, length, pair), lambda b, j: (0, b, 0, key_base + j)),
            pl.BlockSpec((parts, 1, length, pair), lambda b, j: (0, b, 0, value_base + j)),
        ],
        out_specs=[
            pl.BlockSpec((1, span, pair), lambda b, j: (b, 0, j)),
            pl.BlockSpec((1, 1, 2, span), lambda b, j: (b, j, 0, 0)),
        ],
        out_shape=[
            jax.ShapeDtypeStruct((clips, span, width), BF16),
            jax.ShapeDtypeStruct((clips, pairs, 2, span), F32),
        ],
        compiler_params=pltpu.CompilerParams(vmem_limit_bytes=VMEM_LIMIT),
        cost_estimate=pl.CostEstimate(flops=0, bytes_accessed=0, transcendentals=0),
    )(position, queries, keys, values)


def attend_back(position, queries, keys, values, out, grad, logs, key_base, value_base, causal):
    clips, span, width = queries.shape
    parts, unused, length, unused = keys.shape
    pair = 2 * HD
    pairs = width // pair
    work = 2 * clips * span * length * parts * width
    row_spec = pl.BlockSpec((1, span, pair), lambda b, j: (b, 0, j))
    return pl.pallas_call(
        lambda *refs: attend_back_kernel(causal, *refs),
        grid=(clips, pairs),
        in_specs=[
            pl.BlockSpec(memory_space=pltpu.SMEM),
            row_spec,
            pl.BlockSpec((parts, 1, length, pair), lambda b, j: (0, b, 0, key_base + j)),
            pl.BlockSpec((parts, 1, length, pair), lambda b, j: (0, b, 0, value_base + j)),
            row_spec,
            row_spec,
            pl.BlockSpec((1, 1, 2, span), lambda b, j: (b, j, 0, 0)),
        ],
        out_specs=[
            row_spec,
            pl.BlockSpec((parts, 1, length, pair), lambda b, j: (0, b, 0, j)),
            pl.BlockSpec((parts, 1, length, pair), lambda b, j: (0, b, 0, j)),
        ],
        out_shape=[
            jax.ShapeDtypeStruct((clips, span, width), BF16),
            jax.ShapeDtypeStruct((parts, clips, length, width), BF16),
            jax.ShapeDtypeStruct((parts, clips, length, width), BF16),
        ],
        scratch_shapes=[
            pltpu.VMEM((parts, length, pair), F32),
            pltpu.VMEM((parts, length, pair), F32),
        ],
        compiler_params=pltpu.CompilerParams(vmem_limit_bytes=VMEM_LIMIT),
        cost_estimate=pl.CostEstimate(flops=0, bytes_accessed=0, transcendentals=0),
    )(position, queries, keys, values, out, grad, logs)


def strip_parts(block, strips, share, index):
    size = block.shape[-1] // (share * strips)
    return [block[..., (share * j + index) * size : (share * j + index + 1) * size] for j in range(strips)]


KINDS = {"columns": (True, 2, 4), "rows": (False, 2, 4), "feed_columns": (True, 4, 2), "feed_rows": (False, 4, 2)}


class Place:
    def __init__(self, width):
        self.shards = lax.axis_size("shard")
        self.ctx = lax.axis_index("ctx")
        self.z = lax.axis_index("shard")
        self.core = lax.axis_index("core")
        self.y = lax.axis_index("y")
        self.staged = (
            self.shards == 4
            and lax.axis_size("ctx") == 2
            and lax.axis_size("y") == 2
            and (width // self.shards) % (2 * HD) == 0
            and (width // self.shards) % 128 == 0
        )
        self.strips = self.shards if self.staged else 1
        self.quarter = width // 16
        self.spot = jnp.stack(
            [self.z, self.ctx * 2 + self.y, self.y, self.core, self.core * 2 + self.ctx]
        ).astype(jnp.int32)

    def own_columns(self, array):
        rows, width = array.shape
        return lax.dynamic_slice_in_dim(array, self.core * (width // 2), width // 2, 1)

    def own_rows(self, array):
        rows, width = array.shape
        return lax.dynamic_slice_in_dim(array, self.core * (rows // 2), rows // 2, 0)


    def own_spec(self, kind, shard, turn):
        columns, share, pieces = KINDS[kind]
        rows, width = shard.shape
        if columns:
            return pl.BlockSpec((rows // pieces, width), lambda *at: (turn(*at), 0))
        which = 3 if share == 2 else 4
        return pl.BlockSpec(
            (rows // (share * pieces), width), lambda *at: (at[-1][which] * pieces + turn(*at), 0)
        )

    def own_parts(self, batch, blocks, at, store, when=True):
        for (kind, shard, row, column), block in zip(batch, blocks):
            columns, share, pieces = KINDS[kind]
            if not columns:

                @pl.when(when)
                def unused(row=row, column=column, block=block):
                    store(row, column, block[...])

                continue
            for index in range(share):

                @pl.when(when & (at[3 if share == 2 else 4] == index))
                def unused(row=row, column=column, block=block, share=share, index=index):
                    edge = column
                    for part in strip_parts(block, self.strips, share, index):
                        store(row, edge, part)
                        edge += part.shape[-1]

    def first_pieces(self, batches, shapes):
        entries = [entry for batch in batches for entry in batch]

        def here(kind):
            return lambda i, at: at[1 if KINDS[kind][2] == 4 else 2]

        def kernel(at, *refs):
            ins, outs = list(refs[: len(entries)]), refs[len(entries) :]
            for batch, out in zip(batches, outs):

                def store(row, column, part, out=out):
                    out[row : row + part.shape[0], column : column + part.shape[1]] = part

                self.own_parts(batch, [ins.pop(0) for entry in batch], at, store)

        return pl.pallas_call(
            kernel,
            grid_spec=pltpu.PrefetchScalarGridSpec(
                num_scalar_prefetch=1,
                grid=(1,),
                in_specs=[self.own_spec(kind, shard, here(kind)) for kind, shard, row, column in entries],
                out_specs=[pl.BlockSpec(shape, lambda i, at: (0, 0)) for shape in shapes],
            ),
            out_shape=[jax.ShapeDtypeStruct(shape, BF16) for shape in shapes],
            compiler_params=pltpu.CompilerParams(vmem_limit_bytes=VMEM_LIMIT),
        )(self.spot, *[shard for kind, shard, row, column in entries])

    def exchange_z(self, mine):
        return lax.all_gather(mine, "shard", axis=0, tiled=False)

    def foreign(self, gathered):
        return jnp.stack([pick(gathered, self.z ^ k, 0) for k in range(1, 4)])

    def exchange_sides(self, from_z):
        return from_z, swap_row(from_z), swap_ctx(from_z)

    def corners(self, sides):
        from_z, from_y, from_x = sides
        half = from_z.shape[-1] // 2
        return from_z, from_y, from_x, from_x[..., :half], from_y[..., half:]

    def exchange_corners(self, state):
        from_z, from_y, from_x, to_y, to_x = state
        return [from_z], [from_y], [from_x], [swap_row(to_y), swap_ctx(to_x)]

    def assemble(self, batch, turns, outputs):
        pieces = len(turns)
        here = 1 if pieces == 4 else 2
        count = len(batch)
        received = [(turn, array) for turn, arrays in enumerate(turns) for array in arrays]

        def step(turn, array):
            def index(s, k, at):
                now = jnp.maximum(k, 1) - 1
                return (jnp.where(s == turn, now, jnp.where(s < turn, 0, 2)), 0, 0)

            return pl.BlockSpec((1, *array.shape[1:]), index)

        def target(s, k, at):
            return (lax.bitwise_xor(at[0], k) * pieces + lax.bitwise_xor(at[here], s), 0)

        def kernel(at, *refs):
            ins, others, outs = refs[:count], refs[count : count + len(received)], refs[count + len(received) :]
            s, k = pl.program_id(0), pl.program_id(1)

            def store(row, column, part):
                for (first, rows, left, columns), out in zip(outputs, outs):
                    top, bottom = max(first, row), min(first + rows, row + part.shape[0])
                    low, high = max(left, column), min(left + columns, column + part.shape[1])
                    if top < bottom and low < high:
                        out[top - first : bottom - first, low - left : high - left] = part[
                            top - row : bottom - row, low - column : high - column
                        ]

            self.own_parts(batch, ins, at, store, k == 0)
            for turn in range(pieces):

                @pl.when((k > 0) & (s == turn))
                def unused(turn=turn):
                    edge = 0
                    for (which, array), ref in zip(received, others):
                        if which == turn:
                            store(0, edge, ref[0])
                            edge += array.shape[2]

        return pl.pallas_call(
            kernel,
            grid_spec=pltpu.PrefetchScalarGridSpec(
                num_scalar_prefetch=1,
                grid=(pieces, 4),
                in_specs=[
                    self.own_spec(kind, shard, lambda s, k, at: lax.bitwise_xor(at[here], s))
                    for kind, shard, row, column in batch
                ]
                + [step(turn, array) for turn, array in received],
                out_specs=[pl.BlockSpec((rows, columns), target) for first, rows, left, columns in outputs],
            ),
            out_shape=[
                jax.ShapeDtypeStruct((4 * pieces * rows, columns), BF16) for first, rows, left, columns in outputs
            ],
            compiler_params=pltpu.CompilerParams(vmem_limit_bytes=VMEM_LIMIT),
            cost_estimate=pl.CostEstimate(flops=0, bytes_accessed=0, transcendentals=0),
        )(self.spot, *[shard for kind, shard, row, column in batch], *[array for turn, array in received])

    def gather_plain(self, kind, *shards):
        whole = [lax.all_gather(s, "shard", axis=0, tiled=True) for s in shards]
        parts = [self.own_columns(w) if KINDS[kind][0] else self.own_rows(w) for w in whole]
        return jnp.concatenate(parts, axis=1)


    def first_sends(self, grad):
        rows, width = grad.shape[0] // 4, grad.shape[1]
        quarter, half = rows // 4, width // 2
        pieces = grad.reshape(4, 2, 2, quarter, width)
        first, second = pieces[..., :half], pieces[..., half:]
        x, y = self.ctx, self.y
        return pick(first, x, 1), pick(second, y, 2), pick(first, 1 - x, 1), pick(second, 1 - y, 2)

    def first_swap(self, sends):
        keep_a, keep_b, send_a, send_b = sends
        return keep_a, keep_b, swap_ctx(send_a), swap_row(send_b)

    def second_swap(self, state):
        keep_a, keep_b, got_a, got_b = state
        kept_a, kept_b = plus(keep_a, got_a), plus(keep_b, got_b)
        x, y = self.ctx, self.y
        return pick(kept_a, y, 1), pick(kept_b, x, 1), swap_row(pick(kept_a, 1 - y, 1)), swap_ctx(pick(kept_b, 1 - x, 1))

    def second_sum(self, state):
        keep_a, keep_b, got_a, got_b = state
        return jnp.concatenate([plus(keep_a, got_a), plus(keep_b, got_b)], axis=-1)

    def shard_sum(self, kept):
        return lax.psum_scatter(kept, "shard", scatter_dimension=0, tiled=False)

    def packed(self, piece):
        a, b = jnp.split(piece, 2, axis=1)
        block = a.shape[1] // 2
        part, short = block // 2, piece.shape[0] // 2
        rows = [each[:, part + block :] for each in (a, b)]
        return jnp.concatenate(
            [
                jnp.concatenate([a[:, :part], b[:, :part]], axis=1),
                a[:, part : part + block],
                b[:, part : part + block],
                *[jnp.concatenate([each[:short], each[short:]], axis=1) for each in rows],
            ],
            axis=0,
        )

    def spread(self, piece):
        half = piece.shape[-1] // 2
        from_y, from_x = swap_row(piece), swap_ctx(piece)
        corner = jnp.concatenate([swap_row(from_x[..., :half]), swap_ctx(from_y[..., half:])], axis=-1)
        own = jnp.stack([piece, from_y, from_x, corner])
        return own, swap_core(own)

    def feed_gradient(self, lefts, rights, which, joined=None):
        width, columns = lefts[0].shape[1], rights[0].shape[1]
        rows, block = width // 4, columns // 2
        piece = rows // 2
        count = len(lefts)

        def kernel(*refs):
            total = tn(refs[0][...], refs[count][...])
            for i in range(1, count):
                total = total + tn(refs[i][...], refs[count + i][...])
            refs[-1][...] = total.astype(BF16).reshape(refs[-1].shape)

        into = [] if joined is None else [joined]
        return pl.pallas_call(
            kernel,
            grid=(4, 2),
            in_specs=[pl.BlockSpec((each.shape[0], rows), lambda z, j: (0, z)) for each in lefts]
            + [pl.BlockSpec((each.shape[0], block), lambda z, j: (0, j)) for each in rights]
            + [pl.BlockSpec(memory_space=pl.ANY) for each in into],
            out_specs=pl.BlockSpec((1, 2, piece, block), lambda z, j: (z, 0, which, j)),
            out_shape=jax.ShapeDtypeStruct((4, 2, 2 * piece, columns), BF16),
            input_output_aliases={2 * count: 0} if into else {},
            compiler_params=pltpu.CompilerParams(vmem_limit_bytes=VMEM_LIMIT),
        )(*lefts, *rights, *into)

    def finish_up(self, own, other):
        piece, columns = own.shape[1] // 2, own.shape[2]
        size = columns // self.strips

        def spec(x):
            return pl.BlockSpec((1, piece, columns), lambda y, at: (lax.bitwise_xor(2 * x + y, at[1]), 0, 0))

        def kernel(at, *refs):
            out_ref = refs[4]
            for mine in range(2):

                @pl.when(at[3] == mine)
                def unused(mine=mine):
                    for core in range(2):
                        for x in range(2):
                            source = refs[x] if core == mine else refs[2 + x]
                            for j in range(self.strips):
                                edge = (4 * j + 2 * core + x) * size
                                out_ref[:, edge : edge + size] = source[0, :, j * size : (j + 1) * size].astype(F32)

        return pl.pallas_call(
            kernel,
            grid_spec=pltpu.PrefetchScalarGridSpec(
                num_scalar_prefetch=1,
                grid=(2,),
                in_specs=[spec(0), spec(1)] * 2,
                out_specs=pl.BlockSpec((piece, 4 * columns), lambda y, at: (y, 0)),
            ),
            out_shape=jax.ShapeDtypeStruct((2 * piece, 4 * columns), F32),
            compiler_params=pltpu.CompilerParams(vmem_limit_bytes=VMEM_LIMIT),
        )(self.spot, own, own, other, other)

    def finish_down(self, own, other):
        piece, columns = own.shape[1] // 2, own.shape[2]

        def kernel(at, own_ref, other_ref, out_ref):
            mine = pl.program_id(0) == at[3]

            @pl.when(mine)
            def unused():
                out_ref[...] = own_ref[0].astype(F32)

            @pl.when(jnp.logical_not(mine))
            def unused():
                out_ref[...] = other_ref[0].astype(F32)

        return pl.pallas_call(
            kernel,
            grid_spec=pltpu.PrefetchScalarGridSpec(
                num_scalar_prefetch=1,
                grid=(2, 4),
                in_specs=[
                    pl.BlockSpec((1, piece, columns), lambda c, p, at: (lax.bitwise_xor(p, at[1]), 1, 0))
                ] * 2,
                out_specs=pl.BlockSpec((piece, columns), lambda c, p, at: (c * 4 + p, 0)),
            ),
            out_shape=jax.ShapeDtypeStruct((8 * piece, columns), F32),
            compiler_params=pltpu.CompilerParams(vmem_limit_bytes=VMEM_LIMIT),
        )(self.spot, own, other)

    def all_sum(self, array):
        array = lax.psum_scatter(array, "shard", scatter_dimension=0, tiled=True)
        return lax.psum(array, ("ctx", "y", "core"))

    def plain_columns(self, grad, count):
        rows, width = grad.shape
        each = width // count
        outs = []
        for i in range(count):
            whole = jnp.zeros((rows, 2 * each), BF16)
            part = grad[:, i * each : (i + 1) * each]
            whole = lax.dynamic_update_slice_in_dim(whole, part, self.core * each, 1)
            outs.append(self.all_sum(whole).astype(F32))
        return outs

    def plain_rows(self, grad):
        rows, width = grad.shape
        whole = jnp.zeros((2 * rows, width), BF16)
        whole = lax.dynamic_update_slice_in_dim(whole, grad, self.core * rows, 0)
        return self.all_sum(whole).astype(F32)

    def finish_columns(self, own, other, count):
        width = own.shape[2]
        quarter = self.quarter
        size = width // self.strips

        def spec(j):
            return pl.BlockSpec((1, quarter, width), lambda p, at: (lax.bitwise_xor(p, at[1]), j, 0))

        def kernel(at, *refs):
            outs = refs[2 * count :]
            for mine in range(2):

                @pl.when(at[3] == mine)
                def unused(mine=mine):
                    for core in range(2):
                        ins = refs[:count] if core == mine else refs[count : 2 * count]
                        for source, out in zip(ins, outs):
                            for j in range(self.strips):
                                out[:, (2 * j + core) * size : (2 * j + core + 1) * size] = source[
                                    0, :, j * size : (j + 1) * size
                                ].astype(F32)

        return pl.pallas_call(
            kernel,
            grid_spec=pltpu.PrefetchScalarGridSpec(
                num_scalar_prefetch=1,
                grid=(4,),
                in_specs=[spec(j) for j in range(count)] * 2,
                out_specs=[pl.BlockSpec((quarter, 2 * width), lambda p, at: (p, 0))] * count,
            ),
            out_shape=[jax.ShapeDtypeStruct((4 * quarter, 2 * width), F32)] * count,
            compiler_params=pltpu.CompilerParams(vmem_limit_bytes=VMEM_LIMIT),
        )(self.spot, *([own] * count), *([other] * count))

    def finish_rows(self, own, other):
        width = own.shape[2]
        short = self.quarter // 2
        first = 3 * self.quarter // short
        spec = [
            pl.BlockSpec((1, short, width), lambda c, p, at, j=j: (lax.bitwise_xor(p, at[1]), first + j, 0))
            for j in range(2)
        ]

        def kernel(at, *refs):
            out_ref = refs[4]
            mine = pl.program_id(0) == at[3]

            def put(blocks):
                for j, block in enumerate(blocks):
                    out_ref[:, j * width : (j + 1) * width] = block[0].astype(F32)

            @pl.when(mine)
            def unused():
                put(refs[:2])

            @pl.when(jnp.logical_not(mine))
            def unused():
                put(refs[2:4])

        return pl.pallas_call(
            kernel,
            grid_spec=pltpu.PrefetchScalarGridSpec(
                num_scalar_prefetch=1,
                grid=(2, 4),
                in_specs=spec + spec,
                out_specs=pl.BlockSpec((short, 2 * width), lambda c, p, at: (c * 4 + p, 0)),
            ),
            out_shape=jax.ShapeDtypeStruct((8 * short, 2 * width), F32),
            compiler_params=pltpu.CompilerParams(vmem_limit_bytes=VMEM_LIMIT),
        )(self.spot, own, own, other, other)

    def gather_norms(self, shards):
        norms = jnp.stack(shards)
        if not self.staged:
            return lax.all_gather(norms, "shard", axis=1, tiled=True).astype(F32)
        whole = jnp.zeros((4, *norms.shape), norms.dtype)
        whole = lax.dynamic_update_slice_in_dim(whole, norms[None], self.z, 0)
        for k in range(1, 4):
            whole = lax.dynamic_update_slice_in_dim(whole, xor_permute(norms, "shard", k)[None], self.z ^ k, 0)
        return jnp.moveaxis(whole, 0, 1).reshape(norms.shape[0], -1).astype(F32)

    def sum_norms(self, grads):
        share = grads.shape[1] // self.shards
        if not self.staged:
            return lax.dynamic_slice_in_dim(lax.psum(grads, EVERY), self.z * share, share, 1)
        grads = grads + swap_core(grads)
        grads = grads + swap_ctx(grads)
        grads = grads + swap_row(grads)

        def part(z):
            return lax.dynamic_slice_in_dim(grads, z * share, share, 1)

        summed = part(self.z)
        for k in range(1, 4):
            summed = summed + xor_permute(part(self.z ^ k), "shard", k)
        return summed


def beside(*batches):
    return tuple(jnp.concatenate(each, axis=-1) for each in zip(*batches))


def restack(blocks):
    def one(block):
        half = block.shape[-1] // 2
        return jnp.concatenate([block[..., :half], block[..., half:]], axis=-2)

    return tuple(map(one, blocks))


def plus(left, right):
    return (left.astype(F32) + right.astype(F32)).astype(BF16)


def layer_norm(hidden, gain, shift):
    mean = jnp.mean(hidden, axis=-1, keepdims=True)
    centred = hidden - mean
    spread = jnp.mean(centred * centred, axis=-1, keepdims=True)
    return centred * lax.rsqrt(spread + EPS) * gain + shift


def norm_backward(hidden, gain, grad):
    mean = jnp.mean(hidden, axis=-1, keepdims=True)
    centred = hidden - mean
    inverse = lax.rsqrt(jnp.mean(centred * centred, axis=-1, keepdims=True) + EPS)
    unit = centred * inverse
    scaled = grad * gain
    grad_hidden = inverse * (
        scaled - jnp.mean(scaled, axis=-1, keepdims=True) - unit * jnp.mean(scaled * unit, axis=-1, keepdims=True)
    )
    return grad_hidden, jnp.sum(grad * unit, axis=0), jnp.sum(grad, axis=0)


def gelu_parts(pre):
    phi = 0.5 + 0.5 * lax.erf(pre * (0.5 ** 0.5))
    slope = phi + pre * jnp.exp(-0.5 * pre * pre) * ((2.0 * math.pi) ** -0.5)
    return pre * phi, slope


def local(
    frames,
    text_states,
    first_gain,
    first_shift,
    self_query,
    self_key,
    self_value,
    self_output,
    second_gain,
    second_shift,
    cross_query,
    cross_key,
    cross_value,
    cross_output,
    third_gain,
    third_shift,
    up_weight,
    down_weight,
    cotangent,
):
    clips, span, width = frames.shape
    texts = text_states.shape[1]
    rows = clips * span
    place = Place(width)
    position = place.ctx.astype(jnp.int32).reshape(1)
    half = width // 2
    pairs = half // (2 * HD)
    staged = place.staged

    norms = place.gather_norms([first_gain, first_shift, second_gain, second_shift, third_gain, third_shift])
    gain_one, shift_one, gain_two, shift_two, gain_three, shift_three = (norms[i] for i in range(6))
    cotangent_own = cotangent.reshape(rows, width)
    frames_own = frames.reshape(rows, width)
    if staged:
        quarter, short, wide = width // 16, half // 16, width // 8
        inputs = [("columns", self_query, 0, 0), ("columns", self_key, 0, half), ("columns", self_value, 0, width)]
        others = [
            ("rows", self_output, 0, 0),
            ("rows", cross_output, short, 0),
            ("columns", cross_query, 0, width),
            ("columns", cross_key, 0, width + half),
            ("columns", cross_value, 0, 2 * width),
        ]
        hidden = up_weight.shape[1] // 4
        feed = [("feed_columns", up_weight, 0, 0), ("feed_rows", down_weight, 0, hidden)]
        in_piece, other_piece, feed_piece = place.first_pieces(
            [inputs, others, feed],
            [(quarter, width + half), (quarter, 2 * width + half), (wide, hidden + width)],
        )
        in_piece = place.exchange_z(in_piece)
        frames_before = shifted(frames_own, "ctx", 1)
        frames_near = both(frames_own)
        cotangent_far = swap_ctx(cotangent_own)
        in_piece, other_piece, frames_before, frames_near = tied(
            place.foreign(in_piece), other_piece, frames_before, frames_near
        )
        in_piece, other_piece, frames_before = (
            place.exchange_sides(in_piece),
            place.exchange_z(other_piece),
            both(frames_before),
        )
        in_piece, frames_before = tied(place.corners(in_piece), frames_before)
        in_piece = place.exchange_corners(in_piece)
        frames_all = jnp.concatenate([frames_before, frames_near], axis=0)
        normed_one = layer_norm(frames_all.astype(F32), gain_one, shift_one).astype(BF16)
        in_piece, other_piece, feed_piece, normed_one, cotangent_far = tied(
            in_piece, place.foreign(other_piece), feed_piece, normed_one, cotangent_far
        )
        other_piece = place.exchange_sides(other_piece)
        w_feed = lax.all_gather(feed_piece, FEED, axis=0, tiled=True)
        w_query, w_key_value = place.assemble(
            inputs, in_piece, [(0, quarter, 0, half), (0, quarter, half, width)]
        )
    else:
        w_query = place.gather_plain("columns", self_query)
        w_key_value = place.gather_plain("columns", self_key, self_value)
        w_out = place.gather_plain("rows", self_output)
        w_cross_query = place.gather_plain("columns", cross_query)
        w_cross_kv = place.gather_plain("columns", cross_key, cross_value)
        w_cross_out = place.gather_plain("rows", cross_output)
        w_up = place.gather_plain("columns", up_weight)
        w_down = place.gather_plain("rows", down_weight)
        frames_all = jnp.concatenate([both(shifted(frames_own, "ctx", 1)), both(frames_own)], axis=0)
        normed_one = layer_norm(frames_all.astype(F32), gain_one, shift_one).astype(BF16)

    normed_here = normed_one[2 * rows :]
    queries = product(normed_here, w_query).astype(BF16).reshape(2 * clips, span, half)
    key_values = product(normed_one, w_key_value).astype(BF16).reshape(2, 2 * clips, span, width)
    attended, logs = attend(position, queries, key_values, key_values, 0, pairs, True)
    attended = attended.reshape(2 * rows, half)
    if staged:
        other_piece, attended = tied(place.corners(other_piece), attended)
        other_piece = place.exchange_corners(other_piece)
        w_out, w_cross_out, w_cross_query, w_cross_kv = place.assemble(
            others,
            other_piece,
            [(0, short, 0, width), (short, short, 0, width), (0, quarter, width, half), (0, quarter, width + half, width)],
        )
    hidden_zero = frames_own.astype(F32)
    hidden_one = hidden_zero + pair_sum(attended, w_out, product)

    normed_two = both(layer_norm(hidden_one, gain_two, shift_two).astype(BF16))
    text = both(text_states.reshape(clips * texts, width))
    cross_q = product(normed_two, w_cross_query).astype(BF16).reshape(2 * clips, span, half)
    cross_kv = product(text, w_cross_kv).astype(BF16).reshape(1, 2 * clips, texts, width)
    cross_att, cross_logs = attend(position, cross_q, cross_kv, cross_kv, 0, pairs, False)
    cross_att = cross_att.reshape(2 * rows, half)
    hidden_two = hidden_one + pair_sum(cross_att, w_cross_out, product)

    if staged:
        w_feed, hidden_two = tied(w_feed, hidden_two)
        w_up, w_down = w_feed[:, :hidden], w_feed[:, hidden:]
    normed_own = layer_norm(hidden_two, gain_three, shift_three).astype(BF16)
    normed_three = [both(normed_own)]
    grad_branch = [both(cotangent_own)]
    if staged:
        normed_three.append(both(swap_ctx(normed_own)))
        grad_branch.append(both(cotangent_far))
    activated, grad_pre = [], []
    for normed, grad in zip(normed_three, grad_branch):
        act, slope = gelu_parts(product(normed, w_up))
        activated.append(act.astype(BF16))
        grad_pre.append((against(grad, w_down) * slope).astype(BF16))
    if staged:
        far, near = QuadSum(*grad_pre, w_up, against).cores()
        far, activated, normed_three, grad_branch, grad_pre = tied(far, activated, normed_three, grad_branch, grad_pre)
        across = swap_ctx(far)
        feed = place.feed_gradient(activated, grad_branch, 1)
        feed = place.feed_gradient(normed_three, grad_pre, 0, feed)
        feed, near = tied(feed, near)
        feed = lax.psum_scatter(feed.reshape(-1, width), FEED, scatter_dimension=0, tiled=True)
        grad_normed = near + across.astype(F32)
        mixed = QuadSum(*activated, w_down, product)
    else:
        grad_down = over_rows(activated[0], grad_branch[0]).astype(BF16)
        grad_up = over_rows(normed_three[0], grad_pre[0]).astype(BF16)
        grad_normed = pair_sum(grad_pre[0], w_up, against)
    grad_hid, grad_gain_three, grad_shift_three = norm_backward(hidden_two, gain_three, grad_normed)
    grad_res = cotangent_own.astype(F32) + grad_hid

    grad_branch = both(grad_res.astype(BF16))
    grad_cross_out = over_rows(cross_att, grad_branch).astype(BF16)
    grad_catt = against(grad_branch, w_cross_out).astype(BF16).reshape(2 * clips, span, half)
    grad_cq, part_ck, part_cv = attend_back(
        position, cross_q, cross_kv, cross_kv, cross_att.reshape(2 * clips, span, half), grad_catt, cross_logs, 0, pairs, False
    )
    grad_cq = grad_cq.reshape(2 * rows, half)
    part = jnp.concatenate([part_ck, part_cv], axis=-1).reshape(2 * clips, texts, width)
    grad_ckv = (part.astype(F32) + swap_ctx(part).astype(F32)).astype(BF16)
    share = texts // lax.axis_size("ctx")
    start = place.ctx * share

    def part_rows(array):
        array = array.reshape(2 * clips, texts, width)
        return lax.dynamic_slice_in_dim(array, start, share, 1).reshape(2 * clips * share, width)

    grad_cross_kv = over_rows(part_rows(text), part_rows(grad_ckv)).astype(BF16)
    grad_cross_query = over_rows(normed_two, grad_cq).astype(BF16)
    if staged:
        early = beside(
            place.first_sends(grad_cross_query),
            place.first_sends(grad_cross_kv),
            restack(place.first_sends(grad_cross_out)),
        )
        early, grad_cq = tied(early, grad_cq)
        early = place.first_swap(early)
    grad_hid, grad_gain_two, grad_shift_two = norm_backward(
        hidden_one, gain_two, pair_sum(grad_cq, w_cross_query, against)
    )
    grad_res = grad_res + grad_hid

    grad_branch = both(grad_res.astype(BF16))
    grad_out = over_rows(attended, grad_branch).astype(BF16)
    grad_att = against(grad_branch, w_out).astype(BF16).reshape(2 * clips, span, half)
    if staged:
        early, grad_att, mixed.parts = tied(early, grad_att, mixed.parts)
        early = place.second_swap(early)
        mixed_far, mixed_near = mixed.cores()
        mixed = mixed_near + swap_ctx(mixed_far).astype(F32)
    grad_q, grad_k, grad_v = attend_back(
        position,
        queries,
        key_values,
        key_values,
        attended.reshape(2 * clips, span, half),
        grad_att,
        logs,
        0,
        pairs,
        True,
    )
    grad_q = grad_q.reshape(2 * rows, half)
    grad_k = grad_k.reshape(4 * rows, half)
    grad_v = grad_v.reshape(4 * rows, half)
    grad_kv = jnp.concatenate([grad_k, grad_v], axis=1)
    grad_key_value = over_rows(normed_one, grad_kv).astype(BF16)
    grad_query = over_rows(normed_here, grad_q).astype(BF16)
    if staged:
        late = beside(
            place.first_sends(grad_query), place.first_sends(grad_key_value), restack(place.first_sends(grad_out))
        )
        late, grad_q, grad_kv = tied(late, grad_q, grad_kv)
        late = place.first_swap(late)
    grad_normed_before = pair_sum(grad_kv[: 2 * rows], w_key_value, against)
    returned = shifted(grad_normed_before.astype(BF16), "ctx", -1)
    grad_normed = pair_sum(grad_q, w_query, against) + pair_sum(grad_kv[2 * rows :], w_key_value, against)
    if staged:
        early, late, feed, grad_normed = tied(place.second_sum(early), late, feed, grad_normed)
        early, late = place.shard_sum(early), place.second_swap(late)
    grad_text = pair_sum(grad_ckv.reshape(2 * clips * texts, width), w_cross_kv, against).reshape(clips, texts, width)
    mixed = hidden_two + (mixed if staged else pair_sum(activated[0], w_down, product))
    mixed = mixed.astype(BF16).reshape(clips, span, width)
    if staged:
        early, late, mixed, grad_text, feed = tied(early, place.second_sum(late), mixed, grad_text, feed)
        late, early, feed = place.shard_sum(late), place.spread(place.packed(early)), place.spread(feed)
    grad_hid, grad_gain_one, grad_shift_one = norm_backward(
        hidden_zero, gain_one, grad_normed + returned.astype(F32)
    )
    grad_frames = (grad_res + grad_hid).reshape(clips, span, width)

    small = jnp.stack(
        [grad_gain_one, grad_shift_one, grad_gain_two, grad_shift_two, grad_gain_three, grad_shift_three]
    )
    small = place.sum_norms(small)
    if staged:
        own, other = early
        total_cross_query, total_cross_key, total_cross_value = place.finish_columns(own, other, 3)
        total_cross_out = place.finish_rows(own, other)
        late, total_cross_query, total_cross_out = tied(late, total_cross_query, total_cross_out)
        late = place.spread(place.packed(late))
        total_up, total_down = place.finish_up(*feed), place.finish_down(*feed)
        late, total_up, total_down = tied(late, total_up, total_down)
        own, other = late
        total_query, total_key, total_value = place.finish_columns(own, other, 3)
        total_out = place.finish_rows(own, other)
    else:
        total_cross_out, total_out, total_down = map(place.plain_rows, (grad_cross_out, grad_out, grad_down))
        total_cross_key, total_cross_value = place.plain_columns(grad_cross_kv, 2)
        total_key, total_value = place.plain_columns(grad_key_value, 2)
        (total_cross_query,) = place.plain_columns(grad_cross_query, 1)
        (total_query,) = place.plain_columns(grad_query, 1)
        (total_up,) = place.plain_columns(grad_up, 1)
    return (
        mixed,
        grad_frames,
        grad_text,
        small[0],
        small[1],
        total_query,
        total_key,
        total_value,
        total_out,
        small[2],
        small[3],
        total_cross_query,
        total_cross_key,
        total_cross_value,
        total_cross_out,
        small[4],
        small[5],
        total_up,
        total_down,
    )


def solution(mesh):
    ctx, shard, rep = mesh.devices.shape
    mesh = jax.sharding.Mesh(mesh.devices.reshape(ctx, shard, rep // 2, 2), ("ctx", "shard", "y", "core"))
    clips = ("shard", "y", "core")
    rows = P(clips, "ctx", None)
    texts = P(clips, None, None)
    vector = P("shard")
    weight = P("shard", None)
    block = (vector, vector, weight, weight, weight, weight)
    in_specs = (rows, texts, *block, *block, vector, vector, weight, weight, rows)
    out_specs = (rows, rows, texts, *block, *block, vector, vector, weight, weight)
    return jax.shard_map(local, mesh=mesh, in_specs=in_specs, out_specs=out_specs, check_vma=False)
```

```python
import math

import jax
import jax.numpy as jnp
from jax import lax
from jax.experimental import pallas as pl
from jax.experimental.pallas import tpu as pltpu
from jax.sharding import PartitionSpec as P

HD = 64
EPS = 1e-05
NEG = -1e30
BF16 = jnp.bfloat16
F32 = jnp.float32
VMEM_LIMIT = 48 * 1024 * 1024
PLANE = ("ctx", "y")
FEED = ("shard", "y")
EVERY = ("shard", "ctx", "y", "core")


def product(left, right):
    return jnp.dot(left, right, preferred_element_type=F32)


def over_rows(left, right):
    return lax.dot_general(left, right, (((0,), (0,)), ((), ())), preferred_element_type=F32)


def against(left, right):
    return lax.dot_general(left, right, (((1,), (1,)), ((), ())), preferred_element_type=F32)


def xor_permute(array, axis, bit):
    return lax.ppermute(array, axis, [(i, i ^ bit) for i in range(lax.axis_size(axis))])


def swap_ctx(array):
    return xor_permute(array, "ctx", 1)


def swap_row(array):
    return xor_permute(array, "y", 1)


def swap_core(array):
    return xor_permute(array, "core", 1)


def tied(*groups):
    return lax.optimization_barrier(groups)


def shifted(block, axis, distance):
    devices = range(lax.axis_size(axis))
    route = [(i - distance, i) for i in devices if i - distance in devices]
    return lax.ppermute(block, axis, route)


def pick(array, index, axis):
    return lax.dynamic_index_in_dim(array, index, axis, keepdims=False)


def both(own):
    return jnp.concatenate([own, swap_core(own)], axis=0)


def pair_sum(left, right, multiply):
    half = left.shape[0] // 2
    other = swap_core(multiply(left[half:], right).astype(BF16))
    return multiply(left[:half], right) + other.astype(F32)


class QuadSum:
    def __init__(self, near, far, right, multiply):
        half = near.shape[0] // 2
        sent = jnp.concatenate(
            [multiply(far[half:], right).astype(BF16), multiply(near[half:], right).astype(BF16)], axis=0
        )
        self.parts = sent, multiply(far[:half], right), multiply(near[:half], right)

    def cores(self):
        sent, far, near = self.parts
        half = near.shape[0]
        got = swap_core(sent).astype(F32)
        return (far + got[:half]).astype(BF16), near + got[half:]

    def total(self):
        far, near = self.cores()
        return near + swap_ctx(far).astype(F32)


def nt(left, right):
    return lax.dot_general(left, right, (((1,), (1,)), ((), ())), preferred_element_type=F32)


def tn(left, right):
    return lax.dot_general(left, right, (((0,), (0,)), ((), ())), preferred_element_type=F32)


def nn(left, right):
    return lax.dot_general(left, right, (((1,), (0,)), ((), ())), preferred_element_type=F32)


def query_block(span):
    return math.gcd(span, 256)


def key_chunks(causal, block, index):
    if not causal:
        return [(0, None, "none")]
    return [(0, None, "earlier"), (1, (index + 1) * block, "own")]


def masked(scores, mode, position, block, index):
    if mode == "earlier":
        return jnp.where(position > 0, scores, NEG)
    if mode == "own":
        row = lax.broadcasted_iota(jnp.int32, scores.shape, 0)
        column = lax.broadcasted_iota(jnp.int32, scores.shape, 1) + index * block
        return jnp.where(row <= column, scores, NEG)
    return scores


def attend_kernel(causal, position_ref, q_ref, k_ref, v_ref, o_ref, log_ref):
    position = position_ref[0]
    span = q_ref.shape[1]
    block = query_block(span)
    low = lax.broadcasted_iota(jnp.int32, (block, 2 * HD), 1) < HD
    for index in range(span // block):
        rows = pl.ds(index * block, block)
        queries = q_ref[0, rows, :] * BF16(HD ** -0.5)
        parts = []
        for head in range(2):
            side = jnp.where(low == (head == 0), queries, jnp.zeros_like(queries))
            scores = []
            for part, extent, mode in key_chunks(causal, block, index):
                keys = k_ref[part, 0, :extent, :]
                scores.append(masked(nt(keys, side), mode, position, block, index))
            top = scores[0].max(axis=0, keepdims=True)
            for other in scores[1:]:
                top = jnp.maximum(top, other.max(axis=0, keepdims=True))
            weights = [jnp.exp(each - top) for each in scores]
            total = sum(each.sum(axis=0, keepdims=True) for each in weights)
            inverse = 1.0 / total
            out = None
            for weight, (part, extent, mode) in zip(weights, key_chunks(causal, block, index)):
                term = tn(v_ref[part, 0, :extent, :], (weight * inverse).astype(BF16))
                out = term if out is None else out + term
            parts.append(out)
            log_ref[0, 0, head : head + 1, rows] = top + jnp.log(total)
        upper = lax.broadcasted_iota(jnp.int32, parts[0].shape, 0) < HD
        o_ref[0, rows, :] = jnp.where(upper, parts[0], parts[1]).T.astype(BF16)


def attend_back_kernel(
    causal, position_ref, q_ref, k_ref, v_ref, o_ref, g_ref, log_ref, dq_ref, dk_ref, dv_ref, dk_acc, dv_acc
):
    position = position_ref[0]
    span = q_ref.shape[1]
    block = query_block(span)
    low = lax.broadcasted_iota(jnp.int32, (block, 2 * HD), 1) < HD
    dk_acc[...] = jnp.zeros_like(dk_acc)
    dv_acc[...] = jnp.zeros_like(dv_acc)
    for index in range(span // block):
        rows = pl.ds(index * block, block)
        queries = q_ref[0, rows, :] * BF16(HD ** -0.5)
        grads = g_ref[0, rows, :]
        flat = (grads.astype(F32) * o_ref[0, rows, :].astype(F32)).T
        parts = []
        for head in range(2):
            mine = low == (head == 0)
            side = jnp.where(mine, queries, jnp.zeros_like(queries))
            grad = jnp.where(mine, grads, jnp.zeros_like(grads))
            delta = flat[head * HD : (head + 1) * HD].sum(axis=0, keepdims=True)
            log_total = log_ref[0, 0, head : head + 1, rows]
            dq = None
            for part, extent, mode in key_chunks(causal, block, index):
                keys = k_ref[part, 0, :extent, :]
                scores = masked(nt(keys, side), mode, position, block, index)
                probs = jnp.exp(scores - log_total)
                grad_probs = nt(v_ref[part, 0, :extent, :], grad)
                grad_scores = (probs * (grad_probs - delta)).astype(BF16)
                dk_acc[part, :extent, :] += nn(grad_scores, side)
                dv_acc[part, :extent, :] += nn(probs.astype(BF16), grad)
                term = tn(keys, grad_scores)
                dq = term if dq is None else dq + term
            parts.append(dq)
        upper = lax.broadcasted_iota(jnp.int32, parts[0].shape, 0) < HD
        dq_ref[0, rows, :] = (jnp.where(upper, parts[0], parts[1]).T * HD ** -0.5).astype(BF16)
    dk_ref[:, 0] = dk_acc[...].astype(BF16)
    dv_ref[:, 0] = dv_acc[...].astype(BF16)


def attend(position, queries, keys, values, key_base, value_base, causal):
    clips, span, width = queries.shape
    parts, unused, length, unused = keys.shape
    pair = 2 * HD
    pairs = width // pair
    work = 2 * clips * span * length * parts * width
    return pl.pallas_call(
        lambda *refs: attend_kernel(causal, *refs),
        grid=(clips, pairs),
        in_specs=[
            pl.BlockSpec(memory_space=pltpu.SMEM),
            pl.BlockSpec((1, span, pair), lambda b, j: (b, 0, j)),
            pl.BlockSpec((parts, 1, length, pair), lambda b, j: (0, b, 0, key_base + j)),
            pl.BlockSpec((parts, 1, length, pair), lambda b, j: (0, b, 0, value_base + j)),
        ],
        out_specs=[
            pl.BlockSpec((1, span, pair), lambda b, j: (b, 0, j)),
            pl.BlockSpec((1, 1, 2, span), lambda b, j: (b, j, 0, 0)),
        ],
        out_shape=[
            jax.ShapeDtypeStruct((clips, span, width), BF16),
            jax.ShapeDtypeStruct((clips, pairs, 2, span), F32),
        ],
        compiler_params=pltpu.CompilerParams(vmem_limit_bytes=VMEM_LIMIT),
        cost_estimate=pl.CostEstimate(flops=0, bytes_accessed=0, transcendentals=0),
    )(position, queries, keys, values)


def attend_back(position, queries, keys, values, out, grad, logs, key_base, value_base, causal):
    clips, span, width = queries.shape
    parts, unused, length, unused = keys.shape
    pair = 2 * HD
    pairs = width // pair
    work = 2 * clips * span * length * parts * width
    row_spec = pl.BlockSpec((1, span, pair), lambda b, j: (b, 0, j))
    return pl.pallas_call(
        lambda *refs: attend_back_kernel(causal, *refs),
        grid=(clips, pairs),
        in_specs=[
            pl.BlockSpec(memory_space=pltpu.SMEM),
            row_spec,
            pl.BlockSpec((parts, 1, length, pair), lambda b, j: (0, b, 0, key_base + j)),
            pl.BlockSpec((parts, 1, length, pair), lambda b, j: (0, b, 0, value_base + j)),
            row_spec,
            row_spec,
            pl.BlockSpec((1, 1, 2, span), lambda b, j: (b, j, 0, 0)),
        ],
        out_specs=[
            row_spec,
            pl.BlockSpec((parts, 1, length, pair), lambda b, j: (0, b, 0, j)),
            pl.BlockSpec((parts, 1, length, pair), lambda b, j: (0, b, 0, j)),
        ],
        out_shape=[
            jax.ShapeDtypeStruct((clips, span, width), BF16),
            jax.ShapeDtypeStruct((parts, clips, length, width), BF16),
            jax.ShapeDtypeStruct((parts, clips, length, width), BF16),
        ],
        scratch_shapes=[
            pltpu.VMEM((parts, length, pair), F32),
            pltpu.VMEM((parts, length, pair), F32),
        ],
        compiler_params=pltpu.CompilerParams(vmem_limit_bytes=VMEM_LIMIT),
        cost_estimate=pl.CostEstimate(flops=0, bytes_accessed=0, transcendentals=0),
    )(position, queries, keys, values, out, grad, logs)


def strip_parts(block, strips, share, index):
    size = block.shape[-1] // (share * strips)
    return [block[..., (share * j + index) * size : (share * j + index + 1) * size] for j in range(strips)]


KINDS = {"columns": (True, 2, 4), "rows": (False, 2, 4), "feed_columns": (True, 4, 2), "feed_rows": (False, 4, 2)}


class Place:
    def __init__(self, width):
        self.shards = lax.axis_size("shard")
        self.ctx = lax.axis_index("ctx")
        self.z = lax.axis_index("shard")
        self.core = lax.axis_index("core")
        self.y = lax.axis_index("y")
        self.staged = (
            self.shards == 4
            and lax.axis_size("ctx") == 2
            and lax.axis_size("y") == 2
            and (width // self.shards) % (2 * HD) == 0
            and (width // self.shards) % 128 == 0
        )
        self.strips = self.shards if self.staged else 1
        self.quarter = width // 16
        self.spot = jnp.stack(
            [self.z, self.ctx * 2 + self.y, self.y, self.core, self.core * 2 + self.ctx]
        ).astype(jnp.int32)

    def own_columns(self, array):
        rows, width = array.shape
        return lax.dynamic_slice_in_dim(array, self.core * (width // 2), width // 2, 1)

    def own_rows(self, array):
        rows, width = array.shape
        return lax.dynamic_slice_in_dim(array, self.core * (rows // 2), rows // 2, 0)


    def own_spec(self, kind, shard, turn):
        columns, share, pieces = KINDS[kind]
        rows, width = shard.shape
        if columns:
            return pl.BlockSpec((rows // pieces, width), lambda *at: (turn(*at), 0))
        which = 3 if share == 2 else 4
        return pl.BlockSpec(
            (rows // (share * pieces), width), lambda *at: (at[-1][which] * pieces + turn(*at), 0)
        )

    def own_parts(self, batch, blocks, at, store, when=True):
        for (kind, shard, row, column), block in zip(batch, blocks):
            columns, share, pieces = KINDS[kind]
            if not columns:

                @pl.when(when)
                def unused(row=row, column=column, block=block):
                    store(row, column, block[...])

                continue
            for index in range(share):

                @pl.when(when & (at[3 if share == 2 else 4] == index))
                def unused(row=row, column=column, block=block, share=share, index=index):
                    edge = column
                    for part in strip_parts(block, self.strips, share, index):
                        store(row, edge, part)
                        edge += part.shape[-1]

    def first_pieces(self, batches, shapes):
        entries = [entry for batch in batches for entry in batch]

        def here(kind):
            return lambda i, at: at[1 if KINDS[kind][2] == 4 else 2]

        def kernel(at, *refs):
            ins, outs = list(refs[: len(entries)]), refs[len(entries) :]
            for batch, out in zip(batches, outs):

                def store(row, column, part, out=out):
                    out[row : row + part.shape[0], column : column + part.shape[1]] = part

                self.own_parts(batch, [ins.pop(0) for entry in batch], at, store)

        return pl.pallas_call(
            kernel,
            grid_spec=pltpu.PrefetchScalarGridSpec(
                num_scalar_prefetch=1,
                grid=(1,),
                in_specs=[self.own_spec(kind, shard, here(kind)) for kind, shard, row, column in entries],
                out_specs=[pl.BlockSpec(shape, lambda i, at: (0, 0)) for shape in shapes],
            ),
            out_shape=[jax.ShapeDtypeStruct(shape, BF16) for shape in shapes],
            compiler_params=pltpu.CompilerParams(vmem_limit_bytes=VMEM_LIMIT),
        )(self.spot, *[shard for kind, shard, row, column in entries])

    def exchange_z(self, mine):
        return lax.all_gather(mine, "shard", axis=0, tiled=False)

    def foreign(self, gathered):
        return jnp.stack([pick(gathered, self.z ^ k, 0) for k in range(1, 4)])

    def exchange_sides(self, from_z):
        return from_z, swap_row(from_z), swap_ctx(from_z)

    def corners(self, sides):
        from_z, from_y, from_x = sides
        half = from_z.shape[-1] // 2
        return from_z, from_y, from_x, from_x[..., :half], from_y[..., half:]

    def exchange_corners(self, state):
        from_z, from_y, from_x, to_y, to_x = state
        return [from_z], [from_y], [from_x], [swap_row(to_y), swap_ctx(to_x)]

    def assemble(self, batch, turns, outputs):
        pieces = len(turns)
        here = 1 if pieces == 4 else 2
        count = len(batch)
        received = [(turn, array) for turn, arrays in enumerate(turns) for array in arrays]

        def step(turn, array):
            def index(s, k, at):
                now = jnp.maximum(k, 1) - 1
                return (jnp.where(s == turn, now, jnp.where(s < turn, 0, 2)), 0, 0)

            return pl.BlockSpec((1, *array.shape[1:]), index)

        def target(s, k, at):
            return (lax.bitwise_xor(at[0], k) * pieces + lax.bitwise_xor(at[here], s), 0)

        def kernel(at, *refs):
            ins, others, outs = refs[:count], refs[count : count + len(received)], refs[count + len(received) :]
            s, k = pl.program_id(0), pl.program_id(1)

            def store(row, column, part):
                for (first, rows, left, columns), out in zip(outputs, outs):
                    top, bottom = max(first, row), min(first + rows, row + part.shape[0])
                    low, high = max(left, column), min(left + columns, column + part.shape[1])
                    if top < bottom and low < high:
                        out[top - first : bottom - first, low - left : high - left] = part[
                            top - row : bottom - row, low - column : high - column
                        ]

            self.own_parts(batch, ins, at, store, k == 0)
            for turn in range(pieces):

                @pl.when((k > 0) & (s == turn))
                def unused(turn=turn):
                    edge = 0
                    for (which, array), ref in zip(received, others):
                        if which == turn:
                            store(0, edge, ref[0])
                            edge += array.shape[2]

        return pl.pallas_call(
            kernel,
            grid_spec=pltpu.PrefetchScalarGridSpec(
                num_scalar_prefetch=1,
                grid=(pieces, 4),
                in_specs=[
                    self.own_spec(kind, shard, lambda s, k, at: lax.bitwise_xor(at[here], s))
                    for kind, shard, row, column in batch
                ]
                + [step(turn, array) for turn, array in received],
                out_specs=[pl.BlockSpec((rows, columns), target) for first, rows, left, columns in outputs],
            ),
            out_shape=[
                jax.ShapeDtypeStruct((4 * pieces * rows, columns), BF16) for first, rows, left, columns in outputs
            ],
            compiler_params=pltpu.CompilerParams(vmem_limit_bytes=VMEM_LIMIT),
            cost_estimate=pl.CostEstimate(flops=0, bytes_accessed=0, transcendentals=0),
        )(self.spot, *[shard for kind, shard, row, column in batch], *[array for turn, array in received])

    def gather_plain(self, kind, *shards):
        whole = [lax.all_gather(s, "shard", axis=0, tiled=True) for s in shards]
        parts = [self.own_columns(w) if KINDS[kind][0] else self.own_rows(w) for w in whole]
        return jnp.concatenate(parts, axis=1)


    def first_sends(self, grad):
        rows, width = grad.shape[0] // 4, grad.shape[1]
        quarter, half = rows // 4, width // 2
        pieces = grad.reshape(4, 2, 2, quarter, width)
        first, second = pieces[..., :half], pieces[..., half:]
        x, y = self.ctx, self.y
        return pick(first, x, 1), pick(second, y, 2), pick(first, 1 - x, 1), pick(second, 1 - y, 2)

    def first_swap(self, sends):
        keep_a, keep_b, send_a, send_b = sends
        return keep_a, keep_b, swap_ctx(send_a), swap_row(send_b)

    def second_swap(self, state):
        keep_a, keep_b, got_a, got_b = state
        kept_a, kept_b = plus(keep_a, got_a), plus(keep_b, got_b)
        x, y = self.ctx, self.y
        return pick(kept_a, y, 1), pick(kept_b, x, 1), swap_row(pick(kept_a, 1 - y, 1)), swap_ctx(pick(kept_b, 1 - x, 1))

    def second_sum(self, state):
        keep_a, keep_b, got_a, got_b = state
        return jnp.concatenate([plus(keep_a, got_a), plus(keep_b, got_b)], axis=-1)

    def shard_sum(self, kept):
        return lax.psum_scatter(kept, "shard", scatter_dimension=0, tiled=False)

    def packed(self, piece):
        a, b = jnp.split(piece, 2, axis=1)
        block = a.shape[1] // 2
        part, short = block // 2, piece.shape[0] // 2
        rows = [each[:, part + block :] for each in (a, b)]
        return jnp.concatenate(
            [
                jnp.concatenate([a[:, :part], b[:, :part]], axis=1),
                a[:, part : part + block],
                b[:, part : part + block],
                *[jnp.concatenate([each[:short], each[short:]], axis=1) for each in rows],
            ],
            axis=0,
        )


    def spread_sides(self, piece):
        return piece, swap_row(piece), swap_ctx(piece)

    def spread_parts(self, sides):
        piece, from_y, from_x = sides
        half = piece.shape[-1] // 2
        return piece, from_y, from_x, from_x[..., :half], from_y[..., half:]

    def spread_corners(self, parts):
        piece, from_y, from_x, to_y, to_x = parts
        return piece, from_y, from_x, swap_row(to_y), swap_ctx(to_x)

    def spread_cores(self, parts):
        piece, from_y, from_x, left, right = parts
        own = jnp.stack([piece, from_y, from_x, jnp.concatenate([left, right], axis=-1)])
        return own, swap_core(own)

    def feed_gradient(self, lefts, rights, which, joined=None):
        width, columns = lefts[0].shape[1], rights[0].shape[1]
        rows, block = width // 4, columns // 2
        piece = rows // 2
        count = len(lefts)

        def kernel(*refs):
            total = tn(refs[0][...], refs[count][...])
            for i in range(1, count):
                total = total + tn(refs[i][...], refs[count + i][...])
            refs[-1][...] = total.astype(BF16).reshape(refs[-1].shape)

        into = [] if joined is None else [joined]
        return pl.pallas_call(
            kernel,
            grid=(4, 2),
            in_specs=[pl.BlockSpec((each.shape[0], rows), lambda z, j: (0, z)) for each in lefts]
            + [pl.BlockSpec((each.shape[0], block), lambda z, j: (0, j)) for each in rights]
            + [pl.BlockSpec(memory_space=pl.ANY) for each in into],
            out_specs=pl.BlockSpec((1, 2, piece, block), lambda z, j: (z, 0, which, j)),
            out_shape=jax.ShapeDtypeStruct((4, 2, 2 * piece, columns), BF16),
            input_output_aliases={2 * count: 0} if into else {},
            compiler_params=pltpu.CompilerParams(vmem_limit_bytes=VMEM_LIMIT),
        )(*lefts, *rights, *into)

    def finish_up(self, own, other):
        piece, columns = own.shape[1] // 2, own.shape[2]
        size = columns // self.strips

        def spec(x):
            return pl.BlockSpec((1, piece, columns), lambda y, at: (lax.bitwise_xor(2 * x + y, at[1]), 0, 0))

        def kernel(at, *refs):
            out_ref = refs[4]
            for mine in range(2):

                @pl.when(at[3] == mine)
                def unused(mine=mine):
                    for core in range(2):
                        for x in range(2):
                            source = refs[x] if core == mine else refs[2 + x]
                            for j in range(self.strips):
                                edge = (4 * j + 2 * core + x) * size
                                out_ref[:, edge : edge + size] = source[0, :, j * size : (j + 1) * size].astype(F32)

        return pl.pallas_call(
            kernel,
            grid_spec=pltpu.PrefetchScalarGridSpec(
                num_scalar_prefetch=1,
                grid=(2,),
                in_specs=[spec(0), spec(1)] * 2,
                out_specs=pl.BlockSpec((piece, 4 * columns), lambda y, at: (y, 0)),
            ),
            out_shape=jax.ShapeDtypeStruct((2 * piece, 4 * columns), F32),
            compiler_params=pltpu.CompilerParams(vmem_limit_bytes=VMEM_LIMIT),
        )(self.spot, own, own, other, other)

    def finish_down(self, own, other):
        piece, columns = own.shape[1] // 2, own.shape[2]

        def kernel(at, own_ref, other_ref, out_ref):
            mine = pl.program_id(0) == at[3]

            @pl.when(mine)
            def unused():
                out_ref[...] = own_ref[0].astype(F32)

            @pl.when(jnp.logical_not(mine))
            def unused():
                out_ref[...] = other_ref[0].astype(F32)

        return pl.pallas_call(
            kernel,
            grid_spec=pltpu.PrefetchScalarGridSpec(
                num_scalar_prefetch=1,
                grid=(2, 4),
                in_specs=[
                    pl.BlockSpec((1, piece, columns), lambda c, p, at: (lax.bitwise_xor(p, at[1]), 1, 0))
                ] * 2,
                out_specs=pl.BlockSpec((piece, columns), lambda c, p, at: (c * 4 + p, 0)),
            ),
            out_shape=jax.ShapeDtypeStruct((8 * piece, columns), F32),
            compiler_params=pltpu.CompilerParams(vmem_limit_bytes=VMEM_LIMIT),
        )(self.spot, own, other)

    def all_sum(self, array):
        array = lax.psum_scatter(array, "shard", scatter_dimension=0, tiled=True)
        return lax.psum(array, ("ctx", "y", "core"))

    def plain_columns(self, grad, count):
        rows, width = grad.shape
        each = width // count
        outs = []
        for i in range(count):
            whole = jnp.zeros((rows, 2 * each), BF16)
            part = grad[:, i * each : (i + 1) * each]
            whole = lax.dynamic_update_slice_in_dim(whole, part, self.core * each, 1)
            outs.append(self.all_sum(whole).astype(F32))
        return outs

    def plain_rows(self, grad):
        rows, width = grad.shape
        whole = jnp.zeros((2 * rows, width), BF16)
        whole = lax.dynamic_update_slice_in_dim(whole, grad, self.core * rows, 0)
        return self.all_sum(whole).astype(F32)

    def finish_columns(self, own, other, count):
        width = own.shape[2]
        quarter = self.quarter
        size = width // self.strips

        def spec(j):
            return pl.BlockSpec((1, quarter, width), lambda p, at: (lax.bitwise_xor(p, at[1]), j, 0))

        def kernel(at, *refs):
            outs = refs[2 * count :]
            for mine in range(2):

                @pl.when(at[3] == mine)
                def unused(mine=mine):
                    for core in range(2):
                        ins = refs[:count] if core == mine else refs[count : 2 * count]
                        for source, out in zip(ins, outs):
                            for j in range(self.strips):
                                out[:, (2 * j + core) * size : (2 * j + core + 1) * size] = source[
                                    0, :, j * size : (j + 1) * size
                                ].astype(F32)

        return pl.pallas_call(
            kernel,
            grid_spec=pltpu.PrefetchScalarGridSpec(
                num_scalar_prefetch=1,
                grid=(4,),
                in_specs=[spec(j) for j in range(count)] * 2,
                out_specs=[pl.BlockSpec((quarter, 2 * width), lambda p, at: (p, 0))] * count,
            ),
            out_shape=[jax.ShapeDtypeStruct((4 * quarter, 2 * width), F32)] * count,
            compiler_params=pltpu.CompilerParams(vmem_limit_bytes=VMEM_LIMIT),
        )(self.spot, *([own] * count), *([other] * count))

    def finish_rows(self, own, other):
        width = own.shape[2]
        short = self.quarter // 2
        first = 3 * self.quarter // short
        spec = [
            pl.BlockSpec((1, short, width), lambda c, p, at, j=j: (lax.bitwise_xor(p, at[1]), first + j, 0))
            for j in range(2)
        ]

        def kernel(at, *refs):
            out_ref = refs[4]
            mine = pl.program_id(0) == at[3]

            def put(blocks):
                for j, block in enumerate(blocks):
                    out_ref[:, j * width : (j + 1) * width] = block[0].astype(F32)

            @pl.when(mine)
            def unused():
                put(refs[:2])

            @pl.when(jnp.logical_not(mine))
            def unused():
                put(refs[2:4])

        return pl.pallas_call(
            kernel,
            grid_spec=pltpu.PrefetchScalarGridSpec(
                num_scalar_prefetch=1,
                grid=(2, 4),
                in_specs=spec + spec,
                out_specs=pl.BlockSpec((short, 2 * width), lambda c, p, at: (c * 4 + p, 0)),
            ),
            out_shape=jax.ShapeDtypeStruct((8 * short, 2 * width), F32),
            compiler_params=pltpu.CompilerParams(vmem_limit_bytes=VMEM_LIMIT),
        )(self.spot, own, own, other, other)

    def gather_norms(self, shards):
        norms = jnp.stack(shards)
        if not self.staged:
            return lax.all_gather(norms, "shard", axis=1, tiled=True).astype(F32)
        whole = jnp.zeros((4, *norms.shape), norms.dtype)
        whole = lax.dynamic_update_slice_in_dim(whole, norms[None], self.z, 0)
        for k in range(1, 4):
            whole = lax.dynamic_update_slice_in_dim(whole, xor_permute(norms, "shard", k)[None], self.z ^ k, 0)
        return jnp.moveaxis(whole, 0, 1).reshape(norms.shape[0], -1).astype(F32)

    def sum_norms(self, grads):
        share = grads.shape[1] // self.shards
        if not self.staged:
            return lax.dynamic_slice_in_dim(lax.psum(grads, EVERY), self.z * share, share, 1)
        grads = grads + swap_core(grads)
        grads = grads + swap_ctx(grads)
        grads = grads + swap_row(grads)

        def part(z):
            return lax.dynamic_slice_in_dim(grads, z * share, share, 1)

        summed = part(self.z)
        for k in range(1, 4):
            summed = summed + xor_permute(part(self.z ^ k), "shard", k)
        return summed


def beside(*batches):
    return tuple(jnp.concatenate(each, axis=-1) for each in zip(*batches))


def restack(blocks):
    def one(block):
        half = block.shape[-1] // 2
        return jnp.concatenate([block[..., :half], block[..., half:]], axis=-2)

    return tuple(map(one, blocks))


def plus(left, right):
    return (left.astype(F32) + right.astype(F32)).astype(BF16)


def layer_norm(hidden, gain, shift):
    mean = jnp.mean(hidden, axis=-1, keepdims=True)
    centred = hidden - mean
    spread = jnp.mean(centred * centred, axis=-1, keepdims=True)
    return centred * lax.rsqrt(spread + EPS) * gain + shift


def norm_backward(hidden, gain, grad):
    mean = jnp.mean(hidden, axis=-1, keepdims=True)
    centred = hidden - mean
    inverse = lax.rsqrt(jnp.mean(centred * centred, axis=-1, keepdims=True) + EPS)
    unit = centred * inverse
    scaled = grad * gain
    grad_hidden = inverse * (
        scaled - jnp.mean(scaled, axis=-1, keepdims=True) - unit * jnp.mean(scaled * unit, axis=-1, keepdims=True)
    )
    return grad_hidden, jnp.sum(grad * unit, axis=0), jnp.sum(grad, axis=0)


def gelu_parts(pre):
    phi = 0.5 + 0.5 * lax.erf(pre * (0.5 ** 0.5))
    slope = phi + pre * jnp.exp(-0.5 * pre * pre) * ((2.0 * math.pi) ** -0.5)
    return pre * phi, slope


def local(
    frames,
    text_states,
    first_gain,
    first_shift,
    self_query,
    self_key,
    self_value,
    self_output,
    second_gain,
    second_shift,
    cross_query,
    cross_key,
    cross_value,
    cross_output,
    third_gain,
    third_shift,
    up_weight,
    down_weight,
    cotangent,
):
    clips, span, width = frames.shape
    texts = text_states.shape[1]
    rows = clips * span
    place = Place(width)
    position = place.ctx.astype(jnp.int32).reshape(1)
    half = width // 2
    pairs = half // (2 * HD)
    staged = place.staged

    norms = place.gather_norms([first_gain, first_shift, second_gain, second_shift, third_gain, third_shift])
    gain_one, shift_one, gain_two, shift_two, gain_three, shift_three = (norms[i] for i in range(6))
    cotangent_own = cotangent.reshape(rows, width)
    frames_own = frames.reshape(rows, width)
    if staged:
        quarter, short, wide = width // 16, half // 16, width // 8
        inputs = [("columns", self_query, 0, 0), ("columns", self_key, 0, half), ("columns", self_value, 0, width)]
        others = [
            ("rows", self_output, 0, 0),
            ("rows", cross_output, short, 0),
            ("columns", cross_query, 0, width),
            ("columns", cross_key, 0, width + half),
            ("columns", cross_value, 0, 2 * width),
        ]
        hidden = up_weight.shape[1] // 4
        feed = [("feed_columns", up_weight, 0, 0), ("feed_rows", down_weight, 0, hidden)]
        in_piece, other_piece, feed_piece = place.first_pieces(
            [inputs, others, feed],
            [(quarter, width + half), (quarter, 2 * width + half), (wide, hidden + width)],
        )
        in_piece = place.exchange_z(in_piece)
        frames_before = shifted(frames_own, "ctx", 1)
        frames_near = both(frames_own)
        cotangent_far = swap_ctx(cotangent_own)
        in_piece, other_piece, frames_before, frames_near = tied(
            place.foreign(in_piece), other_piece, frames_before, frames_near
        )
        in_piece, other_piece, frames_before = (
            place.exchange_sides(in_piece),
            place.exchange_z(other_piece),
            both(frames_before),
        )
        in_piece, frames_before = tied(place.corners(in_piece), frames_before)
        in_piece = place.exchange_corners(in_piece)
        frames_all = jnp.concatenate([frames_before, frames_near], axis=0)
        normed_one = layer_norm(frames_all.astype(F32), gain_one, shift_one).astype(BF16)
        in_piece, other_piece, feed_piece, normed_one, cotangent_far = tied(
            in_piece, place.foreign(other_piece), feed_piece, normed_one, cotangent_far
        )
        other_piece = place.exchange_sides(other_piece)
        w_feed = lax.all_gather(feed_piece, FEED, axis=0, tiled=True)
        w_query, w_key_value = place.assemble(
            inputs, in_piece, [(0, quarter, 0, half), (0, quarter, half, width)]
        )
    else:
        w_query = place.gather_plain("columns", self_query)
        w_key_value = place.gather_plain("columns", self_key, self_value)
        w_out = place.gather_plain("rows", self_output)
        w_cross_query = place.gather_plain("columns", cross_query)
        w_cross_kv = place.gather_plain("columns", cross_key, cross_value)
        w_cross_out = place.gather_plain("rows", cross_output)
        w_up = place.gather_plain("columns", up_weight)
        w_down = place.gather_plain("rows", down_weight)
        frames_all = jnp.concatenate([both(shifted(frames_own, "ctx", 1)), both(frames_own)], axis=0)
        normed_one = layer_norm(frames_all.astype(F32), gain_one, shift_one).astype(BF16)

    normed_here = normed_one[2 * rows :]
    queries = product(normed_here, w_query).astype(BF16).reshape(2 * clips, span, half)
    key_values = product(normed_one, w_key_value).astype(BF16).reshape(2, 2 * clips, span, width)
    attended, logs = attend(position, queries, key_values, key_values, 0, pairs, True)
    attended = attended.reshape(2 * rows, half)
    if staged:
        other_piece, attended = tied(place.corners(other_piece), attended)
        other_piece = place.exchange_corners(other_piece)
        w_out, w_cross_out, w_cross_query, w_cross_kv = place.assemble(
            others,
            other_piece,
            [(0, short, 0, width), (short, short, 0, width), (0, quarter, width, half), (0, quarter, width + half, width)],
        )
    hidden_zero = frames_own.astype(F32)
    hidden_one = hidden_zero + pair_sum(attended, w_out, product)

    normed_two = both(layer_norm(hidden_one, gain_two, shift_two).astype(BF16))
    text = both(text_states.reshape(clips * texts, width))
    cross_q = product(normed_two, w_cross_query).astype(BF16).reshape(2 * clips, span, half)
    cross_kv = product(text, w_cross_kv).astype(BF16).reshape(1, 2 * clips, texts, width)
    cross_att, cross_logs = attend(position, cross_q, cross_kv, cross_kv, 0, pairs, False)
    cross_att = cross_att.reshape(2 * rows, half)
    hidden_two = hidden_one + pair_sum(cross_att, w_cross_out, product)

    if staged:
        w_feed, hidden_two = tied(w_feed, hidden_two)
        w_up, w_down = w_feed[:, :hidden], w_feed[:, hidden:]
    normed_own = layer_norm(hidden_two, gain_three, shift_three).astype(BF16)
    normed_three, grad_branch, activated, grad_pre = [both(normed_own)], [both(cotangent_own)], [], []

    def feed_rows(normed, grad):
        act, slope = gelu_parts(product(normed, w_up))
        activated.append(act.astype(BF16))
        grad_pre.append((against(grad, w_down) * slope).astype(BF16))

    if staged:
        normed_far = swap_ctx(normed_own)
        grad_branch.append(both(cotangent_far))
        feed_rows(normed_three[0], grad_branch[0])
        normed_far, activated[0], grad_pre[0] = tied(normed_far, activated[0], grad_pre[0])
        normed_three.append(both(normed_far))
        feed_rows(normed_three[1], grad_branch[1])
    else:
        feed_rows(normed_three[0], grad_branch[0])
    if staged:
        far, near = QuadSum(*grad_pre, w_up, against).cores()
        far, activated, normed_three, grad_branch, grad_pre = tied(far, activated, normed_three, grad_branch, grad_pre)
        across = swap_ctx(far)
        feed = place.feed_gradient(activated, grad_branch, 1)
        feed = place.feed_gradient(normed_three, grad_pre, 0, feed)
        feed, near = tied(feed, near)
        feed = lax.psum_scatter(feed.reshape(-1, width), FEED, scatter_dimension=0, tiled=True)
        grad_normed = near + across.astype(F32)
        mixed = QuadSum(*activated, w_down, product)
    else:
        grad_down = over_rows(activated[0], grad_branch[0]).astype(BF16)
        grad_up = over_rows(normed_three[0], grad_pre[0]).astype(BF16)
        grad_normed = pair_sum(grad_pre[0], w_up, against)
    grad_hid, grad_gain_three, grad_shift_three = norm_backward(hidden_two, gain_three, grad_normed)
    grad_res = cotangent_own.astype(F32) + grad_hid

    grad_branch = both(grad_res.astype(BF16))
    grad_cross_out = over_rows(cross_att, grad_branch).astype(BF16)
    grad_catt = against(grad_branch, w_cross_out).astype(BF16).reshape(2 * clips, span, half)
    grad_cq, part_ck, part_cv = attend_back(
        position, cross_q, cross_kv, cross_kv, cross_att.reshape(2 * clips, span, half), grad_catt, cross_logs, 0, pairs, False
    )
    grad_cq = grad_cq.reshape(2 * rows, half)
    part = jnp.concatenate([part_ck, part_cv], axis=-1).reshape(2 * clips, texts, width)
    grad_ckv = (part.astype(F32) + swap_ctx(part).astype(F32)).astype(BF16)
    share = texts // lax.axis_size("ctx")
    start = place.ctx * share

    def part_rows(array):
        array = array.reshape(2 * clips, texts, width)
        return lax.dynamic_slice_in_dim(array, start, share, 1).reshape(2 * clips * share, width)

    grad_cross_kv = over_rows(part_rows(text), part_rows(grad_ckv)).astype(BF16)
    grad_cross_query = over_rows(normed_two, grad_cq).astype(BF16)
    if staged:
        early = beside(
            place.first_sends(grad_cross_query),
            place.first_sends(grad_cross_kv),
            restack(place.first_sends(grad_cross_out)),
        )
        early, grad_cq = tied(early, grad_cq)
        early = place.first_swap(early)
        mixed_far, mixed = mixed.cores()
        mixed = mixed + swap_ctx(mixed_far).astype(F32)
    grad_hid, grad_gain_two, grad_shift_two = norm_backward(
        hidden_one, gain_two, pair_sum(grad_cq, w_cross_query, against)
    )
    grad_res = grad_res + grad_hid

    grad_branch = both(grad_res.astype(BF16))
    grad_out = over_rows(attended, grad_branch).astype(BF16)
    grad_att = against(grad_branch, w_out).astype(BF16).reshape(2 * clips, span, half)
    if staged:
        early, grad_att, mixed, feed = tied(early, grad_att, mixed, feed)
        early, feed = place.second_swap(early), place.spread_sides(feed)
    grad_q, grad_k, grad_v = attend_back(
        position,
        queries,
        key_values,
        key_values,
        attended.reshape(2 * clips, span, half),
        grad_att,
        logs,
        0,
        pairs,
        True,
    )
    grad_q = grad_q.reshape(2 * rows, half)
    grad_k = grad_k.reshape(4 * rows, half)
    grad_v = grad_v.reshape(4 * rows, half)
    grad_kv = jnp.concatenate([grad_k, grad_v], axis=1)
    grad_key_value = over_rows(normed_one, grad_kv).astype(BF16)
    grad_query = over_rows(normed_here, grad_q).astype(BF16)
    if staged:
        late = beside(
            place.first_sends(grad_query), place.first_sends(grad_key_value), restack(place.first_sends(grad_out))
        )
        early, late, feed, grad_q, grad_kv = tied(
            place.second_sum(early), late, place.spread_parts(feed), grad_q, grad_kv
        )
        early, late, feed = place.shard_sum(early), place.first_swap(late), place.spread_corners(feed)
    grad_normed_before = pair_sum(grad_kv[: 2 * rows], w_key_value, against).astype(BF16)
    grad_normed = pair_sum(grad_q, w_query, against) + pair_sum(grad_kv[2 * rows :], w_key_value, against)
    grad_text = pair_sum(grad_ckv.reshape(2 * clips * texts, width), w_cross_kv, against).reshape(clips, texts, width)
    mixed = hidden_two + (mixed if staged else pair_sum(activated[0], w_down, product))
    mixed = mixed.astype(BF16).reshape(clips, span, width)
    if staged:
        late, feed, grad_normed, grad_normed_before, grad_text, mixed = tied(
            late, feed, grad_normed, grad_normed_before, grad_text, mixed
        )
        late, feed = place.second_swap(late), place.spread_cores(feed)
    returned = shifted(grad_normed_before, "ctx", -1)
    if staged:
        early, late = tied(place.packed(early), place.second_sum(late))
        early, late = place.spread_sides(early), place.shard_sum(late)
        total_up, total_down = place.finish_up(*feed), place.finish_down(*feed)
    grad_hid, grad_gain_one, grad_shift_one = norm_backward(
        hidden_zero, gain_one, grad_normed + returned.astype(F32)
    )
    grad_frames = (grad_res + grad_hid).reshape(clips, span, width)

    small = jnp.stack(
        [grad_gain_one, grad_shift_one, grad_gain_two, grad_shift_two, grad_gain_three, grad_shift_three]
    )
    small = place.sum_norms(small)
    if staged:
        early, late, total_up, total_down, grad_frames = tied(
            place.spread_parts(early), place.packed(late), total_up, total_down, grad_frames
        )
        late, early = place.spread_sides(late), place.spread_corners(early)
        late, early = tied(place.spread_parts(late), early)
        late, early = place.spread_corners(late), place.spread_cores(early)
        total_cross_query, total_cross_key, total_cross_value = place.finish_columns(*early, 3)
        total_cross_out = place.finish_rows(*early)
        late, total_cross_query, total_cross_out = tied(late, total_cross_query, total_cross_out)
        late = place.spread_cores(late)
        total_query, total_key, total_value = place.finish_columns(*late, 3)
        total_out = place.finish_rows(*late)
    else:
        total_cross_out, total_out, total_down = map(place.plain_rows, (grad_cross_out, grad_out, grad_down))
        total_cross_key, total_cross_value = place.plain_columns(grad_cross_kv, 2)
        total_key, total_value = place.plain_columns(grad_key_value, 2)
        (total_cross_query,) = place.plain_columns(grad_cross_query, 1)
        (total_query,) = place.plain_columns(grad_query, 1)
        (total_up,) = place.plain_columns(grad_up, 1)
    return (
        mixed,
        grad_frames,
        grad_text,
        small[0],
        small[1],
        total_query,
        total_key,
        total_value,
        total_out,
        small[2],
        small[3],
        total_cross_query,
        total_cross_key,
        total_cross_value,
        total_cross_out,
        small[4],
        small[5],
        total_up,
        total_down,
    )


def solution(mesh):
    ctx, shard, rep = mesh.devices.shape
    mesh = jax.sharding.Mesh(mesh.devices.reshape(ctx, shard, rep // 2, 2), ("ctx", "shard", "y", "core"))
    clips = ("shard", "y", "core")
    rows = P(clips, "ctx", None)
    texts = P(clips, None, None)
    vector = P("shard")
    weight = P("shard", None)
    block = (vector, vector, weight, weight, weight, weight)
    in_specs = (rows, texts, *block, *block, vector, vector, weight, weight, rows)
    out_specs = (rows, rows, texts, *block, *block, vector, vector, weight, weight)
    return jax.shard_map(local, mesh=mesh, in_specs=in_specs, out_specs=out_specs, check_vma=False)
```

```python
import math

import jax
import jax.numpy as jnp
from jax import lax
from jax.experimental import pallas as pl
from jax.experimental.pallas import tpu as pltpu
from jax.sharding import PartitionSpec as P

HD = 64
EPS = 1e-05
NEG = -1e30
BF16 = jnp.bfloat16
F32 = jnp.float32
VMEM_LIMIT = 48 * 1024 * 1024
PLANE = ("ctx", "y")
FEED = ("shard", "y")
EVERY = ("shard", "ctx", "y", "core")


def product(left, right):
    return jnp.dot(left, right, preferred_element_type=F32)


def over_rows(left, right):
    return lax.dot_general(left, right, (((0,), (0,)), ((), ())), preferred_element_type=F32)


def against(left, right):
    return lax.dot_general(left, right, (((1,), (1,)), ((), ())), preferred_element_type=F32)


def xor_permute(array, axis, bit):
    return lax.ppermute(array, axis, [(i, i ^ bit) for i in range(lax.axis_size(axis))])


def swap_ctx(array):
    return xor_permute(array, "ctx", 1)


def swap_row(array):
    return xor_permute(array, "y", 1)


def swap_core(array):
    return xor_permute(array, "core", 1)


def tied(*groups):
    return lax.optimization_barrier(groups)


def shifted(block, axis, distance):
    devices = range(lax.axis_size(axis))
    route = [(i - distance, i) for i in devices if i - distance in devices]
    return lax.ppermute(block, axis, route)


def pick(array, index, axis):
    return lax.dynamic_index_in_dim(array, index, axis, keepdims=False)


def both(own):
    return jnp.concatenate([own, swap_core(own)], axis=0)


def pair_sum(left, right, multiply):
    half = left.shape[0] // 2
    other = swap_core(multiply(left[half:], right).astype(BF16))
    return multiply(left[:half], right) + other.astype(F32)


class QuadSum:
    def __init__(self, near, far, right, multiply):
        half = near.shape[0] // 2
        sent = jnp.concatenate(
            [multiply(far[half:], right).astype(BF16), multiply(near[half:], right).astype(BF16)], axis=0
        )
        self.parts = sent, multiply(far[:half], right), multiply(near[:half], right)

    def cores(self):
        sent, far, near = self.parts
        half = near.shape[0]
        got = swap_core(sent).astype(F32)
        return (far + got[:half]).astype(BF16), near + got[half:]

    def total(self):
        far, near = self.cores()
        return near + swap_ctx(far).astype(F32)


def nt(left, right):
    return lax.dot_general(left, right, (((1,), (1,)), ((), ())), preferred_element_type=F32)


def tn(left, right):
    return lax.dot_general(left, right, (((0,), (0,)), ((), ())), preferred_element_type=F32)


def nn(left, right):
    return lax.dot_general(left, right, (((1,), (0,)), ((), ())), preferred_element_type=F32)


def query_block(span):
    return math.gcd(span, 256)


def key_chunks(causal, block, index):
    if not causal:
        return [(0, None, "none")]
    return [(0, None, "earlier"), (1, (index + 1) * block, "own")]


def masked(scores, mode, position, block, index):
    if mode == "earlier":
        return jnp.where(position > 0, scores, NEG)
    if mode == "own":
        row = lax.broadcasted_iota(jnp.int32, scores.shape, 0)
        column = lax.broadcasted_iota(jnp.int32, scores.shape, 1) + index * block
        return jnp.where(row <= column, scores, NEG)
    return scores


def attend_kernel(causal, position_ref, q_ref, k_ref, v_ref, o_ref, log_ref):
    position = position_ref[0]
    span = q_ref.shape[1]
    block = query_block(span)
    low = lax.broadcasted_iota(jnp.int32, (block, 2 * HD), 1) < HD
    for index in range(span // block):
        rows = pl.ds(index * block, block)
        queries = q_ref[0, rows, :] * BF16(HD ** -0.5)
        parts = []
        for head in range(2):
            side = jnp.where(low == (head == 0), queries, jnp.zeros_like(queries))
            scores = []
            for part, extent, mode in key_chunks(causal, block, index):
                keys = k_ref[part, 0, :extent, :]
                scores.append(masked(nt(keys, side), mode, position, block, index))
            top = scores[0].max(axis=0, keepdims=True)
            for other in scores[1:]:
                top = jnp.maximum(top, other.max(axis=0, keepdims=True))
            weights = [jnp.exp(each - top) for each in scores]
            total = sum(each.sum(axis=0, keepdims=True) for each in weights)
            inverse = 1.0 / total
            out = None
            for weight, (part, extent, mode) in zip(weights, key_chunks(causal, block, index)):
                term = tn(v_ref[part, 0, :extent, :], (weight * inverse).astype(BF16))
                out = term if out is None else out + term
            parts.append(out)
            log_ref[0, 0, head : head + 1, rows] = top + jnp.log(total)
        upper = lax.broadcasted_iota(jnp.int32, parts[0].shape, 0) < HD
        o_ref[0, rows, :] = jnp.where(upper, parts[0], parts[1]).T.astype(BF16)


def attend_back_kernel(
    causal, position_ref, q_ref, k_ref, v_ref, o_ref, g_ref, log_ref, dq_ref, dk_ref, dv_ref, dk_acc, dv_acc
):
    position = position_ref[0]
    span = q_ref.shape[1]
    block = query_block(span)
    low = lax.broadcasted_iota(jnp.int32, (block, 2 * HD), 1) < HD
    dk_acc[...] = jnp.zeros_like(dk_acc)
    dv_acc[...] = jnp.zeros_like(dv_acc)
    for index in range(span // block):
        rows = pl.ds(index * block, block)
        queries = q_ref[0, rows, :] * BF16(HD ** -0.5)
        grads = g_ref[0, rows, :]
        flat = (grads.astype(F32) * o_ref[0, rows, :].astype(F32)).T
        parts = []
        for head in range(2):
            mine = low == (head == 0)
            side = jnp.where(mine, queries, jnp.zeros_like(queries))
            grad = jnp.where(mine, grads, jnp.zeros_like(grads))
            delta = flat[head * HD : (head + 1) * HD].sum(axis=0, keepdims=True)
            log_total = log_ref[0, 0, head : head + 1, rows]
            dq = None
            for part, extent, mode in key_chunks(causal, block, index):
                keys = k_ref[part, 0, :extent, :]
                scores = masked(nt(keys, side), mode, position, block, index)
                probs = jnp.exp(scores - log_total)
                grad_probs = nt(v_ref[part, 0, :extent, :], grad)
                grad_scores = (probs * (grad_probs - delta)).astype(BF16)
                dk_acc[part, :extent, :] += nn(grad_scores, side)
                dv_acc[part, :extent, :] += nn(probs.astype(BF16), grad)
                term = tn(keys, grad_scores)
                dq = term if dq is None else dq + term
            parts.append(dq)
        upper = lax.broadcasted_iota(jnp.int32, parts[0].shape, 0) < HD
        dq_ref[0, rows, :] = (jnp.where(upper, parts[0], parts[1]).T * HD ** -0.5).astype(BF16)
    dk_ref[:, 0] = dk_acc[...].astype(BF16)
    dv_ref[:, 0] = dv_acc[...].astype(BF16)


def attend(position, queries, keys, values, key_base, value_base, causal):
    clips, span, width = queries.shape
    parts, unused, length, unused = keys.shape
    pair = 2 * HD
    pairs = width // pair
    work = 2 * clips * span * length * parts * width
    return pl.pallas_call(
        lambda *refs: attend_kernel(causal, *refs),
        grid=(clips, pairs),
        in_specs=[
            pl.BlockSpec(memory_space=pltpu.SMEM),
            pl.BlockSpec((1, span, pair), lambda b, j: (b, 0, j)),
            pl.BlockSpec((parts, 1, length, pair), lambda b, j: (0, b, 0, key_base + j)),
            pl.BlockSpec((parts, 1, length, pair), lambda b, j: (0, b, 0, value_base + j)),
        ],
        out_specs=[
            pl.BlockSpec((1, span, pair), lambda b, j: (b, 0, j)),
            pl.BlockSpec((1, 1, 2, span), lambda b, j: (b, j, 0, 0)),
        ],
        out_shape=[
            jax.ShapeDtypeStruct((clips, span, width), BF16),
            jax.ShapeDtypeStruct((clips, pairs, 2, span), F32),
        ],
        compiler_params=pltpu.CompilerParams(vmem_limit_bytes=VMEM_LIMIT),
        cost_estimate=pl.CostEstimate(flops=0, bytes_accessed=0, transcendentals=0),
    )(position, queries, keys, values)


def attend_back(position, queries, keys, values, out, grad, logs, key_base, value_base, causal):
    clips, span, width = queries.shape
    parts, unused, length, unused = keys.shape
    pair = 2 * HD
    pairs = width // pair
    work = 2 * clips * span * length * parts * width
    row_spec = pl.BlockSpec((1, span, pair), lambda b, j: (b, 0, j))
    return pl.pallas_call(
        lambda *refs: attend_back_kernel(causal, *refs),
        grid=(clips, pairs),
        in_specs=[
            pl.BlockSpec(memory_space=pltpu.SMEM),
            row_spec,
            pl.BlockSpec((parts, 1, length, pair), lambda b, j: (0, b, 0, key_base + j)),
            pl.BlockSpec((parts, 1, length, pair), lambda b, j: (0, b, 0, value_base + j)),
            row_spec,
            row_spec,
            pl.BlockSpec((1, 1, 2, span), lambda b, j: (b, j, 0, 0)),
        ],
        out_specs=[
            row_spec,
            pl.BlockSpec((parts, 1, length, pair), lambda b, j: (0, b, 0, j)),
            pl.BlockSpec((parts, 1, length, pair), lambda b, j: (0, b, 0, j)),
        ],
        out_shape=[
            jax.ShapeDtypeStruct((clips, span, width), BF16),
            jax.ShapeDtypeStruct((parts, clips, length, width), BF16),
            jax.ShapeDtypeStruct((parts, clips, length, width), BF16),
        ],
        scratch_shapes=[
            pltpu.VMEM((parts, length, pair), F32),
            pltpu.VMEM((parts, length, pair), F32),
        ],
        compiler_params=pltpu.CompilerParams(vmem_limit_bytes=VMEM_LIMIT),
        cost_estimate=pl.CostEstimate(flops=0, bytes_accessed=0, transcendentals=0),
    )(position, queries, keys, values, out, grad, logs)


def strip_parts(block, strips, share, index):
    size = block.shape[-1] // (share * strips)
    return [block[..., (share * j + index) * size : (share * j + index + 1) * size] for j in range(strips)]


KINDS = {"columns": (True, 2, 4), "rows": (False, 2, 4), "feed_columns": (True, 4, 2), "feed_rows": (False, 4, 2)}


class Place:
    def __init__(self, width):
        self.shards = lax.axis_size("shard")
        self.ctx = lax.axis_index("ctx")
        self.z = lax.axis_index("shard")
        self.core = lax.axis_index("core")
        self.y = lax.axis_index("y")
        self.staged = (
            self.shards == 4
            and lax.axis_size("ctx") == 2
            and lax.axis_size("y") == 2
            and (width // self.shards) % (2 * HD) == 0
            and (width // self.shards) % 128 == 0
        )
        self.strips = self.shards if self.staged else 1
        self.quarter = width // 16
        self.spot = jnp.stack(
            [self.z, self.ctx * 2 + self.y, self.y, self.core, self.core * 2 + self.ctx]
        ).astype(jnp.int32)

    def own_columns(self, array):
        rows, width = array.shape
        return lax.dynamic_slice_in_dim(array, self.core * (width // 2), width // 2, 1)

    def own_rows(self, array):
        rows, width = array.shape
        return lax.dynamic_slice_in_dim(array, self.core * (rows // 2), rows // 2, 0)


    def own_spec(self, kind, shard, turn):
        columns, share, pieces = KINDS[kind]
        rows, width = shard.shape
        if columns:
            return pl.BlockSpec((rows // pieces, width), lambda *at: (turn(*at), 0))
        which = 3 if share == 2 else 4
        return pl.BlockSpec(
            (rows // (share * pieces), width), lambda *at: (at[-1][which] * pieces + turn(*at), 0)
        )

    def own_parts(self, batch, blocks, at, store, when=True):
        for (kind, shard, row, column), block in zip(batch, blocks):
            columns, share, pieces = KINDS[kind]
            if not columns:

                @pl.when(when)
                def unused(row=row, column=column, block=block):
                    store(row, column, block[...])

                continue
            for index in range(share):

                @pl.when(when & (at[3 if share == 2 else 4] == index))
                def unused(row=row, column=column, block=block, share=share, index=index):
                    edge = column
                    for part in strip_parts(block, self.strips, share, index):
                        store(row, edge, part)
                        edge += part.shape[-1]

    def first_pieces(self, batches, shapes):
        entries = [entry for batch in batches for entry in batch]

        def here(kind):
            return lambda i, at: at[1 if KINDS[kind][2] == 4 else 2]

        def kernel(at, *refs):
            ins, outs = list(refs[: len(entries)]), refs[len(entries) :]
            for batch, out in zip(batches, outs):

                def store(row, column, part, out=out):
                    out[row : row + part.shape[0], column : column + part.shape[1]] = part

                self.own_parts(batch, [ins.pop(0) for entry in batch], at, store)

        return pl.pallas_call(
            kernel,
            grid_spec=pltpu.PrefetchScalarGridSpec(
                num_scalar_prefetch=1,
                grid=(1,),
                in_specs=[self.own_spec(kind, shard, here(kind)) for kind, shard, row, column in entries],
                out_specs=[pl.BlockSpec(shape, lambda i, at: (0, 0)) for shape in shapes],
            ),
            out_shape=[jax.ShapeDtypeStruct(shape, BF16) for shape in shapes],
            compiler_params=pltpu.CompilerParams(vmem_limit_bytes=VMEM_LIMIT),
        )(self.spot, *[shard for kind, shard, row, column in entries])

    def exchange_z(self, mine):
        return lax.all_gather(mine, "shard", axis=0, tiled=False)

    def foreign(self, gathered):
        return jnp.stack([pick(gathered, self.z ^ k, 0) for k in range(1, 4)])

    def exchange_sides(self, from_z):
        return from_z, swap_row(from_z), swap_ctx(from_z)

    def corners(self, sides):
        from_z, from_y, from_x = sides
        half = from_z.shape[-1] // 2
        return from_z, from_y, from_x, from_x[..., :half], from_y[..., half:]

    def exchange_corners(self, state):
        from_z, from_y, from_x, to_y, to_x = state
        return [from_z], [from_y], [from_x], [swap_row(to_y), swap_ctx(to_x)]

    def assemble(self, batch, turns, outputs):
        pieces = len(turns)
        here = 1 if pieces == 4 else 2
        count = len(batch)
        received = [(turn, array) for turn, arrays in enumerate(turns) for array in arrays]

        def step(turn, array):
            def index(s, k, at):
                now = jnp.maximum(k, 1) - 1
                return (jnp.where(s == turn, now, jnp.where(s < turn, 0, 2)), 0, 0)

            return pl.BlockSpec((1, *array.shape[1:]), index)

        def target(s, k, at):
            return (lax.bitwise_xor(at[0], k) * pieces + lax.bitwise_xor(at[here], s), 0)

        def kernel(at, *refs):
            ins, others, outs = refs[:count], refs[count : count + len(received)], refs[count + len(received) :]
            s, k = pl.program_id(0), pl.program_id(1)

            def store(row, column, part):
                for (first, rows, left, columns), out in zip(outputs, outs):
                    top, bottom = max(first, row), min(first + rows, row + part.shape[0])
                    low, high = max(left, column), min(left + columns, column + part.shape[1])
                    if top < bottom and low < high:
                        out[top - first : bottom - first, low - left : high - left] = part[
                            top - row : bottom - row, low - column : high - column
                        ]

            self.own_parts(batch, ins, at, store, k == 0)
            for turn in range(pieces):

                @pl.when((k > 0) & (s == turn))
                def unused(turn=turn):
                    edge = 0
                    for (which, array), ref in zip(received, others):
                        if which == turn:
                            store(0, edge, ref[0])
                            edge += array.shape[2]

        return pl.pallas_call(
            kernel,
            grid_spec=pltpu.PrefetchScalarGridSpec(
                num_scalar_prefetch=1,
                grid=(pieces, 4),
                in_specs=[
                    self.own_spec(kind, shard, lambda s, k, at: lax.bitwise_xor(at[here], s))
                    for kind, shard, row, column in batch
                ]
                + [step(turn, array) for turn, array in received],
                out_specs=[pl.BlockSpec((rows, columns), target) for first, rows, left, columns in outputs],
            ),
            out_shape=[
                jax.ShapeDtypeStruct((4 * pieces * rows, columns), BF16) for first, rows, left, columns in outputs
            ],
            compiler_params=pltpu.CompilerParams(vmem_limit_bytes=VMEM_LIMIT),
            cost_estimate=pl.CostEstimate(flops=0, bytes_accessed=0, transcendentals=0),
        )(self.spot, *[shard for kind, shard, row, column in batch], *[array for turn, array in received])

    def gather_plain(self, kind, *shards):
        whole = [lax.all_gather(s, "shard", axis=0, tiled=True) for s in shards]
        parts = [self.own_columns(w) if KINDS[kind][0] else self.own_rows(w) for w in whole]
        return jnp.concatenate(parts, axis=1)


    def first_sends(self, grad):
        rows, width = grad.shape[0] // 4, grad.shape[1]
        quarter, half = rows // 4, width // 2
        pieces = grad.reshape(4, 2, 2, quarter, width)
        first, second = pieces[..., :half], pieces[..., half:]
        x, y = self.ctx, self.y
        return pick(first, x, 1), pick(second, y, 2), pick(first, 1 - x, 1), pick(second, 1 - y, 2)

    def first_swap(self, sends):
        keep_a, keep_b, send_a, send_b = sends
        return keep_a, keep_b, swap_ctx(send_a), swap_row(send_b)

    def second_swap(self, state):
        keep_a, keep_b, got_a, got_b = state
        kept_a, kept_b = plus(keep_a, got_a), plus(keep_b, got_b)
        x, y = self.ctx, self.y
        return pick(kept_a, y, 1), pick(kept_b, x, 1), swap_row(pick(kept_a, 1 - y, 1)), swap_ctx(pick(kept_b, 1 - x, 1))

    def second_sum(self, state):
        keep_a, keep_b, got_a, got_b = state
        return jnp.concatenate([plus(keep_a, got_a), plus(keep_b, got_b)], axis=-1)

    def shard_sum(self, kept):
        return lax.psum_scatter(kept, "shard", scatter_dimension=0, tiled=False)

    def packed(self, piece):
        a, b = jnp.split(piece, 2, axis=1)
        block = a.shape[1] // 2
        part, short = block // 2, piece.shape[0] // 2
        rows = [each[:, part + block :] for each in (a, b)]
        return jnp.concatenate(
            [
                jnp.concatenate([a[:, :part], b[:, :part]], axis=1),
                a[:, part : part + block],
                b[:, part : part + block],
                *[jnp.concatenate([each[:short], each[short:]], axis=1) for each in rows],
            ],
            axis=0,
        )


    def spread_sides(self, piece):
        return piece, swap_row(piece), swap_ctx(piece)

    def spread_parts(self, sides):
        piece, from_y, from_x = sides
        half = piece.shape[-1] // 2
        return piece, from_y, from_x, from_x[..., :half], from_y[..., half:]

    def spread_corners(self, parts):
        piece, from_y, from_x, to_y, to_x = parts
        return piece, from_y, from_x, swap_row(to_y), swap_ctx(to_x)

    def spread_cores(self, parts):
        piece, from_y, from_x, left, right = parts
        own = jnp.stack([piece, from_y, from_x, jnp.concatenate([left, right], axis=-1)])
        return own, swap_core(own)

    def feed_gradient(self, lefts, rights, which, joined=None):
        width, columns = lefts[0].shape[1], rights[0].shape[1]
        rows, block = width // 4, columns // 2
        piece = rows // 2
        count = len(lefts)

        def kernel(*refs):
            total = tn(refs[0][...], refs[count][...])
            for i in range(1, count):
                total = total + tn(refs[i][...], refs[count + i][...])
            refs[-1][...] = total.astype(BF16).reshape(refs[-1].shape)

        into = [] if joined is None else [joined]
        return pl.pallas_call(
            kernel,
            grid=(4, 2),
            in_specs=[pl.BlockSpec((each.shape[0], rows), lambda z, j: (0, z)) for each in lefts]
            + [pl.BlockSpec((each.shape[0], block), lambda z, j: (0, j)) for each in rights]
            + [pl.BlockSpec(memory_space=pl.ANY) for each in into],
            out_specs=pl.BlockSpec((1, 2, piece, block), lambda z, j: (z, 0, which, j)),
            out_shape=jax.ShapeDtypeStruct((4, 2, 2 * piece, columns), BF16),
            input_output_aliases={2 * count: 0} if into else {},
            compiler_params=pltpu.CompilerParams(vmem_limit_bytes=VMEM_LIMIT),
        )(*lefts, *rights, *into)

    def finish_up(self, own, other):
        piece, columns = own.shape[1] // 2, own.shape[2]
        size = columns // self.strips

        def spec(x):
            return pl.BlockSpec((1, piece, columns), lambda y, at: (lax.bitwise_xor(2 * x + y, at[1]), 0, 0))

        def kernel(at, *refs):
            out_ref = refs[4]
            for mine in range(2):

                @pl.when(at[3] == mine)
                def unused(mine=mine):
                    for core in range(2):
                        for x in range(2):
                            source = refs[x] if core == mine else refs[2 + x]
                            for j in range(self.strips):
                                edge = (4 * j + 2 * core + x) * size
                                out_ref[:, edge : edge + size] = source[0, :, j * size : (j + 1) * size].astype(F32)

        return pl.pallas_call(
            kernel,
            grid_spec=pltpu.PrefetchScalarGridSpec(
                num_scalar_prefetch=1,
                grid=(2,),
                in_specs=[spec(0), spec(1)] * 2,
                out_specs=pl.BlockSpec((piece, 4 * columns), lambda y, at: (y, 0)),
            ),
            out_shape=jax.ShapeDtypeStruct((2 * piece, 4 * columns), F32),
            cost_estimate=pl.CostEstimate(flops=0, bytes_accessed=6 * own.size, transcendentals=0),
            compiler_params=pltpu.CompilerParams(vmem_limit_bytes=VMEM_LIMIT),
        )(self.spot, own, own, other, other)

    def finish_down(self, own, other):
        piece, columns = own.shape[1] // 2, own.shape[2]

        def kernel(at, own_ref, other_ref, out_ref):
            mine = pl.program_id(0) == at[3]

            @pl.when(mine)
            def unused():
                out_ref[...] = own_ref[0].astype(F32)

            @pl.when(jnp.logical_not(mine))
            def unused():
                out_ref[...] = other_ref[0].astype(F32)

        return pl.pallas_call(
            kernel,
            grid_spec=pltpu.PrefetchScalarGridSpec(
                num_scalar_prefetch=1,
                grid=(2, 4),
                in_specs=[
                    pl.BlockSpec((1, piece, columns), lambda c, p, at: (lax.bitwise_xor(p, at[1]), 1, 0))
                ] * 2,
                out_specs=pl.BlockSpec((piece, columns), lambda c, p, at: (c * 4 + p, 0)),
            ),
            out_shape=jax.ShapeDtypeStruct((8 * piece, columns), F32),
            cost_estimate=pl.CostEstimate(flops=0, bytes_accessed=6 * own.size, transcendentals=0),
            compiler_params=pltpu.CompilerParams(vmem_limit_bytes=VMEM_LIMIT),
        )(self.spot, own, other)

    def all_sum(self, array):
        array = lax.psum_scatter(array, "shard", scatter_dimension=0, tiled=True)
        return lax.psum(array, ("ctx", "y", "core"))

    def plain_columns(self, grad, count):
        rows, width = grad.shape
        each = width // count
        outs = []
        for i in range(count):
            whole = jnp.zeros((rows, 2 * each), BF16)
            part = grad[:, i * each : (i + 1) * each]
            whole = lax.dynamic_update_slice_in_dim(whole, part, self.core * each, 1)
            outs.append(self.all_sum(whole).astype(F32))
        return outs

    def plain_rows(self, grad):
        rows, width = grad.shape
        whole = jnp.zeros((2 * rows, width), BF16)
        whole = lax.dynamic_update_slice_in_dim(whole, grad, self.core * rows, 0)
        return self.all_sum(whole).astype(F32)

    def finish_columns(self, own, other, count):
        width = own.shape[2]
        quarter = self.quarter
        size = width // self.strips

        def spec(j):
            return pl.BlockSpec((1, quarter, width), lambda p, at: (lax.bitwise_xor(p, at[1]), j, 0))

        def kernel(at, *refs):
            outs = refs[2 * count :]
            for mine in range(2):

                @pl.when(at[3] == mine)
                def unused(mine=mine):
                    for core in range(2):
                        ins = refs[:count] if core == mine else refs[count : 2 * count]
                        for source, out in zip(ins, outs):
                            for j in range(self.strips):
                                out[:, (2 * j + core) * size : (2 * j + core + 1) * size] = source[
                                    0, :, j * size : (j + 1) * size
                                ].astype(F32)

        return pl.pallas_call(
            kernel,
            grid_spec=pltpu.PrefetchScalarGridSpec(
                num_scalar_prefetch=1,
                grid=(4,),
                in_specs=[spec(j) for j in range(count)] * 2,
                out_specs=[pl.BlockSpec((quarter, 2 * width), lambda p, at: (p, 0))] * count,
            ),
            out_shape=[jax.ShapeDtypeStruct((4 * quarter, 2 * width), F32)] * count,
            compiler_params=pltpu.CompilerParams(vmem_limit_bytes=VMEM_LIMIT),
        )(self.spot, *([own] * count), *([other] * count))

    def finish_rows(self, own, other):
        width = own.shape[2]
        short = self.quarter // 2
        first = 3 * self.quarter // short
        spec = [
            pl.BlockSpec((1, short, width), lambda c, p, at, j=j: (lax.bitwise_xor(p, at[1]), first + j, 0))
            for j in range(2)
        ]

        def kernel(at, *refs):
            out_ref = refs[4]
            mine = pl.program_id(0) == at[3]

            def put(blocks):
                for j, block in enumerate(blocks):
                    out_ref[:, j * width : (j + 1) * width] = block[0].astype(F32)

            @pl.when(mine)
            def unused():
                put(refs[:2])

            @pl.when(jnp.logical_not(mine))
            def unused():
                put(refs[2:4])

        return pl.pallas_call(
            kernel,
            grid_spec=pltpu.PrefetchScalarGridSpec(
                num_scalar_prefetch=1,
                grid=(2, 4),
                in_specs=spec + spec,
                out_specs=pl.BlockSpec((short, 2 * width), lambda c, p, at: (c * 4 + p, 0)),
            ),
            out_shape=jax.ShapeDtypeStruct((8 * short, 2 * width), F32),
            compiler_params=pltpu.CompilerParams(vmem_limit_bytes=VMEM_LIMIT),
        )(self.spot, own, own, other, other)

    def gather_norms(self, shards):
        norms = jnp.stack(shards)
        if not self.staged:
            return lax.all_gather(norms, "shard", axis=1, tiled=True).astype(F32)
        whole = jnp.zeros((4, *norms.shape), norms.dtype)
        whole = lax.dynamic_update_slice_in_dim(whole, norms[None], self.z, 0)
        for k in range(1, 4):
            whole = lax.dynamic_update_slice_in_dim(whole, xor_permute(norms, "shard", k)[None], self.z ^ k, 0)
        return jnp.moveaxis(whole, 0, 1).reshape(norms.shape[0], -1).astype(F32)

    def sum_norms(self, grads):
        share = grads.shape[1] // self.shards
        if not self.staged:
            return lax.dynamic_slice_in_dim(lax.psum(grads, EVERY), self.z * share, share, 1)
        grads = grads + swap_core(grads)
        grads = grads + swap_ctx(grads)
        grads = grads + swap_row(grads)

        def part(z):
            return lax.dynamic_slice_in_dim(grads, z * share, share, 1)

        summed = part(self.z)
        for k in range(1, 4):
            summed = summed + xor_permute(part(self.z ^ k), "shard", k)
        return summed


def beside(*batches):
    return tuple(jnp.concatenate(each, axis=-1) for each in zip(*batches))


def restack(blocks):
    def one(block):
        half = block.shape[-1] // 2
        return jnp.concatenate([block[..., :half], block[..., half:]], axis=-2)

    return tuple(map(one, blocks))


def plus(left, right):
    return (left.astype(F32) + right.astype(F32)).astype(BF16)


def layer_norm(hidden, gain, shift):
    mean = jnp.mean(hidden, axis=-1, keepdims=True)
    centred = hidden - mean
    spread = jnp.mean(centred * centred, axis=-1, keepdims=True)
    return centred * lax.rsqrt(spread + EPS) * gain + shift


def norm_backward(hidden, gain, grad):
    mean = jnp.mean(hidden, axis=-1, keepdims=True)
    centred = hidden - mean
    inverse = lax.rsqrt(jnp.mean(centred * centred, axis=-1, keepdims=True) + EPS)
    unit = centred * inverse
    scaled = grad * gain
    grad_hidden = inverse * (
        scaled - jnp.mean(scaled, axis=-1, keepdims=True) - unit * jnp.mean(scaled * unit, axis=-1, keepdims=True)
    )
    return grad_hidden, jnp.sum(grad * unit, axis=0), jnp.sum(grad, axis=0)


def gelu_parts(pre):
    phi = 0.5 + 0.5 * lax.erf(pre * (0.5 ** 0.5))
    slope = phi + pre * jnp.exp(-0.5 * pre * pre) * ((2.0 * math.pi) ** -0.5)
    return pre * phi, slope


def local(
    frames,
    text_states,
    first_gain,
    first_shift,
    self_query,
    self_key,
    self_value,
    self_output,
    second_gain,
    second_shift,
    cross_query,
    cross_key,
    cross_value,
    cross_output,
    third_gain,
    third_shift,
    up_weight,
    down_weight,
    cotangent,
):
    clips, span, width = frames.shape
    texts = text_states.shape[1]
    rows = clips * span
    place = Place(width)
    position = place.ctx.astype(jnp.int32).reshape(1)
    half = width // 2
    pairs = half // (2 * HD)
    staged = place.staged

    norms = place.gather_norms([first_gain, first_shift, second_gain, second_shift, third_gain, third_shift])
    gain_one, shift_one, gain_two, shift_two, gain_three, shift_three = (norms[i] for i in range(6))
    cotangent_own = cotangent.reshape(rows, width)
    frames_own = frames.reshape(rows, width)
    if staged:
        quarter, short, wide = width // 16, half // 16, width // 8
        inputs = [("columns", self_query, 0, 0), ("columns", self_key, 0, half), ("columns", self_value, 0, width)]
        others = [
            ("rows", self_output, 0, 0),
            ("rows", cross_output, short, 0),
            ("columns", cross_query, 0, width),
            ("columns", cross_key, 0, width + half),
            ("columns", cross_value, 0, 2 * width),
        ]
        hidden = up_weight.shape[1] // 4
        feed = [("feed_columns", up_weight, 0, 0), ("feed_rows", down_weight, 0, hidden)]
        in_piece, other_piece, feed_piece = place.first_pieces(
            [inputs, others, feed],
            [(quarter, width + half), (quarter, 2 * width + half), (wide, hidden + width)],
        )
        in_piece = place.exchange_z(in_piece)
        frames_before = shifted(frames_own, "ctx", 1)
        frames_near = both(frames_own)
        cotangent_far = swap_ctx(cotangent_own)
        in_piece, other_piece, frames_before, frames_near = tied(
            place.foreign(in_piece), other_piece, frames_before, frames_near
        )
        in_piece, other_piece, frames_before = (
            place.exchange_sides(in_piece),
            place.exchange_z(other_piece),
            both(frames_before),
        )
        in_piece, frames_before = tied(place.corners(in_piece), frames_before)
        in_piece = place.exchange_corners(in_piece)
        frames_all = jnp.concatenate([frames_before, frames_near], axis=0)
        normed_one = layer_norm(frames_all.astype(F32), gain_one, shift_one).astype(BF16)
        in_piece, other_piece, feed_piece, normed_one, cotangent_far = tied(
            in_piece, place.foreign(other_piece), feed_piece, normed_one, cotangent_far
        )
        other_piece = place.exchange_sides(other_piece)
        w_feed = lax.all_gather(feed_piece, FEED, axis=0, tiled=True)
        w_query, w_key_value = place.assemble(
            inputs, in_piece, [(0, quarter, 0, half), (0, quarter, half, width)]
        )
    else:
        w_query = place.gather_plain("columns", self_query)
        w_key_value = place.gather_plain("columns", self_key, self_value)
        w_out = place.gather_plain("rows", self_output)
        w_cross_query = place.gather_plain("columns", cross_query)
        w_cross_kv = place.gather_plain("columns", cross_key, cross_value)
        w_cross_out = place.gather_plain("rows", cross_output)
        w_up = place.gather_plain("columns", up_weight)
        w_down = place.gather_plain("rows", down_weight)
        frames_all = jnp.concatenate([both(shifted(frames_own, "ctx", 1)), both(frames_own)], axis=0)
        normed_one = layer_norm(frames_all.astype(F32), gain_one, shift_one).astype(BF16)

    normed_here = normed_one[2 * rows :]
    queries = product(normed_here, w_query).astype(BF16).reshape(2 * clips, span, half)
    key_values = product(normed_one, w_key_value).astype(BF16).reshape(2, 2 * clips, span, width)
    attended, logs = attend(position, queries, key_values, key_values, 0, pairs, True)
    attended = attended.reshape(2 * rows, half)
    if staged:
        other_piece, attended = tied(place.corners(other_piece), attended)
        other_piece = place.exchange_corners(other_piece)
        w_out, w_cross_out, w_cross_query, w_cross_kv = place.assemble(
            others,
            other_piece,
            [(0, short, 0, width), (short, short, 0, width), (0, quarter, width, half), (0, quarter, width + half, width)],
        )
    hidden_zero = frames_own.astype(F32)
    hidden_one = hidden_zero + pair_sum(attended, w_out, product)

    normed_two = both(layer_norm(hidden_one, gain_two, shift_two).astype(BF16))
    text = both(text_states.reshape(clips * texts, width))
    cross_q = product(normed_two, w_cross_query).astype(BF16).reshape(2 * clips, span, half)
    cross_kv = product(text, w_cross_kv).astype(BF16).reshape(1, 2 * clips, texts, width)
    cross_att, cross_logs = attend(position, cross_q, cross_kv, cross_kv, 0, pairs, False)
    cross_att = cross_att.reshape(2 * rows, half)
    hidden_two = hidden_one + pair_sum(cross_att, w_cross_out, product)

    if staged:
        w_feed, hidden_two = tied(w_feed, hidden_two)
        w_up, w_down = w_feed[:, :hidden], w_feed[:, hidden:]
    normed_own = layer_norm(hidden_two, gain_three, shift_three).astype(BF16)
    normed_three, grad_branch, activated, grad_pre = [both(normed_own)], [both(cotangent_own)], [], []

    def feed_rows(normed, grad):
        act, slope = gelu_parts(product(normed, w_up))
        activated.append(act.astype(BF16))
        grad_pre.append((against(grad, w_down) * slope).astype(BF16))

    if staged:
        normed_far = swap_ctx(normed_own)
        grad_branch.append(both(cotangent_far))
        feed_rows(normed_three[0], grad_branch[0])
        normed_far, activated[0], grad_pre[0] = tied(normed_far, activated[0], grad_pre[0])
        normed_three.append(both(normed_far))
        feed_rows(normed_three[1], grad_branch[1])
    else:
        feed_rows(normed_three[0], grad_branch[0])
    if staged:
        far, near = QuadSum(*grad_pre, w_up, against).cores()
        far, activated, normed_three, grad_branch, grad_pre = tied(far, activated, normed_three, grad_branch, grad_pre)
        across = swap_ctx(far)
        feed = place.feed_gradient(activated, grad_branch, 1)
        feed = place.feed_gradient(normed_three, grad_pre, 0, feed)
        feed, near = tied(feed, near)
        feed = lax.psum_scatter(feed.reshape(-1, width), FEED, scatter_dimension=0, tiled=True)
        grad_normed = near + across.astype(F32)
        mixed = QuadSum(*activated, w_down, product)
    else:
        grad_down = over_rows(activated[0], grad_branch[0]).astype(BF16)
        grad_up = over_rows(normed_three[0], grad_pre[0]).astype(BF16)
        grad_normed = pair_sum(grad_pre[0], w_up, against)
    grad_hid, grad_gain_three, grad_shift_three = norm_backward(hidden_two, gain_three, grad_normed)
    grad_res = cotangent_own.astype(F32) + grad_hid

    grad_branch = both(grad_res.astype(BF16))
    grad_cross_out = over_rows(cross_att, grad_branch).astype(BF16)
    grad_catt = against(grad_branch, w_cross_out).astype(BF16).reshape(2 * clips, span, half)
    grad_cq, part_ck, part_cv = attend_back(
        position, cross_q, cross_kv, cross_kv, cross_att.reshape(2 * clips, span, half), grad_catt, cross_logs, 0, pairs, False
    )
    grad_cq = grad_cq.reshape(2 * rows, half)
    part = jnp.concatenate([part_ck, part_cv], axis=-1).reshape(2 * clips, texts, width)
    grad_ckv = (part.astype(F32) + swap_ctx(part).astype(F32)).astype(BF16)
    share = texts // lax.axis_size("ctx")
    start = place.ctx * share

    def part_rows(array):
        array = array.reshape(2 * clips, texts, width)
        return lax.dynamic_slice_in_dim(array, start, share, 1).reshape(2 * clips * share, width)

    grad_cross_kv = over_rows(part_rows(text), part_rows(grad_ckv)).astype(BF16)
    grad_cross_query = over_rows(normed_two, grad_cq).astype(BF16)
    if staged:
        early = beside(
            place.first_sends(grad_cross_query),
            place.first_sends(grad_cross_kv),
            restack(place.first_sends(grad_cross_out)),
        )
        early, grad_cq = tied(early, grad_cq)
        early = place.first_swap(early)
        mixed_far, mixed = mixed.cores()
        mixed = mixed + swap_ctx(mixed_far).astype(F32)
    grad_hid, grad_gain_two, grad_shift_two = norm_backward(
        hidden_one, gain_two, pair_sum(grad_cq, w_cross_query, against)
    )
    grad_res = grad_res + grad_hid

    grad_branch = both(grad_res.astype(BF16))
    grad_out = over_rows(attended, grad_branch).astype(BF16)
    grad_att = against(grad_branch, w_out).astype(BF16).reshape(2 * clips, span, half)
    if staged:
        early, grad_att, mixed, feed = tied(early, grad_att, mixed, feed)
        early, feed = place.second_swap(early), place.spread_sides(feed)
    grad_q, grad_k, grad_v = attend_back(
        position,
        queries,
        key_values,
        key_values,
        attended.reshape(2 * clips, span, half),
        grad_att,
        logs,
        0,
        pairs,
        True,
    )
    grad_q = grad_q.reshape(2 * rows, half)
    grad_k = grad_k.reshape(4 * rows, half)
    grad_v = grad_v.reshape(4 * rows, half)
    grad_kv = jnp.concatenate([grad_k, grad_v], axis=1)
    grad_key_value = over_rows(normed_one, grad_kv).astype(BF16)
    grad_query = over_rows(normed_here, grad_q).astype(BF16)
    if staged:
        late = beside(
            place.first_sends(grad_query), place.first_sends(grad_key_value), restack(place.first_sends(grad_out))
        )
        early, late, feed, grad_q, grad_kv = tied(
            place.second_sum(early), late, place.spread_parts(feed), grad_q, grad_kv
        )
        early, late, feed = place.shard_sum(early), place.first_swap(late), place.spread_corners(feed)
    grad_normed_before = pair_sum(grad_kv[: 2 * rows], w_key_value, against).astype(BF16)
    grad_normed = pair_sum(grad_q, w_query, against) + pair_sum(grad_kv[2 * rows :], w_key_value, against)
    grad_text = pair_sum(grad_ckv.reshape(2 * clips * texts, width), w_cross_kv, against).reshape(clips, texts, width)
    mixed = hidden_two + (mixed if staged else pair_sum(activated[0], w_down, product))
    mixed = mixed.astype(BF16).reshape(clips, span, width)
    if staged:
        late, feed, grad_normed, grad_normed_before, grad_text, mixed = tied(
            late, feed, grad_normed, grad_normed_before, grad_text, mixed
        )
        late, feed = place.second_swap(late), place.spread_cores(feed)
    returned = shifted(grad_normed_before, "ctx", -1)
    if staged:
        early, late = tied(place.packed(early), place.second_sum(late))
        early, late = place.spread_sides(early), place.shard_sum(late)
        total_up, total_down = place.finish_up(*feed), place.finish_down(*feed)
        returned, total_up, total_down = tied(returned, total_up, total_down)
    grad_hid, grad_gain_one, grad_shift_one = norm_backward(
        hidden_zero, gain_one, grad_normed + returned.astype(F32)
    )
    grad_frames = (grad_res + grad_hid).reshape(clips, span, width)

    small = jnp.stack(
        [grad_gain_one, grad_shift_one, grad_gain_two, grad_shift_two, grad_gain_three, grad_shift_three]
    )
    small = place.sum_norms(small)
    if staged:
        early, late, grad_frames = tied(place.spread_parts(early), place.packed(late), grad_frames)
        late, early = place.spread_sides(late), place.spread_corners(early)
        late, early, small = tied(place.spread_parts(late), early, small)
        late, early = place.spread_corners(late), place.spread_cores(early)
        total_cross_query, total_cross_key, total_cross_value = place.finish_columns(*early, 3)
        total_cross_out = place.finish_rows(*early)
        late, total_cross_query, total_cross_out = tied(late, total_cross_query, total_cross_out)
        late = place.spread_cores(late)
        total_query, total_key, total_value = place.finish_columns(*late, 3)
        total_out = place.finish_rows(*late)
    else:
        total_cross_out, total_out, total_down = map(place.plain_rows, (grad_cross_out, grad_out, grad_down))
        total_cross_key, total_cross_value = place.plain_columns(grad_cross_kv, 2)
        total_key, total_value = place.plain_columns(grad_key_value, 2)
        (total_cross_query,) = place.plain_columns(grad_cross_query, 1)
        (total_query,) = place.plain_columns(grad_query, 1)
        (total_up,) = place.plain_columns(grad_up, 1)
    return (
        mixed,
        grad_frames,
        grad_text,
        small[0],
        small[1],
        total_query,
        total_key,
        total_value,
        total_out,
        small[2],
        small[3],
        total_cross_query,
        total_cross_key,
        total_cross_value,
        total_cross_out,
        small[4],
        small[5],
        total_up,
        total_down,
    )


def solution(mesh):
    ctx, shard, rep = mesh.devices.shape
    mesh = jax.sharding.Mesh(mesh.devices.reshape(ctx, shard, rep // 2, 2), ("ctx", "shard", "y", "core"))
    clips = ("shard", "y", "core")
    rows = P(clips, "ctx", None)
    texts = P(clips, None, None)
    vector = P("shard")
    weight = P("shard", None)
    block = (vector, vector, weight, weight, weight, weight)
    in_specs = (rows, texts, *block, *block, vector, vector, weight, weight, rows)
    out_specs = (rows, rows, texts, *block, *block, vector, vector, weight, weight)
    return jax.shard_map(local, mesh=mesh, in_specs=in_specs, out_specs=out_specs, check_vma=False)
```

```python
import math

import jax
import jax.numpy as jnp
from jax import lax
from jax.experimental import pallas as pl
from jax.experimental.pallas import tpu as pltpu
from jax.sharding import PartitionSpec as P

HD = 64
EPS = 1e-05
NEG = -1e30
BF16 = jnp.bfloat16
F32 = jnp.float32
VMEM_LIMIT = 48 * 1024 * 1024
PLANE = ("ctx", "y")
FEED = ("shard", "y")
EVERY = ("shard", "ctx", "y", "core")


def product(left, right):
    return jnp.dot(left, right, preferred_element_type=F32)


def over_rows(left, right):
    return lax.dot_general(left, right, (((0,), (0,)), ((), ())), preferred_element_type=F32)


def against(left, right):
    return lax.dot_general(left, right, (((1,), (1,)), ((), ())), preferred_element_type=F32)


def xor_permute(array, axis, bit):
    return lax.ppermute(array, axis, [(i, i ^ bit) for i in range(lax.axis_size(axis))])


def swap_ctx(array):
    return xor_permute(array, "ctx", 1)


def swap_row(array):
    return xor_permute(array, "y", 1)


def swap_core(array):
    return xor_permute(array, "core", 1)


def tied(*groups):
    return lax.optimization_barrier(groups)


def shifted(block, axis, distance):
    devices = range(lax.axis_size(axis))
    route = [(i - distance, i) for i in devices if i - distance in devices]
    return lax.ppermute(block, axis, route)


def pick(array, index, axis):
    return lax.dynamic_index_in_dim(array, index, axis, keepdims=False)


def both(own):
    return jnp.concatenate([own, swap_core(own)], axis=0)


def pair_sum(left, right, multiply):
    half = left.shape[0] // 2
    other = swap_core(multiply(left[half:], right).astype(BF16))
    return multiply(left[:half], right) + other.astype(F32)


class QuadSum:
    def __init__(self, near, far, right, multiply):
        half = near.shape[0] // 2
        sent = jnp.concatenate(
            [multiply(far[half:], right).astype(BF16), multiply(near[half:], right).astype(BF16)], axis=0
        )
        self.parts = sent, multiply(far[:half], right), multiply(near[:half], right)

    def cores(self):
        sent, far, near = self.parts
        half = near.shape[0]
        got = swap_core(sent).astype(F32)
        return (far + got[:half]).astype(BF16), near + got[half:]

    def total(self):
        far, near = self.cores()
        return near + swap_ctx(far).astype(F32)


def nt(left, right):
    return lax.dot_general(left, right, (((1,), (1,)), ((), ())), preferred_element_type=F32)


def tn(left, right):
    return lax.dot_general(left, right, (((0,), (0,)), ((), ())), preferred_element_type=F32)


def nn(left, right):
    return lax.dot_general(left, right, (((1,), (0,)), ((), ())), preferred_element_type=F32)


def query_block(span):
    return math.gcd(span, 256)


def key_chunks(causal, block, index):
    if not causal:
        return [(0, None, "none")]
    return [(0, None, "earlier"), (1, (index + 1) * block, "own")]


def masked(scores, mode, position, block, index):
    if mode == "earlier":
        return jnp.where(position > 0, scores, NEG)
    if mode == "own":
        row = lax.broadcasted_iota(jnp.int32, scores.shape, 0)
        column = lax.broadcasted_iota(jnp.int32, scores.shape, 1) + index * block
        return jnp.where(row <= column, scores, NEG)
    return scores


def attend_kernel(causal, position_ref, q_ref, k_ref, v_ref, o_ref, log_ref):
    position = position_ref[0]
    span = q_ref.shape[1]
    block = query_block(span)
    low = lax.broadcasted_iota(jnp.int32, (block, 2 * HD), 1) < HD
    for index in range(span // block):
        rows = pl.ds(index * block, block)
        queries = q_ref[0, rows, :] * BF16(HD ** -0.5)
        parts = []
        for head in range(2):
            side = jnp.where(low == (head == 0), queries, jnp.zeros_like(queries))
            scores = []
            for part, extent, mode in key_chunks(causal, block, index):
                keys = k_ref[part, 0, :extent, :]
                scores.append(masked(nt(keys, side), mode, position, block, index))
            top = scores[0].max(axis=0, keepdims=True)
            for other in scores[1:]:
                top = jnp.maximum(top, other.max(axis=0, keepdims=True))
            weights = [jnp.exp(each - top) for each in scores]
            total = sum(each.sum(axis=0, keepdims=True) for each in weights)
            inverse = 1.0 / total
            out = None
            for weight, (part, extent, mode) in zip(weights, key_chunks(causal, block, index)):
                term = tn(v_ref[part, 0, :extent, :], (weight * inverse).astype(BF16))
                out = term if out is None else out + term
            parts.append(out)
            log_ref[0, 0, head : head + 1, rows] = top + jnp.log(total)
        upper = lax.broadcasted_iota(jnp.int32, parts[0].shape, 0) < HD
        o_ref[0, rows, :] = jnp.where(upper, parts[0], parts[1]).T.astype(BF16)


def attend_back_kernel(
    causal, position_ref, q_ref, k_ref, v_ref, o_ref, g_ref, log_ref, dq_ref, dk_ref, dv_ref, dk_acc, dv_acc
):
    position = position_ref[0]
    span = q_ref.shape[1]
    block = query_block(span)
    low = lax.broadcasted_iota(jnp.int32, (block, 2 * HD), 1) < HD
    dk_acc[...] = jnp.zeros_like(dk_acc)
    dv_acc[...] = jnp.zeros_like(dv_acc)
    for index in range(span // block):
        rows = pl.ds(index * block, block)
        queries = q_ref[0, rows, :] * BF16(HD ** -0.5)
        grads = g_ref[0, rows, :]
        flat = (grads.astype(F32) * o_ref[0, rows, :].astype(F32)).T
        parts = []
        for head in range(2):
            mine = low == (head == 0)
            side = jnp.where(mine, queries, jnp.zeros_like(queries))
            grad = jnp.where(mine, grads, jnp.zeros_like(grads))
            delta = flat[head * HD : (head + 1) * HD].sum(axis=0, keepdims=True)
            log_total = log_ref[0, 0, head : head + 1, rows]
            dq = None
            for part, extent, mode in key_chunks(causal, block, index):
                keys = k_ref[part, 0, :extent, :]
                scores = masked(nt(keys, side), mode, position, block, index)
                probs = jnp.exp(scores - log_total)
                grad_probs = nt(v_ref[part, 0, :extent, :], grad)
                grad_scores = (probs * (grad_probs - delta)).astype(BF16)
                dk_acc[part, :extent, :] += nn(grad_scores, side)
                dv_acc[part, :extent, :] += nn(probs.astype(BF16), grad)
                term = tn(keys, grad_scores)
                dq = term if dq is None else dq + term
            parts.append(dq)
        upper = lax.broadcasted_iota(jnp.int32, parts[0].shape, 0) < HD
        dq_ref[0, rows, :] = (jnp.where(upper, parts[0], parts[1]).T * HD ** -0.5).astype(BF16)
    dk_ref[:, 0] = dk_acc[...].astype(BF16)
    dv_ref[:, 0] = dv_acc[...].astype(BF16)


def attend(position, queries, keys, values, key_base, value_base, causal):
    clips, span, width = queries.shape
    parts, unused, length, unused = keys.shape
    pair = 2 * HD
    pairs = width // pair
    work = 2 * clips * span * length * parts * width
    return pl.pallas_call(
        lambda *refs: attend_kernel(causal, *refs),
        grid=(clips, pairs),
        in_specs=[
            pl.BlockSpec(memory_space=pltpu.SMEM),
            pl.BlockSpec((1, span, pair), lambda b, j: (b, 0, j)),
            pl.BlockSpec((parts, 1, length, pair), lambda b, j: (0, b, 0, key_base + j)),
            pl.BlockSpec((parts, 1, length, pair), lambda b, j: (0, b, 0, value_base + j)),
        ],
        out_specs=[
            pl.BlockSpec((1, span, pair), lambda b, j: (b, 0, j)),
            pl.BlockSpec((1, 1, 2, span), lambda b, j: (b, j, 0, 0)),
        ],
        out_shape=[
            jax.ShapeDtypeStruct((clips, span, width), BF16),
            jax.ShapeDtypeStruct((clips, pairs, 2, span), F32),
        ],
        compiler_params=pltpu.CompilerParams(vmem_limit_bytes=VMEM_LIMIT),
        cost_estimate=pl.CostEstimate(flops=0, bytes_accessed=0, transcendentals=0),
    )(position, queries, keys, values)


def attend_back(position, queries, keys, values, out, grad, logs, key_base, value_base, causal):
    clips, span, width = queries.shape
    parts, unused, length, unused = keys.shape
    pair = 2 * HD
    pairs = width // pair
    work = 2 * clips * span * length * parts * width
    row_spec = pl.BlockSpec((1, span, pair), lambda b, j: (b, 0, j))
    return pl.pallas_call(
        lambda *refs: attend_back_kernel(causal, *refs),
        grid=(clips, pairs),
        in_specs=[
            pl.BlockSpec(memory_space=pltpu.SMEM),
            row_spec,
            pl.BlockSpec((parts, 1, length, pair), lambda b, j: (0, b, 0, key_base + j)),
            pl.BlockSpec((parts, 1, length, pair), lambda b, j: (0, b, 0, value_base + j)),
            row_spec,
            row_spec,
            pl.BlockSpec((1, 1, 2, span), lambda b, j: (b, j, 0, 0)),
        ],
        out_specs=[
            row_spec,
            pl.BlockSpec((parts, 1, length, pair), lambda b, j: (0, b, 0, j)),
            pl.BlockSpec((parts, 1, length, pair), lambda b, j: (0, b, 0, j)),
        ],
        out_shape=[
            jax.ShapeDtypeStruct((clips, span, width), BF16),
            jax.ShapeDtypeStruct((parts, clips, length, width), BF16),
            jax.ShapeDtypeStruct((parts, clips, length, width), BF16),
        ],
        scratch_shapes=[
            pltpu.VMEM((parts, length, pair), F32),
            pltpu.VMEM((parts, length, pair), F32),
        ],
        compiler_params=pltpu.CompilerParams(vmem_limit_bytes=VMEM_LIMIT),
        cost_estimate=pl.CostEstimate(flops=0, bytes_accessed=0, transcendentals=0),
    )(position, queries, keys, values, out, grad, logs)


def strip_parts(block, strips, share, index):
    size = block.shape[-1] // (share * strips)
    return [block[..., (share * j + index) * size : (share * j + index + 1) * size] for j in range(strips)]


KINDS = {"columns": (True, 2, 4), "rows": (False, 2, 4), "feed_columns": (True, 4, 2), "feed_rows": (False, 4, 2)}


class Place:
    def __init__(self, width):
        self.shards = lax.axis_size("shard")
        self.ctx = lax.axis_index("ctx")
        self.z = lax.axis_index("shard")
        self.core = lax.axis_index("core")
        self.y = lax.axis_index("y")
        self.staged = (
            self.shards == 4
            and lax.axis_size("ctx") == 2
            and lax.axis_size("y") == 2
            and (width // self.shards) % (2 * HD) == 0
            and (width // self.shards) % 128 == 0
        )
        self.strips = self.shards if self.staged else 1
        self.quarter = width // 16
        self.spot = jnp.stack(
            [self.z, self.ctx * 2 + self.y, self.y, self.core, self.core * 2 + self.ctx]
        ).astype(jnp.int32)

    def own_columns(self, array):
        rows, width = array.shape
        return lax.dynamic_slice_in_dim(array, self.core * (width // 2), width // 2, 1)

    def own_rows(self, array):
        rows, width = array.shape
        return lax.dynamic_slice_in_dim(array, self.core * (rows // 2), rows // 2, 0)


    def own_spec(self, kind, shard, turn):
        columns, share, pieces = KINDS[kind]
        rows, width = shard.shape
        if columns:
            return pl.BlockSpec((rows // pieces, width), lambda *at: (turn(*at), 0))
        which = 3 if share == 2 else 4
        return pl.BlockSpec(
            (rows // (share * pieces), width), lambda *at: (at[-1][which] * pieces + turn(*at), 0)
        )

    def own_parts(self, batch, blocks, at, store, when=True):
        for (kind, shard, row, column), block in zip(batch, blocks):
            columns, share, pieces = KINDS[kind]
            if not columns:

                @pl.when(when)
                def unused(row=row, column=column, block=block):
                    store(row, column, block[...])

                continue
            for index in range(share):

                @pl.when(when & (at[3 if share == 2 else 4] == index))
                def unused(row=row, column=column, block=block, share=share, index=index):
                    edge = column
                    for part in strip_parts(block, self.strips, share, index):
                        store(row, edge, part)
                        edge += part.shape[-1]

    def first_pieces(self, batches, shapes):
        entries = [entry for batch in batches for entry in batch]

        def here(kind):
            return lambda i, at: at[1 if KINDS[kind][2] == 4 else 2]

        def kernel(at, *refs):
            ins, outs = list(refs[: len(entries)]), refs[len(entries) :]
            for batch, out in zip(batches, outs):

                def store(row, column, part, out=out):
                    out[row : row + part.shape[0], column : column + part.shape[1]] = part

                self.own_parts(batch, [ins.pop(0) for entry in batch], at, store)

        return pl.pallas_call(
            kernel,
            grid_spec=pltpu.PrefetchScalarGridSpec(
                num_scalar_prefetch=1,
                grid=(1,),
                in_specs=[self.own_spec(kind, shard, here(kind)) for kind, shard, row, column in entries],
                out_specs=[pl.BlockSpec(shape, lambda i, at: (0, 0)) for shape in shapes],
            ),
            out_shape=[jax.ShapeDtypeStruct(shape, BF16) for shape in shapes],
            compiler_params=pltpu.CompilerParams(vmem_limit_bytes=VMEM_LIMIT),
        )(self.spot, *[shard for kind, shard, row, column in entries])

    def exchange_z(self, mine):
        return lax.all_gather(mine, "shard", axis=0, tiled=False)

    def foreign(self, gathered):
        return jnp.stack([pick(gathered, self.z ^ k, 0) for k in range(1, 4)])

    def exchange_sides(self, from_z):
        return from_z, swap_row(from_z), swap_ctx(from_z)

    def corners(self, sides):
        from_z, from_y, from_x = sides
        half = from_z.shape[-1] // 2
        return from_z, from_y, from_x, from_x[..., :half], from_y[..., half:]

    def exchange_corners(self, state):
        from_z, from_y, from_x, to_y, to_x = state
        return [from_z], [from_y], [from_x], [swap_row(to_y), swap_ctx(to_x)]

    def assemble(self, batch, turns, outputs):
        pieces = len(turns)
        here = 1 if pieces == 4 else 2
        count = len(batch)
        received = [(turn, array) for turn, arrays in enumerate(turns) for array in arrays]

        def step(turn, array):
            def index(s, k, at):
                now = jnp.maximum(k, 1) - 1
                return (jnp.where(s == turn, now, jnp.where(s < turn, 0, 2)), 0, 0)

            return pl.BlockSpec((1, *array.shape[1:]), index)

        def target(s, k, at):
            return (lax.bitwise_xor(at[0], k) * pieces + lax.bitwise_xor(at[here], s), 0)

        def kernel(at, *refs):
            ins, others, outs = refs[:count], refs[count : count + len(received)], refs[count + len(received) :]
            s, k = pl.program_id(0), pl.program_id(1)

            def store(row, column, part):
                for (first, rows, left, columns), out in zip(outputs, outs):
                    top, bottom = max(first, row), min(first + rows, row + part.shape[0])
                    low, high = max(left, column), min(left + columns, column + part.shape[1])
                    if top < bottom and low < high:
                        out[top - first : bottom - first, low - left : high - left] = part[
                            top - row : bottom - row, low - column : high - column
                        ]

            self.own_parts(batch, ins, at, store, k == 0)
            for turn in range(pieces):

                @pl.when((k > 0) & (s == turn))
                def unused(turn=turn):
                    edge = 0
                    for (which, array), ref in zip(received, others):
                        if which == turn:
                            store(0, edge, ref[0])
                            edge += array.shape[2]

        return pl.pallas_call(
            kernel,
            grid_spec=pltpu.PrefetchScalarGridSpec(
                num_scalar_prefetch=1,
                grid=(pieces, 4),
                in_specs=[
                    self.own_spec(kind, shard, lambda s, k, at: lax.bitwise_xor(at[here], s))
                    for kind, shard, row, column in batch
                ]
                + [step(turn, array) for turn, array in received],
                out_specs=[pl.BlockSpec((rows, columns), target) for first, rows, left, columns in outputs],
            ),
            out_shape=[
                jax.ShapeDtypeStruct((4 * pieces * rows, columns), BF16) for first, rows, left, columns in outputs
            ],
            compiler_params=pltpu.CompilerParams(vmem_limit_bytes=VMEM_LIMIT),
            cost_estimate=pl.CostEstimate(flops=0, bytes_accessed=0, transcendentals=0),
        )(self.spot, *[shard for kind, shard, row, column in batch], *[array for turn, array in received])

    def gather_plain(self, kind, *shards):
        whole = [lax.all_gather(s, "shard", axis=0, tiled=True) for s in shards]
        parts = [self.own_columns(w) if KINDS[kind][0] else self.own_rows(w) for w in whole]
        return jnp.concatenate(parts, axis=1)


    def first_sends(self, grad):
        rows, width = grad.shape[0] // 4, grad.shape[1]
        quarter, half = rows // 4, width // 2
        pieces = grad.reshape(4, 2, 2, quarter, width)
        first, second = pieces[..., :half], pieces[..., half:]
        x, y = self.ctx, self.y
        return pick(first, x, 1), pick(second, y, 2), pick(first, 1 - x, 1), pick(second, 1 - y, 2)

    def first_swap(self, sends):
        keep_a, keep_b, send_a, send_b = sends
        return keep_a, keep_b, swap_ctx(send_a), swap_row(send_b)

    def second_swap(self, state):
        keep_a, keep_b, got_a, got_b = state
        kept_a, kept_b = plus(keep_a, got_a), plus(keep_b, got_b)
        x, y = self.ctx, self.y
        return pick(kept_a, y, 1), pick(kept_b, x, 1), swap_row(pick(kept_a, 1 - y, 1)), swap_ctx(pick(kept_b, 1 - x, 1))

    def second_sum(self, state):
        keep_a, keep_b, got_a, got_b = state
        return jnp.concatenate([plus(keep_a, got_a), plus(keep_b, got_b)], axis=-1)

    def shard_sum(self, kept):
        return lax.psum_scatter(kept, "shard", scatter_dimension=0, tiled=False)

    def packed(self, piece):
        a, b = jnp.split(piece, 2, axis=1)
        block = a.shape[1] // 2
        part, short = block // 2, piece.shape[0] // 2
        rows = [each[:, part + block :] for each in (a, b)]
        return jnp.concatenate(
            [
                jnp.concatenate([a[:, :part], b[:, :part]], axis=1),
                a[:, part : part + block],
                b[:, part : part + block],
                *[jnp.concatenate([each[:short], each[short:]], axis=1) for each in rows],
            ],
            axis=0,
        )


    def spread_sides(self, piece):
        return piece, swap_row(piece), swap_ctx(piece)

    def spread_parts(self, sides):
        piece, from_y, from_x = sides
        half = piece.shape[-1] // 2
        return piece, from_y, from_x, from_x[..., :half], from_y[..., half:]

    def spread_corners(self, parts):
        piece, from_y, from_x, to_y, to_x = parts
        return piece, from_y, from_x, swap_row(to_y), swap_ctx(to_x)

    def spread_cores(self, parts):
        piece, from_y, from_x, left, right = parts
        own = jnp.stack([piece, from_y, from_x, jnp.concatenate([left, right], axis=-1)])
        return own, swap_core(own)

    def feed_gradient(self, lefts, rights, which, joined=None):
        width, columns = lefts[0].shape[1], rights[0].shape[1]
        rows, block = width // 4, columns // 2
        piece = rows // 2
        count = len(lefts)

        def kernel(*refs):
            total = tn(refs[0][...], refs[count][...])
            for i in range(1, count):
                total = total + tn(refs[i][...], refs[count + i][...])
            refs[-1][...] = total.astype(BF16).reshape(refs[-1].shape)

        into = [] if joined is None else [joined]
        return pl.pallas_call(
            kernel,
            grid=(4, 2),
            in_specs=[pl.BlockSpec((each.shape[0], rows), lambda z, j: (0, z)) for each in lefts]
            + [pl.BlockSpec((each.shape[0], block), lambda z, j: (0, j)) for each in rights]
            + [pl.BlockSpec(memory_space=pl.ANY) for each in into],
            out_specs=pl.BlockSpec((1, 2, piece, block), lambda z, j: (z, 0, which, j)),
            out_shape=jax.ShapeDtypeStruct((4, 2, 2 * piece, columns), BF16),
            input_output_aliases={2 * count: 0} if into else {},
            compiler_params=pltpu.CompilerParams(vmem_limit_bytes=VMEM_LIMIT),
        )(*lefts, *rights, *into)

    def finish_up(self, own, other):
        piece, columns = own.shape[1] // 2, own.shape[2]
        size = columns // self.strips

        def spec(x):
            return pl.BlockSpec((1, piece, columns), lambda y, at: (lax.bitwise_xor(2 * x + y, at[1]), 0, 0))

        def kernel(at, *refs):
            out_ref = refs[4]
            for mine in range(2):

                @pl.when(at[3] == mine)
                def unused(mine=mine):
                    for core in range(2):
                        for x in range(2):
                            source = refs[x] if core == mine else refs[2 + x]
                            for j in range(self.strips):
                                edge = (4 * j + 2 * core + x) * size
                                out_ref[:, edge : edge + size] = source[0, :, j * size : (j + 1) * size].astype(F32)

        return pl.pallas_call(
            kernel,
            grid_spec=pltpu.PrefetchScalarGridSpec(
                num_scalar_prefetch=1,
                grid=(2,),
                in_specs=[spec(0), spec(1)] * 2,
                out_specs=pl.BlockSpec((piece, 4 * columns), lambda y, at: (y, 0)),
            ),
            out_shape=jax.ShapeDtypeStruct((2 * piece, 4 * columns), F32),
            compiler_params=pltpu.CompilerParams(vmem_limit_bytes=VMEM_LIMIT),
        )(self.spot, own, own, other, other)

    def finish_down(self, own, other):
        piece, columns = own.shape[1] // 2, own.shape[2]

        def kernel(at, own_ref, other_ref, out_ref):
            mine = pl.program_id(0) == at[3]

            @pl.when(mine)
            def unused():
                out_ref[...] = own_ref[0].astype(F32)

            @pl.when(jnp.logical_not(mine))
            def unused():
                out_ref[...] = other_ref[0].astype(F32)

        return pl.pallas_call(
            kernel,
            grid_spec=pltpu.PrefetchScalarGridSpec(
                num_scalar_prefetch=1,
                grid=(2, 4),
                in_specs=[
                    pl.BlockSpec((1, piece, columns), lambda c, p, at: (lax.bitwise_xor(p, at[1]), 1, 0))
                ] * 2,
                out_specs=pl.BlockSpec((piece, columns), lambda c, p, at: (c * 4 + p, 0)),
            ),
            out_shape=jax.ShapeDtypeStruct((8 * piece, columns), F32),
            compiler_params=pltpu.CompilerParams(vmem_limit_bytes=VMEM_LIMIT),
        )(self.spot, own, other)

    def all_sum(self, array):
        array = lax.psum_scatter(array, "shard", scatter_dimension=0, tiled=True)
        return lax.psum(array, ("ctx", "y", "core"))

    def plain_columns(self, grad, count):
        rows, width = grad.shape
        each = width // count
        outs = []
        for i in range(count):
            whole = jnp.zeros((rows, 2 * each), BF16)
            part = grad[:, i * each : (i + 1) * each]
            whole = lax.dynamic_update_slice_in_dim(whole, part, self.core * each, 1)
            outs.append(self.all_sum(whole).astype(F32))
        return outs

    def plain_rows(self, grad):
        rows, width = grad.shape
        whole = jnp.zeros((2 * rows, width), BF16)
        whole = lax.dynamic_update_slice_in_dim(whole, grad, self.core * rows, 0)
        return self.all_sum(whole).astype(F32)

    def finish_columns(self, own, other, count):
        width = own.shape[2]
        quarter = self.quarter
        size = width // self.strips

        def spec(j):
            return pl.BlockSpec((1, quarter, width), lambda p, at: (lax.bitwise_xor(p, at[1]), j, 0))

        def kernel(at, *refs):
            outs = refs[2 * count :]
            for mine in range(2):

                @pl.when(at[3] == mine)
                def unused(mine=mine):
                    for core in range(2):
                        ins = refs[:count] if core == mine else refs[count : 2 * count]
                        for source, out in zip(ins, outs):
                            for j in range(self.strips):
                                out[:, (2 * j + core) * size : (2 * j + core + 1) * size] = source[
                                    0, :, j * size : (j + 1) * size
                                ].astype(F32)

        return pl.pallas_call(
            kernel,
            grid_spec=pltpu.PrefetchScalarGridSpec(
                num_scalar_prefetch=1,
                grid=(4,),
                in_specs=[spec(j) for j in range(count)] * 2,
                out_specs=[pl.BlockSpec((quarter, 2 * width), lambda p, at: (p, 0))] * count,
            ),
            out_shape=[jax.ShapeDtypeStruct((4 * quarter, 2 * width), F32)] * count,
            compiler_params=pltpu.CompilerParams(vmem_limit_bytes=VMEM_LIMIT),
        )(self.spot, *([own] * count), *([other] * count))

    def finish_rows(self, own, other):
        width = own.shape[2]
        short = self.quarter // 2
        first = 3 * self.quarter // short
        spec = [
            pl.BlockSpec((1, short, width), lambda c, p, at, j=j: (lax.bitwise_xor(p, at[1]), first + j, 0))
            for j in range(2)
        ]

        def kernel(at, *refs):
            out_ref = refs[4]
            mine = pl.program_id(0) == at[3]

            def put(blocks):
                for j, block in enumerate(blocks):
                    out_ref[:, j * width : (j + 1) * width] = block[0].astype(F32)

            @pl.when(mine)
            def unused():
                put(refs[:2])

            @pl.when(jnp.logical_not(mine))
            def unused():
                put(refs[2:4])

        return pl.pallas_call(
            kernel,
            grid_spec=pltpu.PrefetchScalarGridSpec(
                num_scalar_prefetch=1,
                grid=(2, 4),
                in_specs=spec + spec,
                out_specs=pl.BlockSpec((short, 2 * width), lambda c, p, at: (c * 4 + p, 0)),
            ),
            out_shape=jax.ShapeDtypeStruct((8 * short, 2 * width), F32),
            compiler_params=pltpu.CompilerParams(vmem_limit_bytes=VMEM_LIMIT),
        )(self.spot, own, own, other, other)

    def gather_norms(self, shards):
        norms = jnp.stack(shards)
        if not self.staged:
            return lax.all_gather(norms, "shard", axis=1, tiled=True).astype(F32)
        whole = jnp.zeros((4, *norms.shape), norms.dtype)
        whole = lax.dynamic_update_slice_in_dim(whole, norms[None], self.z, 0)
        for k in range(1, 4):
            whole = lax.dynamic_update_slice_in_dim(whole, xor_permute(norms, "shard", k)[None], self.z ^ k, 0)
        return jnp.moveaxis(whole, 0, 1).reshape(norms.shape[0], -1).astype(F32)

    def sum_norms(self, grads):
        share = grads.shape[1] // self.shards
        if not self.staged:
            return lax.dynamic_slice_in_dim(lax.psum(grads, EVERY), self.z * share, share, 1)
        grads = grads + swap_core(grads)
        grads = grads + swap_ctx(grads)
        grads = grads + swap_row(grads)

        def part(z):
            return lax.dynamic_slice_in_dim(grads, z * share, share, 1)

        summed = part(self.z)
        for k in range(1, 4):
            summed = summed + xor_permute(part(self.z ^ k), "shard", k)
        return summed


def beside(*batches):
    return tuple(jnp.concatenate(each, axis=-1) for each in zip(*batches))


def restack(blocks):
    def one(block):
        half = block.shape[-1] // 2
        return jnp.concatenate([block[..., :half], block[..., half:]], axis=-2)

    return tuple(map(one, blocks))


def plus(left, right):
    return (left.astype(F32) + right.astype(F32)).astype(BF16)


def layer_norm(hidden, gain, shift):
    mean = jnp.mean(hidden, axis=-1, keepdims=True)
    centred = hidden - mean
    spread = jnp.mean(centred * centred, axis=-1, keepdims=True)
    return centred * lax.rsqrt(spread + EPS) * gain + shift


def norm_backward(hidden, gain, grad):
    mean = jnp.mean(hidden, axis=-1, keepdims=True)
    centred = hidden - mean
    inverse = lax.rsqrt(jnp.mean(centred * centred, axis=-1, keepdims=True) + EPS)
    unit = centred * inverse
    scaled = grad * gain
    grad_hidden = inverse * (
        scaled - jnp.mean(scaled, axis=-1, keepdims=True) - unit * jnp.mean(scaled * unit, axis=-1, keepdims=True)
    )
    return grad_hidden, jnp.sum(grad * unit, axis=0), jnp.sum(grad, axis=0)


def gelu_parts(pre):
    phi = 0.5 + 0.5 * lax.erf(pre * (0.5 ** 0.5))
    slope = phi + pre * jnp.exp(-0.5 * pre * pre) * ((2.0 * math.pi) ** -0.5)
    return pre * phi, slope


def local(
    frames,
    text_states,
    first_gain,
    first_shift,
    self_query,
    self_key,
    self_value,
    self_output,
    second_gain,
    second_shift,
    cross_query,
    cross_key,
    cross_value,
    cross_output,
    third_gain,
    third_shift,
    up_weight,
    down_weight,
    cotangent,
):
    clips, span, width = frames.shape
    texts = text_states.shape[1]
    rows = clips * span
    place = Place(width)
    position = place.ctx.astype(jnp.int32).reshape(1)
    half = width // 2
    pairs = half // (2 * HD)
    staged = place.staged

    norms = place.gather_norms([first_gain, first_shift, second_gain, second_shift, third_gain, third_shift])
    gain_one, shift_one, gain_two, shift_two, gain_three, shift_three = (norms[i] for i in range(6))
    cotangent_own = cotangent.reshape(rows, width)
    frames_own = frames.reshape(rows, width)
    if staged:
        quarter, short, wide = width // 16, half // 16, width // 8
        inputs = [("columns", self_query, 0, 0), ("columns", self_key, 0, half), ("columns", self_value, 0, width)]
        others = [
            ("rows", self_output, 0, 0),
            ("rows", cross_output, short, 0),
            ("columns", cross_query, 0, width),
            ("columns", cross_key, 0, width + half),
            ("columns", cross_value, 0, 2 * width),
        ]
        hidden = up_weight.shape[1] // 4
        feed = [("feed_columns", up_weight, 0, 0), ("feed_rows", down_weight, 0, hidden)]
        in_piece, other_piece, feed_piece = place.first_pieces(
            [inputs, others, feed],
            [(quarter, width + half), (quarter, 2 * width + half), (wide, hidden + width)],
        )
        in_piece = place.exchange_z(in_piece)
        frames_before = shifted(frames_own, "ctx", 1)
        frames_near = both(frames_own)
        cotangent_far = swap_ctx(cotangent_own)
        in_piece, other_piece, frames_before, frames_near = tied(
            place.foreign(in_piece), other_piece, frames_before, frames_near
        )
        in_piece, other_piece, frames_before = (
            place.exchange_sides(in_piece),
            place.exchange_z(other_piece),
            both(frames_before),
        )
        in_piece, frames_before = tied(place.corners(in_piece), frames_before)
        in_piece = place.exchange_corners(in_piece)
        frames_all = jnp.concatenate([frames_before, frames_near], axis=0)
        normed_one = layer_norm(frames_all.astype(F32), gain_one, shift_one).astype(BF16)
        in_piece, other_piece, feed_piece, normed_one, cotangent_far = tied(
            in_piece, place.foreign(other_piece), feed_piece, normed_one, cotangent_far
        )
        other_piece = place.exchange_sides(other_piece)
        w_feed = lax.all_gather(feed_piece, FEED, axis=0, tiled=True)
        w_query, w_key_value = place.assemble(
            inputs, in_piece, [(0, quarter, 0, half), (0, quarter, half, width)]
        )
    else:
        w_query = place.gather_plain("columns", self_query)
        w_key_value = place.gather_plain("columns", self_key, self_value)
        w_out = place.gather_plain("rows", self_output)
        w_cross_query = place.gather_plain("columns", cross_query)
        w_cross_kv = place.gather_plain("columns", cross_key, cross_value)
        w_cross_out = place.gather_plain("rows", cross_output)
        w_up = place.gather_plain("columns", up_weight)
        w_down = place.gather_plain("rows", down_weight)
        frames_all = jnp.concatenate([both(shifted(frames_own, "ctx", 1)), both(frames_own)], axis=0)
        normed_one = layer_norm(frames_all.astype(F32), gain_one, shift_one).astype(BF16)

    normed_here = normed_one[2 * rows :]
    queries = product(normed_here, w_query).astype(BF16).reshape(2 * clips, span, half)
    key_values = product(normed_one, w_key_value).astype(BF16).reshape(2, 2 * clips, span, width)
    attended, logs = attend(position, queries, key_values, key_values, 0, pairs, True)
    attended = attended.reshape(2 * rows, half)
    if staged:
        other_piece, attended = tied(place.corners(other_piece), attended)
        other_piece = place.exchange_corners(other_piece)
        w_out, w_cross_out, w_cross_query, w_cross_kv = place.assemble(
            others,
            other_piece,
            [(0, short, 0, width), (short, short, 0, width), (0, quarter, width, half), (0, quarter, width + half, width)],
        )
    hidden_zero = frames_own.astype(F32)
    hidden_one = hidden_zero + pair_sum(attended, w_out, product)

    normed_two = both(layer_norm(hidden_one, gain_two, shift_two).astype(BF16))
    text = both(text_states.reshape(clips * texts, width))
    cross_q = product(normed_two, w_cross_query).astype(BF16).reshape(2 * clips, span, half)
    cross_kv = product(text, w_cross_kv).astype(BF16).reshape(1, 2 * clips, texts, width)
    cross_att, cross_logs = attend(position, cross_q, cross_kv, cross_kv, 0, pairs, False)
    cross_att = cross_att.reshape(2 * rows, half)
    hidden_two = hidden_one + pair_sum(cross_att, w_cross_out, product)

    if staged:
        w_feed, hidden_two = tied(w_feed, hidden_two)
        w_up, w_down = w_feed[:, :hidden], w_feed[:, hidden:]
    normed_own = layer_norm(hidden_two, gain_three, shift_three).astype(BF16)
    normed_three, grad_branch, activated, grad_pre = [both(normed_own)], [both(cotangent_own)], [], []

    def feed_rows(normed, grad):
        act, slope = gelu_parts(product(normed, w_up))
        activated.append(act.astype(BF16))
        grad_pre.append((against(grad, w_down) * slope).astype(BF16))

    if staged:
        normed_far = swap_ctx(normed_own)
        grad_branch.append(both(cotangent_far))
        feed_rows(normed_three[0], grad_branch[0])
        normed_far, activated[0], grad_pre[0] = tied(normed_far, activated[0], grad_pre[0])
        normed_three.append(both(normed_far))
        feed_rows(normed_three[1], grad_branch[1])
    else:
        feed_rows(normed_three[0], grad_branch[0])
    if staged:
        far, near = QuadSum(*grad_pre, w_up, against).cores()
        far, activated, normed_three, grad_branch, grad_pre = tied(far, activated, normed_three, grad_branch, grad_pre)
        across = swap_ctx(far)
        feed = place.feed_gradient(activated, grad_branch, 1)
        feed = place.feed_gradient(normed_three, grad_pre, 0, feed)
        feed, near = tied(feed, near)
        feed = lax.psum_scatter(feed.reshape(-1, width), FEED, scatter_dimension=0, tiled=True)
        grad_normed = near + across.astype(F32)
        mixed = QuadSum(*activated, w_down, product)
    else:
        grad_down = over_rows(activated[0], grad_branch[0]).astype(BF16)
        grad_up = over_rows(normed_three[0], grad_pre[0]).astype(BF16)
        grad_normed = pair_sum(grad_pre[0], w_up, against)
    grad_hid, grad_gain_three, grad_shift_three = norm_backward(hidden_two, gain_three, grad_normed)
    grad_res = cotangent_own.astype(F32) + grad_hid

    grad_branch = both(grad_res.astype(BF16))
    grad_cross_out = over_rows(cross_att, grad_branch).astype(BF16)
    grad_catt = against(grad_branch, w_cross_out).astype(BF16).reshape(2 * clips, span, half)
    grad_cq, part_ck, part_cv = attend_back(
        position, cross_q, cross_kv, cross_kv, cross_att.reshape(2 * clips, span, half), grad_catt, cross_logs, 0, pairs, False
    )
    grad_cq = grad_cq.reshape(2 * rows, half)
    part = jnp.concatenate([part_ck, part_cv], axis=-1).reshape(2 * clips, texts, width)
    grad_ckv = (part.astype(F32) + swap_ctx(part).astype(F32)).astype(BF16)
    share = texts // lax.axis_size("ctx")
    start = place.ctx * share

    def part_rows(array):
        array = array.reshape(2 * clips, texts, width)
        return lax.dynamic_slice_in_dim(array, start, share, 1).reshape(2 * clips * share, width)

    grad_cross_kv = over_rows(part_rows(text), part_rows(grad_ckv)).astype(BF16)
    grad_cross_query = over_rows(normed_two, grad_cq).astype(BF16)
    if staged:
        early = beside(
            place.first_sends(grad_cross_query),
            place.first_sends(grad_cross_kv),
            restack(place.first_sends(grad_cross_out)),
        )
        early, grad_cq = tied(early, grad_cq)
        early = place.first_swap(early)
        mixed_far, mixed = mixed.cores()
        mixed = mixed + swap_ctx(mixed_far).astype(F32)
    grad_hid, grad_gain_two, grad_shift_two = norm_backward(
        hidden_one, gain_two, pair_sum(grad_cq, w_cross_query, against)
    )
    grad_res = grad_res + grad_hid

    grad_branch = both(grad_res.astype(BF16))
    grad_out = over_rows(attended, grad_branch).astype(BF16)
    grad_att = against(grad_branch, w_out).astype(BF16).reshape(2 * clips, span, half)
    if staged:
        early, grad_att, mixed, feed = tied(early, grad_att, mixed, feed)
        early, feed = place.second_swap(early), place.spread_sides(feed)
    grad_q, grad_k, grad_v = attend_back(
        position,
        queries,
        key_values,
        key_values,
        attended.reshape(2 * clips, span, half),
        grad_att,
        logs,
        0,
        pairs,
        True,
    )
    grad_q = grad_q.reshape(2 * rows, half)
    grad_k = grad_k.reshape(4 * rows, half)
    grad_v = grad_v.reshape(4 * rows, half)
    grad_kv = jnp.concatenate([grad_k, grad_v], axis=1)
    grad_key_value = over_rows(normed_one, grad_kv).astype(BF16)
    grad_query = over_rows(normed_here, grad_q).astype(BF16)
    if staged:
        late = beside(
            place.first_sends(grad_query), place.first_sends(grad_key_value), restack(place.first_sends(grad_out))
        )
        early, late, feed, grad_q, grad_kv = tied(
            place.second_sum(early), late, place.spread_parts(feed), grad_q, grad_kv
        )
        early, late, feed = place.shard_sum(early), place.first_swap(late), place.spread_corners(feed)
    grad_normed_before = pair_sum(grad_kv[: 2 * rows], w_key_value, against).astype(BF16)
    grad_normed = pair_sum(grad_q, w_query, against) + pair_sum(grad_kv[2 * rows :], w_key_value, against)
    grad_text = pair_sum(grad_ckv.reshape(2 * clips * texts, width), w_cross_kv, against).reshape(clips, texts, width)
    mixed = hidden_two + (mixed if staged else pair_sum(activated[0], w_down, product))
    mixed = mixed.astype(BF16).reshape(clips, span, width)
    if staged:
        late, feed, grad_normed, grad_normed_before, grad_text, mixed = tied(
            late, feed, grad_normed, grad_normed_before, grad_text, mixed
        )
        late, feed = place.second_swap(late), place.spread_cores(feed)
    returned = shifted(grad_normed_before, "ctx", -1)
    if staged:
        early, late = tied(place.packed(early), place.second_sum(late))
        early, late = place.spread_sides(early), place.shard_sum(late)
        total_up, total_down = place.finish_up(*feed), place.finish_down(*feed)
    grad_hid, grad_gain_one, grad_shift_one = norm_backward(
        hidden_zero, gain_one, grad_normed + returned.astype(F32)
    )
    grad_frames = (grad_res + grad_hid).reshape(clips, span, width)

    small = jnp.stack(
        [grad_gain_one, grad_shift_one, grad_gain_two, grad_shift_two, grad_gain_three, grad_shift_three]
    )
    small = place.sum_norms(small)
    if staged:
        early, late, grad_frames = tied(place.spread_parts(early), place.packed(late), grad_frames)
        late, early = place.spread_sides(late), place.spread_corners(early)
        late, early, total_up, total_down, small = tied(
            place.spread_parts(late), early, total_up, total_down, small
        )
        late, early = place.spread_corners(late), place.spread_cores(early)
        total_cross_query, total_cross_key, total_cross_value = place.finish_columns(*early, 3)
        total_cross_out = place.finish_rows(*early)
        late, total_cross_query, total_cross_out = tied(late, total_cross_query, total_cross_out)
        late = place.spread_cores(late)
        total_query, total_key, total_value = place.finish_columns(*late, 3)
        total_out = place.finish_rows(*late)
    else:
        total_cross_out, total_out, total_down = map(place.plain_rows, (grad_cross_out, grad_out, grad_down))
        total_cross_key, total_cross_value = place.plain_columns(grad_cross_kv, 2)
        total_key, total_value = place.plain_columns(grad_key_value, 2)
        (total_cross_query,) = place.plain_columns(grad_cross_query, 1)
        (total_query,) = place.plain_columns(grad_query, 1)
        (total_up,) = place.plain_columns(grad_up, 1)
    return (
        mixed,
        grad_frames,
        grad_text,
        small[0],
        small[1],
        total_query,
        total_key,
        total_value,
        total_out,
        small[2],
        small[3],
        total_cross_query,
        total_cross_key,
        total_cross_value,
        total_cross_out,
        small[4],
        small[5],
        total_up,
        total_down,
    )


def solution(mesh):
    ctx, shard, rep = mesh.devices.shape
    mesh = jax.sharding.Mesh(mesh.devices.reshape(ctx, shard, rep // 2, 2), ("ctx", "shard", "y", "core"))
    clips = ("shard", "y", "core")
    rows = P(clips, "ctx", None)
    texts = P(clips, None, None)
    vector = P("shard")
    weight = P("shard", None)
    block = (vector, vector, weight, weight, weight, weight)
    in_specs = (rows, texts, *block, *block, vector, vector, weight, weight, rows)
    out_specs = (rows, rows, texts, *block, *block, vector, vector, weight, weight)
    return jax.shard_map(local, mesh=mesh, in_specs=in_specs, out_specs=out_specs, check_vma=False)
```
